256 devices in a mesh: lat: 8 (over z_lo, core), lon: 8 (over z_hi, x), dp: 4 (over y).
Axes of the slice: x: 4, y: 4, z: 8 (z_hi: 2, z_lo: 4; z = z_hi * 4 + z_lo), core: 2. Of those that a mesh axis runs over, the one named last changes fastest.
Arguments:
- features: bfloat16 [4, 128, 720, 128], P('dp', 'lat', 'lon'), may hold values from -6 to 6
- cotangent: bfloat16 [4, 128, 720, 128], P('dp', 'lat', 'lon'), may hold values from -6 to 6
- mix_weight: bfloat16 [3, 128, 128], replicated, may hold values from -0.3125 to 0.3125
- amplitude: float32 [3, 128, 5], replicated, may hold values from -4 to 4
- row_spans: int32 [128], replicated, may hold values from 1 to 90, as said below
Outputs:
- convolved: bfloat16 [4, 128, 720, 128], P('dp', 'lat', 'lon')
- grad_features: float32 [4, 128, 720, 128], P('dp', 'lat', 'lon')
- grad_weight: float32 [3, 128, 128], replicated
The draws below stay inside these ranges and needn't reach their ends.
Inputs may be any that keep to these rules, and one draw needn't show every extreme that they name: For each row i, with base = 2 * 720 // (6 i + 1): row_spans[i] lies between max(1, min(90, base)) and min(90, base + 2), and equals min(90, base + 2) on every even row i. Row 0 reaches 90 cells.
All inputs are finite; a program needn't handle non-finite values.
Results may differ from the reference program's by a relative error of at most 0.0058.
Values may be sent and summed in bfloat16 or wider, within the bound.
No kernel may reach another device: no remote copies, remote signals or barrier semaphores. Data moves between devices by JAX's collectives and lax.ppermute only.
A program may use at most 64 MiB of HBM per device.

```python
import math
import jax
import jax.numpy as jnp
from jax import lax

C = 128
K = 3
NLAT = 128
NLON = 720
BATCH = 4


def draw_row_spans(key, part):
    key = jax.random.fold_in(key, 11)
    latitude = jnp.arange(NLAT, dtype=jnp.int32)
    jitter = jax.random.randint(key, (NLAT,), 0, 3, dtype=jnp.int32)
    jitter = jnp.where(latitude % 2 == 0, 2, jitter)
    spread = 2 * NLON // (6 * latitude + 1) + jitter
    return jnp.clip(spread, 1, NLON // 8).astype(jnp.int32)


def block_scale(rng, shape, split, low, top_value):
    factor_of = 1.0
    for dim, parts in split:
        heights = jax.random.uniform(jax.random.fold_in(jax.random.fold_in(rng, 6), dim), (parts,), jnp.float32, low / len(split), top_value / len(split))
        factor_of = factor_of * jnp.repeat(jnp.exp(heights), shape[dim] // parts).reshape((-1,) + (1,) * (len(shape) - 1 - dim))
    return factor_of


def scatter_about(key, shape, deviation, bound, pieces=(), kind=jnp.bfloat16):
    values = jax.random.normal(key, shape, jnp.float32) * deviation
    if len(pieces) > 0:
        values = block_scale(key, shape, pieces, -0.22, 0.18) * values
    return jnp.clip(values, min=-bound, max=bound).astype(kind)


def setup_inputs(seed: int = 0) -> dict:
    splits = jax.random.split(jax.random.key(seed), 6)
    return {
        "features": scatter_about(splits[0], (BATCH, NLAT, NLON, C), 1.0, 6.0, ((0, 4), (1, 8), (2, 8))),
        "cotangent": scatter_about(splits[1], (BATCH, NLAT, NLON, C), 1.0, 6.0, ((0, 4), (1, 8), (2, 8))),
        "mix_weight": scatter_about(splits[2], (K, C, C), (K * C) ** -0.5, 0.3125),
        "amplitude": scatter_about(splits[3], (K, NLAT, 5), 1.0, 4.0, (), jnp.float32),
        "row_spans": draw_row_spans(jax.random.fold_in(splits[5], 71), 0),
    }


def basis_values(amplitude_part, extent, offsets):
    divisor = extent.astype(jnp.float32) + 1.0
    scaled = offsets.astype(jnp.float32) / divisor
    shapes = jnp.concatenate([1.0 - jnp.abs(scaled), scaled, jnp.cos(jnp.pi * scaled)], axis=0)
    values = amplitude_part * shapes * (1.0 / jnp.sqrt(divisor))
    return jnp.where(jnp.abs(offsets) <= extent, values, 0.0).astype(jnp.bfloat16)

def signed_offset(positions, cycle_len):
    return (positions + cycle_len // 2) % cycle_len - cycle_len // 2

def kernel_spectra(amplitude_rows, span_values, offsets):
    values = basis_values(amplitude_rows[:, :, None], span_values[None, :, None], offsets)
    values = lax.optimization_barrier(values).astype(jnp.float32)
    return jnp.fft.rfft(values, axis=-1)

def reference(features, cotangent, mix_weight, amplitude, row_spans):
    positions = jnp.arange(NLON, dtype=jnp.int32)
    forward_offsets = signed_offset((NLON - positions) % NLON, NLON)[None, None, :]
    backward_offsets = signed_offset(positions, NLON)[None, None, :]
    weight_wide = mix_weight.astype(jnp.float32)
    spectra = jnp.fft.rfft(features.astype(jnp.float32), axis=2)
    spectra = jnp.pad(spectra, ((0, 0), (2, 2), (0, 0), (0, 0)))

    def forward_step(weight_total, row_index):
        amplitude_rows = lax.dynamic_index_in_dim(amplitude, row_index, 1, keepdims=False)
        span_values = jnp.full((5,), row_spans[row_index], jnp.int32)
        kernels = kernel_spectra(amplitude_rows, span_values, forward_offsets)
        row_spectra = lax.dynamic_slice_in_dim(spectra, row_index, 5, 1)
        mixed_spectra = jnp.einsum('kef,befc->kbfc', kernels, row_spectra)
        basis_row = jnp.fft.irfft(mixed_spectra, n=NLON, axis=2).astype(jnp.bfloat16)
        basis_wide = lax.optimization_barrier(basis_row).astype(jnp.float32)
        convolved_row = jnp.einsum('kbjc,kcd->bjd', basis_wide, weight_wide).astype(jnp.bfloat16)
        cotangent_row = lax.dynamic_index_in_dim(cotangent, row_index, 1, keepdims=False).astype(jnp.float32)
        weight_total = weight_total + jnp.einsum('kbjc,bjd->kcd', basis_wide, cotangent_row)
        return (weight_total, convolved_row)
    cotangent_pad = jnp.pad(cotangent, ((0, 0), (2, 2), (0, 0), (0, 0)))
    shifts = jnp.arange(5, dtype=jnp.int32)

    def backward_row(row_index):
        near_rows = lax.dynamic_slice_in_dim(cotangent_pad, row_index, 5, 1).astype(jnp.float32)
        cograd = jnp.einsum('bqjd,kcd->qkbjc', near_rows, weight_wide).astype(jnp.bfloat16)
        cograd = lax.optimization_barrier(cograd).astype(jnp.float32)
        cograd_spectra = jnp.fft.rfft(cograd, axis=3)
        source = row_index - 2 + shifts
        inside = (source >= 0) & (source < NLAT)
        clipped = jnp.clip(source, 0, NLAT - 1).astype(jnp.int32)
        amplitude_rows = jnp.where(inside[None, :], amplitude[:, clipped, 4 - shifts], 0.0)
        kernels = kernel_spectra(amplitude_rows, row_spans[clipped], backward_offsets)
        summed_spectra = jnp.einsum('kqf,qkbfc->bfc', kernels, cograd_spectra)
        return jnp.fft.irfft(summed_spectra, n=NLON, axis=1)
    weight_total, convolved_rows = lax.scan(forward_step, jnp.zeros((K, C, C), jnp.float32), jnp.arange(NLAT, dtype=jnp.int32))
    grad_rows = lax.map(backward_row, jnp.arange(NLAT, dtype=jnp.int32))
    convolved = jnp.transpose(convolved_rows, (1, 0, 2, 3))
    grad_features = jnp.transpose(grad_rows, (1, 0, 2, 3))
    grad_weight = weight_total * (1.0 / math.sqrt(BATCH * NLAT * NLON))
    return (convolved, grad_features, grad_weight)
```

```python
import functools
import math

import jax
import jax.numpy as jnp
from jax import lax
from jax.experimental import pallas as pl
from jax.experimental.pallas import tpu as pltpu
from jax.sharding import PartitionSpec as P

ROWS = 16
COLS = 90
CHAN = 128
PAD = 96
NEAR = 16
HIGH = 7
F32 = jnp.float32
BF16 = jnp.bfloat16
LL = ("lat", "lon")


def offsets_of(group):
    col = lax.broadcasted_iota(jnp.int32, (PAD, 128), 0)
    lane = lax.broadcasted_iota(jnp.int32, (PAD, 128), 1)
    none = jnp.full((PAD, 128), 1000000, jnp.int32)
    if group == 0:
        source = jnp.where(lane < PAD, lane, jnp.where(lane < PAD + NEAR, lane - 112, lane - 22))
        source = jnp.where((lane >= COLS) & (lane < PAD), none, source)
    elif group == 1:
        source = jnp.where(lane < 64, lane - 80, lane + 42)
    else:
        source = jnp.where(lane < 16, lane - 90, lane + 148)
        source = jnp.where((lane >= 10) & (lane < 22), none, source)
        source = jnp.where(lane >= 32, none, source)
    return (source - col).astype(F32)


def fill_shapes(table, offsets, spans, inverse, first, start, count):
    def fill(row, carry):
        ext = first + row
        inside = jnp.abs(offsets) <= spans[ext].astype(F32)
        scaled = jnp.where(inside, offsets * inverse[ext], 0.0)
        square = scaled * scaled
        half = jnp.full(square.shape, 4.7108746e-07, F32)
        for term in (-2.5202042e-05, 9.1926025e-04, -2.0863481e-02, 2.5366950e-01, -1.2337005, 1.0):
            half = half * square + term
        cosine = 2.0 * half * half - 1.0
        shapes = (1.0 - jnp.abs(scaled), scaled, cosine)
        for k in range(3):
            at = pl.multiple_of((row * 3 + k) * PAD, PAD)
            table[pl.ds(at, PAD), :] = jnp.where(inside, shapes[k], 0.0)
        return carry

    lax.fori_loop(start, start + count, fill, 0)


def band_pass(data, total, table, blocks, amps, first, rows, backward, fresh):
    def step(row, carry):
        for slot in range(5):
            for k in range(3):
                if backward:
                    ext, tap, sign = row + slot, 4 - slot, (-1.0 if k == 1 else 1.0)
                else:
                    ext, tap, sign = row + 2, slot, 1.0
                factor = amps[(first + ext) * 15 + k * 5 + tap] * sign
                shape = table[pl.ds(pl.multiple_of((ext * 3 + k) * PAD, PAD), PAD), :]
                blocks[k * PAD : (k + 1) * PAD, slot * 128 : (slot + 1) * 128] = (shape * factor).astype(BF16)
        near = data[pl.ds(pl.multiple_of(row * 128, 128), 640), :]
        term = jnp.dot(blocks[...], near, preferred_element_type=F32)
        at = pl.ds(pl.multiple_of(row * 288, 288), 288)
        if fresh:
            total[at, :] = term
        else:
            total[at, :] += term
        return carry

    lax.fori_loop(0, rows, step, 0)


def convolve(info, spans, inverse, amps, own, halo_a, halo_b, which, data, total, table, blocks, backward):
    lat = info[0]
    first = info[2]
    even = lat % 2 == 0

    def place(group, lo, hi, at_lo):
        for row in range(2):
            a = halo_a[which, row, lo:hi, :]
            b = halo_b[which, row, lo:hi, :] if lo < 128 else jnp.zeros((hi - lo, CHAN), BF16)
            data[row * 128 + at_lo : row * 128 + at_lo + hi - lo, :] = jnp.where(even, b, a)
            data[(18 + row) * 128 + at_lo : (18 + row) * 128 + at_lo + hi - lo, :] = jnp.where(even, a, b)

    data[256 : 256 + 2048, :] = own[0][...].reshape(2048, CHAN)
    place(0, 0, 128, 0)
    ext_start, ext_count = (0, 20) if backward else (2, 16)
    fill_shapes(table, offsets_of(0), spans, inverse, first, ext_start, ext_count)
    band_pass(data, total, table, blocks, amps, first, ROWS, backward, True)

    def wide(rows):
        data[...] = jnp.zeros(data.shape, BF16)
        data[256 : 256 + 2048, :] = own[1][...].reshape(2048, CHAN)
        place(1, 128, 160, 48)
        fill_shapes(table, offsets_of(1), spans, inverse, first, ext_start, ext_count)
        band_pass(data, total, table, blocks, amps, first, rows, backward, False)

    if backward:
        pl.when(lat == 1)(lambda: wide(2))

    @pl.when(lat == 0)
    def _():
        wide(ROWS)
        rows = 5 if backward else 3
        data[...] = jnp.zeros(data.shape, BF16)
        for row in range(5):
            data[(2 + row) * 128 : (2 + row) * 128 + 32, :] = own[2][row]
        if backward:
            fill_shapes(table, offsets_of(2), spans, inverse, first, 0, 9)
        else:
            fill_shapes(table, offsets_of(2), spans, inverse, first, 2, 3)
        band_pass(data, total, table, blocks, amps, first, rows, backward, False)


def forward_kernel(info, spans, inverse, amps, own0, own1, own2, cot, halo_a, halo_b, basis, grad, data, total, table, blocks):
    convolve(info, spans, inverse, amps, (own0, own1, own2), halo_a, halo_b, 0, data, total, table, blocks, False)

    def pack(row, carry):
        for k in range(3):
            at = pl.multiple_of(row * 288 + k * PAD, PAD)
            basis[pl.ds(pl.multiple_of(row * PAD, PAD), PAD), k * 128 : (k + 1) * 128] = total[pl.ds(at, PAD), :].astype(BF16)
        return carry

    lax.fori_loop(0, ROWS, pack, 0)
    cotangent = cot[:, :PAD, :].reshape(ROWS * PAD, CHAN)
    product = lax.dot_general(cotangent, basis[...], (((0,), (0,)), ((), ())), preferred_element_type=F32)
    for k in range(3):
        grad[k * 128 : (k + 1) * 128, :] = product[:, k * 128 : (k + 1) * 128].T


def mix_kernel(basis, weight, out):
    def step(row, carry):
        mixed = jnp.dot(basis[pl.ds(pl.multiple_of(row * PAD, PAD), PAD), :], weight[...], preferred_element_type=F32)
        out[0, row] = mixed.astype(BF16)[:COLS]
        return carry

    lax.fori_loop(0, ROWS, step, 0)


def backward_kernel(info, spans, inverse, amps, own0, own1, own2, halo_a, halo_b, weight, out, data, total, table, blocks):
    convolve(info, spans, inverse, amps, (own0, own1, own2), halo_a, halo_b, 1, data, total, table, blocks, True)

    def step(row, carry):
        mixed = jnp.zeros((PAD, CHAN), F32)
        for k in range(3):
            part = total[pl.ds(pl.multiple_of(row * 288 + k * PAD, PAD), PAD), :].astype(BF16)
            mixed += jnp.dot(part, weight[k], preferred_element_type=F32)
        out[0, row] = mixed[:COLS]
        return carry

    lax.fori_loop(0, ROWS, step, 0)


def assemble_kernel(info, field, cot, small_a, small_b, large_a, large_b, *outs):
    lat, lon = info[0], info[1]
    odd = lon % 2 == 1
    polar = lat < 2
    groups = (outs[0:3], outs[3:6])
    lat_a, lat_b = outs[6], outs[7]
    for which, source in enumerate((field, cot)):
        own0, own1, own2 = groups[which]
        own0[:, :PAD, :] = jnp.zeros((ROWS, PAD, CHAN), BF16)
        own0[:, :COLS, :] = source[0]

        def left_right(at, size, rows, shape):
            a = large_a[which, pl.ds(at, size), :]
            b = large_b[which, pl.ds(at, size), :]
            return jnp.where(odd, b, a).reshape(shape), jnp.where(odd, a, b).reshape(shape)

        left, right = left_right(0, 256, ROWS, (ROWS, NEAR, CHAN))
        own0[:, 96:112, :] = jnp.where(polar, left, jnp.where(odd, small_b[which], small_a[which]))
        own0[:, 112:128, :] = jnp.where(polar, right, jnp.where(odd, small_a[which], small_b[which]))

        @pl.when(polar)
        def _(own1=own1, own2=own2, left_right=left_right):
            own1[...] = jnp.zeros(own1.shape, BF16)
            left, right = left_right(256, HIGH * 64, HIGH, (HIGH, 64, CHAN))
            own1[:HIGH, :64, :] = left
            own1[:HIGH, 64:, :] = right
            rest = ROWS - HIGH
            left, right = left_right(256 + HIGH * 64, rest * 32, rest, (rest, 32, CHAN))
            own1[HIGH:, 32:64, :] = left
            own1[HIGH:, 64:96, :] = right
            left, right = left_right(256 + HIGH * 64 + rest * 32, 80, 5, (5, 16, CHAN))
            own2[:, :16, :] = left
            own2[:, 16:, :] = right

        @pl.when(jnp.logical_not(polar))
        def _(own1=own1, own2=own2):
            own1[...] = jnp.zeros(own1.shape, BF16)
            own2[...] = jnp.zeros(own2.shape, BF16)

        even = lat % 2 == 0
        for row in range(2):
            lat_a[which, row, :128, :] = jnp.where(even, own0[14 + row], own0[row])
            lat_a[which, row, 128:, :] = jnp.where(even, own1[14 + row, 48:80, :], own1[row, 48:80, :])
            lat_b[which, row] = jnp.where(even, own0[row], own0[14 + row])


def edge_of(both, right):
    if right:
        near, far, last = both[:, :, 74:90], both[:, :HIGH, 10:74], both[:, :5, 0:16]
        rest = both[:, HIGH:, 42:74]
    else:
        near, far, last = both[:, :, 0:16], both[:, :HIGH, 16:80], both[:, :5, 74:90]
        rest = both[:, HIGH:, 16:48]
    flat = [part.reshape(2, -1, CHAN) for part in (near, far, rest, last)]
    return near, jnp.concatenate(flat, axis=1)


def pairs_of_lon(parity, lats):
    out = []
    for lat in lats:
        for lon in range(8):
            other = lon ^ 1 if parity == 0 else ((lon + 1) % 8 if lon % 2 else (lon - 1) % 8)
            out.append((lat * 8 + lon, lat * 8 + other))
    return out


def pairs_of_lat(parity):
    out = []
    for lat in range(8):
        other = lat ^ 1 if parity == 0 else (lat + 1 if lat % 2 else lat - 1)
        if 0 <= other < 8:
            out.append((lat, other))
    return out


def z_pairs():
    across = {0: 6, 6: 0, 1: 7, 7: 1, 2: 4, 4: 2, 3: 5, 5: 3}
    out = []
    for lat in range(8):
        for lon in range(8):
            other = across[(lon >> 2) * 4 + (lat >> 1)]
            out.append((lat * 8 + lon, ((other % 4) * 2 + lat % 2) * 8 + (other // 4) * 4 + lon % 4))
    return out


def reduce_all(part):
    flip = lambda x, axis, bit: lax.ppermute(x, axis, [(i, i ^ bit) for i in range(lax.axis_size(axis))])
    core = lax.axis_index("lat") % 2
    half = part.shape[0] // 2
    mine = lax.dynamic_slice_in_dim(part, core * half, half, 0)
    other = lax.dynamic_slice_in_dim(part, (1 - core) * half, half, 0)
    mine = mine + flip(other, "lat", 1)
    for axis in ("dp", "lon"):
        one, two, three = (flip(mine, axis, bit) for bit in (1, 2, 3))
        mine = (mine + one) + (two + three)
    mine = mine + flip(mine, "lat", 2)
    mine = mine + flip(mine, "lat", 4)
    mine = mine + lax.ppermute(mine, LL, z_pairs())
    other = flip(mine, "lat", 1)
    return jnp.where(core == 0, jnp.concatenate([mine, other]), jnp.concatenate([other, mine]))


VMEM = pl.BlockSpec(memory_space=pltpu.VMEM)
SMEM = pl.BlockSpec(memory_space=pltpu.SMEM)
PARAMS = pltpu.CompilerParams(vmem_limit_bytes=48 * 1024 * 1024)


def call(kernel, outs, scratch, flops, scalars, arrays):
    moved = sum(math.prod(x.shape) * x.dtype.itemsize for x in (*arrays, *outs))
    return pl.pallas_call(
        kernel,
        out_shape=outs,
        in_specs=[SMEM] * len(scalars) + [VMEM] * len(arrays),
        out_specs=[VMEM] * len(outs),
        scratch_shapes=scratch,
        compiler_params=PARAMS,
        cost_estimate=pl.CostEstimate(flops=flops, bytes_accessed=moved, transcendentals=0),
    )(*scalars, *arrays)


def shape(dims, dtype=BF16):
    return jax.ShapeDtypeStruct(dims, dtype)


def body(features, cotangent, mix_weight, amplitude, row_spans):
    lat, lon = lax.axis_index("lat"), lax.axis_index("lon")
    info = jnp.stack([lat, lon, lat * ROWS]).astype(jnp.int32)
    divisor = row_spans.astype(F32) + 1.0
    spans = jnp.pad(row_spans, (2, 2))
    inverse = jnp.pad(1.0 / divisor, (2, 2), constant_values=1.0)
    amps = amplitude * (1.0 / jnp.sqrt(divisor))[None, :, None]
    amps = jnp.pad(amps.transpose(1, 0, 2), ((2, 2), (0, 0), (0, 0))).reshape(-1)
    scalars = (info, spans, inverse, amps)

    both = jnp.concatenate([features, cotangent], axis=0)
    right_near, right_all = edge_of(both, True)
    left_near, left_all = edge_of(both, False)
    odd = lon % 2 == 1
    small_a = lax.ppermute(jnp.where(odd, right_near, left_near), LL, pairs_of_lon(1, range(2, 8)))
    large_a = lax.ppermute(jnp.where(odd, right_all, left_all), LL, pairs_of_lon(1, range(2)))
    small_b = lax.ppermute(jnp.where(odd, left_near, right_near), LL, pairs_of_lon(0, range(2, 8)))
    large_b = lax.ppermute(jnp.where(odd, left_all, right_all), LL, pairs_of_lon(0, range(2)))

    groups = [shape((ROWS, 128, CHAN)), shape((ROWS, 128, CHAN)), shape((5, 32, CHAN))]
    outs = groups + groups + [shape((2, 2, 160, CHAN)), shape((2, 2, 128, CHAN))]
    arrays = (features, cotangent, small_a, small_b, large_a, large_b)
    *gathered, lat_a, lat_b = call(assemble_kernel, outs, [], 0, (info,), arrays)
    halo_a = lax.ppermute(lat_a, "lat", pairs_of_lat(0))
    halo_b = lax.ppermute(lat_b, "lat", pairs_of_lat(1))

    scratch = [
        pltpu.VMEM((20 * 128, CHAN), BF16),
        pltpu.VMEM((ROWS * 288, CHAN), F32),
        pltpu.VMEM((20 * 288, 128), F32),
        pltpu.VMEM((288, 640), BF16),
    ]
    band_flops = 2 * ROWS * 288 * 640 * CHAN
    basis, part = call(
        forward_kernel,
        [shape((ROWS * PAD, 384)), shape((384, CHAN), F32)],
        scratch,
        2 * band_flops,
        scalars,
        (*gathered[:3], gathered[3], halo_a, halo_b),
    )
    (convolved,) = call(mix_kernel, [shape(features.shape)], [], 2 * ROWS * PAD * 384 * CHAN, (), (basis, mix_weight.reshape(384, CHAN)))
    (grad_features,) = call(
        backward_kernel,
        [shape(features.shape, F32)],
        scratch,
        2 * band_flops,
        scalars,
        (*gathered[3:], halo_a, halo_b, mix_weight.transpose(0, 2, 1)),
    )
    cells = 4 * 128 * 720
    grad_weight = reduce_all(part).reshape(3, 128, 128) * (1.0 / math.sqrt(cells))
    return convolved, grad_features, grad_weight


def solution(mesh):
    cells = P("dp", "lat", "lon", None)
    return jax.shard_map(
        body,
        mesh=mesh,
        in_specs=(cells, cells, P(), P(), P()),
        out_specs=(cells, cells, P()),
        check_vma=False,
    )
```

```python
import functools
import math

import jax
import jax.numpy as jnp
from jax import lax
from jax.experimental import pallas as pl
from jax.experimental.pallas import tpu as pltpu
from jax.sharding import PartitionSpec as P

ROWS = 16
COLS = 90
CHAN = 128
PAD = 96
F32 = jnp.float32
BF16 = jnp.bfloat16
LL = ("lat", "lon")
POLAR_FAR = 40
SECOND = 18
OTHERS = 9


def offsets_of(group):
    col = lax.broadcasted_iota(jnp.int32, (PAD, 128), 0)
    lane = lax.broadcasted_iota(jnp.int32, (PAD, 128), 1)
    none = jnp.full((PAD, 128), 1000000, jnp.int32)
    if group == 0:
        source = jnp.where(lane < PAD, lane, jnp.where(lane < PAD + 16, lane - 112, lane - 22))
        source = jnp.where((lane >= COLS) & (lane < PAD), none, source)
    elif group == 1:
        source = jnp.where(lane < 64, lane - 80, lane + 42)
    else:
        source = jnp.where(lane < 16, lane - 90, lane + 148)
        source = jnp.where((lane >= 10) & (lane < 22), none, source)
        source = jnp.where(lane >= 32, none, source)
    return (source - col).astype(F32)


def fill_shapes(table, offsets, spans, first, low, high):
    def fill(row, carry):
        span = spans[row_of(first, row)].astype(F32)
        divisor = jnp.full((1, 128), span + 1.0, F32)
        norm = lax.rsqrt(divisor)
        inside = jnp.abs(offsets) <= span
        scaled = jnp.where(inside, offsets * (1.0 / divisor), 0.0)
        square = scaled * scaled
        half = jnp.full(square.shape, 4.7108746e-07, F32)
        for term in (-2.5202042e-05, 9.1926025e-04, -2.0863481e-02, 2.5366950e-01, -1.2337005, 1.0):
            half = half * square + term
        cosine = 2.0 * half * half - 1.0
        shapes = (1.0 - jnp.abs(scaled), scaled, cosine)
        for k in range(3):
            at = pl.multiple_of(row * 288 + k * PAD, PAD)
            table[pl.ds(at, PAD), :] = jnp.where(inside, shapes[k] * norm, 0.0).astype(BF16)
        return carry

    lax.fori_loop(low, high, fill, 0)


def row_of(first, ext):
    return jnp.clip(first + ext - 2, 0, 127)


def factor_of(amps, first, ext, k, tap):
    return amps[tap, k, row_of(first, ext)]


def pack_kernel(info, field, cot, near_a, second_a, polar_a, second_b, polar_b, token, whole, sems):
    odd = info[1] % 2 == 1

    def edges(is_odd):
        copies = []
        for which, source in enumerate((field, cot)):
            for out, width, right in ((near_a, OTHERS, is_odd), (second_a, SECOND, is_odd), (second_b, SECOND, not is_odd)):
                begin = COLS - width if right else 0
                copies.append((source.at[0, begin : begin + width], out.at[which]))
        copies = [pltpu.make_async_copy(a, b, sems.at[i]) for i, (a, b) in enumerate(copies)]
        for copy in copies:
            copy.start()

        @pl.when(info[0] == 0)
        def _():
            loads = []
            for which, source in enumerate((field, cot)):
                for part in range(3):
                    at = pl.ds(part * 30, 30)
                    sem = sems.at[6 + which * 3 + part]
                    loads.append(pltpu.make_async_copy(source.at[0, at], whole.at[which, at], sem))
            for load in loads:
                load.start()
            for load in loads:
                load.wait()
            for which in range(2):
                low = whole[which, :, :8]
                left, right = whole[which, :POLAR_FAR, 8:], whole[which, COLS - POLAR_FAR :, 8:]
                polar_a[which, :COLS] = low
                polar_b[which, :COLS] = low
                polar_a[which, COLS:] = right if is_odd else left
                polar_b[which, COLS:] = left if is_odd else right

        for copy in copies:
            copy.wait()

    pl.when(odd)(lambda: edges(True))
    pl.when(jnp.logical_not(odd))(lambda: edges(False))
    token[...] = jnp.zeros((8, 128), F32)


def pre_kernel(info, spans, field, cot, token, own_f, own_c, shape0, shape1, shape2):
    lat, first = info[0], info[2]
    for source, own in ((field, own_f), (cot, own_c)):
        own[:, COLS:, :] = jnp.zeros((ROWS, 128 - COLS, CHAN), BF16)
        own[:, :COLS, :] = jnp.swapaxes(source[0], 0, 1)
    fill_shapes(shape0, offsets_of(0), spans, first, 0, 20)

    @pl.when(lat < 2)
    def _():
        low = jnp.where(lat == 0, 2, 0)
        fill_shapes(shape1, offsets_of(1), spans, first, low, jnp.where(lat == 0, 18, 2))

    @pl.when(lat == 0)
    def _():
        fill_shapes(shape2, offsets_of(2), spans, first, 2, 5)


def assemble_kernel(info, old_f, old_c, near_a, second_a, polar_a, second_b, polar_b, *outs):
    lat, lon = info[0], info[1]
    odd = lon % 2 == 1
    groups = ((outs[0], outs[2], outs[4]), (outs[1], outs[3], outs[5]))
    lat_a, lat_b = outs[6], outs[7]

    def left_right(a_ref, b_ref, which, lo, hi):
        left = jnp.where(odd, b_ref[which, lo:hi], a_ref[which, lo:hi])
        right = jnp.where(odd, a_ref[which, lo:hi], b_ref[which, lo:hi])
        return jnp.swapaxes(left, 0, 1), jnp.swapaxes(right, 0, 1)

    for which in range(2):
        own0, own1, own2 = groups[which]
        own0[...] = (old_f, old_c)[which][...]

        @pl.when(lat >= 2)
        def _(which=which, own0=own0):
            a = near_a[which]
            left = jnp.where(odd, second_b[which, SECOND - OTHERS :], a)
            right = jnp.where(odd, a, second_b[which, :OTHERS])
            own0[:, 112 - OTHERS : 112, :] = jnp.swapaxes(left, 0, 1)
            own0[:, 112 : 112 + OTHERS, :] = jnp.swapaxes(right, 0, 1)

        @pl.when(lat == 1)
        def _(which=which, own0=own0, own1=own1):
            left, right = left_right(second_a, second_b, which, 0, SECOND)
            own0[:, 96:112, :] = left[:, 2:]
            own0[:, 112:128, :] = right[:, :16]
            own1[...] = jnp.zeros(own1.shape, BF16)
            own1[:, 62:64, :] = left[:, :2]
            own1[:, 64:66, :] = right[:, 16:]

        @pl.when(lat == 0)
        def _(which=which, own0=own0, own1=own1, own2=own2):
            left, right = left_right(polar_a, polar_b, which, 0, COLS)
            own0[:8, 96:112, :] = left[:, 74:90]
            own0[:8, 112:128, :] = right[:, 0:16]
            own1[:8, :64, :] = left[:, 10:74]
            own1[:8, 64:, :] = right[:, 16:80]
            own2[:, :16, :] = left[:5, 0:16]
            own2[:, 16:, :] = right[:5, 74:90]
            left, right = left_right(polar_a, polar_b, which, COLS, COLS + POLAR_FAR)
            own0[8:, 96:112, :] = left[:, 24:40]
            own0[8:, 112:128, :] = right[:, 0:16]
            own1[8:] = jnp.zeros((8, 128, CHAN), BF16)
            own1[8:, 40:64, :] = left[:, 0:24]
            own1[8:, 64:88, :] = right[:, 16:40]

        even = lat % 2 == 0
        for row in range(2):
            lat_a[which, row, :128, :] = jnp.where(even, own0[14 + row], own0[row])
            lat_a[which, row, 128:, :] = jnp.where(even, own1[14 + row, 48:80, :], own1[row, 48:80, :])
            lat_b[which, row] = jnp.where(even, own0[row], own0[14 + row])


def filtered(shapes, amps, first, ext, rows):
    total = None
    for taps in ((0, 1), (2, 3), (4,)):
        gathered = jnp.concatenate([rows[tap] for tap in taps], axis=1) if len(taps) > 1 else rows[taps[0]]
        product = jnp.dot(shapes, gathered, preferred_element_type=F32)
        for index, tap in enumerate(taps):
            part = product[:, index * 128 : (index + 1) * 128]
            scaled = [part[k * PAD : (k + 1) * PAD] * factor_of(amps, first, ext, k, tap) for k in range(3)]
            total = scaled if total is None else [x + y for x, y in zip(total, scaled)]
    return total


def rows_at(ref, start, count=288):
    return ref[pl.ds(start if isinstance(start, int) else pl.multiple_of(start, 32), count), :]


def store_basis(basis, row, values):
    at = row * PAD if isinstance(row, int) else pl.multiple_of(row * PAD, PAD)
    for k in range(3):
        basis[pl.ds(at, PAD), k * 128 : (k + 1) * 128] = values[k].astype(BF16)


def times_cotangent(cot, basis):
    return lax.dot_general(cot, basis, (((0,), (0,)), ((), ())), preferred_element_type=F32)


def inner_kernel(info, amps, own0, own1, own2, shape0, shape1, shape2, cot, basis, part):
    lat, first = info[0], info[2]

    def one(row, wide, extra=None):
        shapes = rows_at(shape0, (row + 2) * 288)
        rows = [own0[row - 2 + tap] for tap in range(5)]
        if wide:
            shapes = jnp.concatenate([shapes, rows_at(shape1, (row + 2) * 288)], axis=1)
            rows = [jnp.concatenate([near, own1[row - 2 + tap]], axis=0) for tap, near in enumerate(rows)]
        values = filtered(shapes, amps, first, row + 2, rows)
        if extra is not None:
            values = [x + y for x, y in zip(values, extra)]
        store_basis(basis, row - 2, values)

    def loop(start, wide):
        def step(row, carry):
            one(row, wide)
            return carry

        lax.fori_loop(start, 14, step, 0)

    @pl.when(lat != 0)
    def _():
        loop(2, False)

    @pl.when(lat == 0)
    def _():
        far = filtered(shape2[4 * 288 : 5 * 288, :32], amps, first, 4, [own2[tap] for tap in range(5)])
        one(2, True, far)
        loop(3, True)

    part[...] = times_cotangent(cot[2:14, :PAD, :].reshape(12 * PAD, CHAN), basis[...])


def halo_row(halo_a, halo_b, which, row, even, top):
    a, b = halo_a[which, row, :128], halo_b[which, row]
    return jnp.where(even, b, a) if top else jnp.where(even, a, b)


def far_halo_row(halo_a, which, row):
    zeros = jnp.zeros((48, CHAN), BF16)
    return jnp.concatenate([zeros, halo_a[which, row, 128:], zeros], axis=0)


def outer_kernel(info, amps, own0, own1, own2, shape0, shape1, shape2, cot, halo_a, halo_b, part, basis, mine, other, grad):
    lat, first = info[0], info[2]
    even = lat % 2 == 0

    def run(wide):
        for place, row in enumerate((0, 1, 14, 15)):
            shapes = shape0[(row + 2) * 288 : (row + 3) * 288, :]
            rows = []
            for at in range(row - 2, row + 3):
                if 0 <= at < ROWS:
                    gathered = own0[at]
                else:
                    gathered = halo_row(halo_a, halo_b, 0, at + 2 if at < 0 else at - ROWS, even, at < 0)
                if wide:
                    if 0 <= at < ROWS:
                        far = own1[at]
                    elif at < 0:
                        far = jnp.zeros((128, CHAN), BF16)
                    else:
                        far = far_halo_row(halo_a, 0, at - ROWS)
                    gathered = jnp.concatenate([gathered, far], axis=0)
                rows.append(gathered)
            if wide:
                shapes = jnp.concatenate([shapes, shape1[(row + 2) * 288 : (row + 3) * 288, :]], axis=1)
            values = filtered(shapes, amps, first, row + 2, rows)
            if wide and row < 2:
                zeros = jnp.zeros((32, CHAN), BF16)
                rows = [own2[at] if at >= 0 else zeros for at in range(row - 2, row + 3)]
                far = filtered(shape2[(row + 2) * 288 : (row + 3) * 288, :32], amps, first, row + 2, rows)
                values = [x + y for x, y in zip(values, far)]
            store_basis(basis, place, values)

    pl.when(lat != 0)(lambda: run(False))
    pl.when(lat == 0)(lambda: run(True))
    ends = jnp.concatenate([cot[0:2, :PAD, :], cot[14:16, :PAD, :]], axis=0).reshape(4 * PAD, CHAN)
    product = part[...] + times_cotangent(ends, basis[...])
    for k in range(3):
        grad[k * 128 : (k + 1) * 128, :] = product[:, k * 128 : (k + 1) * 128].T
    core = lat % 2
    mine[...] = grad[pl.ds(pl.multiple_of(core * 192, 192), 192), :]
    other[...] = grad[pl.ds(pl.multiple_of((1 - core) * 192, 192), 192), :]


def mix_kernel(inner, outer, weight, before, out, token):
    w = weight[...]

    def mixed(basis, rows):
        return jnp.dot(basis, w, preferred_element_type=F32).astype(BF16).reshape(rows, PAD, CHAN)[:, :COLS]

    ends = mixed(outer[...], 4)
    whole = jnp.concatenate([ends[:2], mixed(inner[...], 12), ends[2:]], axis=0)
    out[0] = jnp.swapaxes(whole, 0, 1)
    token[...] = before[...]


def back_kernel(piece, info, amps, own0, own1, own2, shape0, shape1, shape2, halo_a, halo_b, weight, before, *refs):
    out, token, spread = refs[-3:]
    lat, first = info[0], info[2]
    even = lat % 2 == 0
    begin = 8 * piece

    def put(index, value, fresh):
        at = index * 288 if isinstance(index, int) else pl.multiple_of(index * 288, 32)
        if fresh:
            spread[pl.ds(at, 288), :] = value
        else:
            spread[pl.ds(at, 288), :] += value

    def own_rows(low, high, wide):
        def step(ext, carry):
            shapes, rows = rows_at(shape0, ext * 288), own0[ext - 2]
            if wide:
                shapes = jnp.concatenate([shapes, rows_at(shape1, ext * 288)], axis=1)
                rows = jnp.concatenate([rows, own1[ext - 2]], axis=0)
            put(ext - begin, jnp.dot(shapes, rows, preferred_element_type=F32), True)
            return carry

        lax.fori_loop(low, high, step, 0)

    low, high = max(begin, 2), min(begin + 12, 18)
    pl.when(lat != 0)(lambda: own_rows(low, high, False))
    pl.when(lat == 0)(lambda: own_rows(low, high, True))
    for row in range(2):
        ext = row if piece == 0 else 18 + row
        gathered = halo_row(halo_a, halo_b, 1, row, even, piece == 0)
        put(ext - begin, jnp.dot(shape0[ext * 288 : (ext + 1) * 288, :], gathered, preferred_element_type=F32), True)
    if piece == 0:

        @pl.when(lat == 1)
        def _():
            for row in range(2):
                far = far_halo_row(halo_a, 1, row)
                put(row, jnp.dot(shape1[row * 288 : (row + 1) * 288, :], far, preferred_element_type=F32), False)

        @pl.when(lat == 0)
        def _():
            for ext in range(2, 5):
                shapes = shape2[ext * 288 : (ext + 1) * 288, :32]
                put(ext, jnp.dot(shapes, own2[ext - 2], preferred_element_type=F32), False)

    if piece:
        out[...] = refs[0][...]
    rows = []
    for row in range(8):
        mixed = None
        for k in range(3):
            total = None
            for slot in range(5):
                factor = factor_of(amps, first, begin + row + slot, k, 4 - slot) * (-1.0 if k == 1 else 1.0)
                at = (row + slot) * 288 + k * PAD
                term = spread[at : at + PAD, :] * factor
                total = term if total is None else total + term
            term = lax.dot_general(total.astype(BF16), weight[k], (((1,), (1,)), ((), ())), preferred_element_type=F32)
            mixed = term if mixed is None else mixed + term
        rows.append(mixed[None, :COLS])
    out[0, :, begin : begin + 8, :] = jnp.swapaxes(jnp.concatenate(rows, axis=0), 0, 1)
    token[...] = before[...]


def sum_kernel(count, *refs):
    parts = [ref[...] for ref in refs[:count]]
    while len(parts) > 1:
        parts = [parts[i] + parts[i + 1] for i in range(0, len(parts), 2)]
    refs[-2][...] = parts[0]
    refs[-1][...] = jnp.zeros((8, 128), F32)


def join_kernel(info, mine, other, out):
    scale = 1.0 / math.sqrt(4 * 128 * 720)
    core = info[0] % 2
    out[pl.ds(pl.multiple_of(core * 192, 192), 192), :] = mine[...] * scale
    out[pl.ds(pl.multiple_of((1 - core) * 192, 192), 192), :] = other[...] * scale


def pairs_of_lon(parity, lats):
    out = []
    for lat in lats:
        for lon in range(8):
            other = lon ^ 1 if parity == 0 else ((lon + 1) % 8 if lon % 2 else (lon - 1) % 8)
            out.append((lat * 8 + lon, lat * 8 + other))
    return out


def pairs_of_lat(parity):
    out = []
    for lat in range(8):
        other = lat ^ 1 if parity == 0 else (lat + 1 if lat % 2 else lat - 1)
        if 0 <= other < 8:
            out.append((lat, other))
    return out


def z_pairs():
    across = {0: 6, 6: 0, 1: 7, 7: 1, 2: 4, 4: 2, 3: 5, 5: 3}
    out = []
    for lat in range(8):
        for lon in range(8):
            other = across[(lon >> 2) * 4 + (lat >> 1)]
            out.append((lat * 8 + lon, ((other % 4) * 2 + lat % 2) * 8 + (other // 4) * 4 + lon % 4))
    return out


def flip(x, axis, bit):
    return lax.ppermute(x, axis, [(i, i ^ bit) for i in range(lax.axis_size(axis))])


VMEM = pl.BlockSpec(memory_space=pltpu.VMEM)
SMEM = pl.BlockSpec(memory_space=pltpu.SMEM)


def call(kernel, outs, scratch, flops, scalars, arrays, limit=12, space=pltpu.VMEM):
    moved = sum(math.prod(x.shape) * x.dtype.itemsize for x in (*arrays, *outs))
    return pl.pallas_call(
        kernel,
        out_shape=outs,
        in_specs=[SMEM] * len(scalars) + [pl.BlockSpec(memory_space=space)] * len(arrays),
        out_specs=[VMEM] * len(outs),
        scratch_shapes=scratch,
        compiler_params=pltpu.CompilerParams(vmem_limit_bytes=limit * 1024 * 1024),
        cost_estimate=pl.CostEstimate(flops=flops, bytes_accessed=moved, transcendentals=0),
    )(*scalars, *arrays)


def shape(dims, dtype=BF16):
    return jax.ShapeDtypeStruct(dims, dtype)


def body(features, cotangent, mix_weight, amplitude, row_spans):
    lat, lon = lax.axis_index("lat"), lax.axis_index("lon")
    info = jnp.stack([lat, lon, lat * ROWS]).astype(jnp.int32)
    amps = amplitude.transpose(2, 0, 1)

    field, cot = features.transpose(0, 2, 1, 3), cotangent.transpose(0, 2, 1, 3)
    token = shape((8, 128), F32)
    near = shape((2, OTHERS, ROWS, CHAN))
    second = shape((2, SECOND, ROWS, CHAN))
    polar = shape((2, COLS + POLAR_FAR, 8, CHAN))
    *messages, before = call(
        pack_kernel,
        [near, second, polar, second, polar, token],
        [pltpu.VMEM((2, COLS, ROWS, CHAN), BF16), pltpu.SemaphoreType.DMA((12,))],
        0,
        (info,),
        (field, cot),
        limit=56,
        space=pl.ANY,
    )
    targets = ((1, range(2, 8)), (1, (1,)), (1, (0,)), (0, range(1, 8)), (0, (0,)))
    got = [None] * 5
    for index in (2, 1, 0, 4, 3):
        got[index] = lax.ppermute(messages[index], LL, pairs_of_lon(*targets[index]))

    gathered = shape((ROWS, 128, CHAN))
    tables = [shape((20 * 288, 128)), shape((20 * 288, 128)), shape((5 * 288, 128))]
    own_f, own_c, *shapes = call(
        pre_kernel, [gathered, gathered, *tables], [], 2 * 10**8, (info, row_spans), (field, cot, before)
    )
    own2 = shape((5, 32, CHAN))
    own0_f, own0_c, own1_f, own1_c, own2_f, own2_c, lat_a, lat_b = call(
        assemble_kernel,
        [gathered] * 4 + [own2] * 2 + [shape((2, 2, 160, CHAN)), shape((2, 2, 128, CHAN))],
        [],
        0,
        (info,),
        (own_f, own_c, *got),
    )
    halo_a = lax.ppermute(lat_a, "lat", pairs_of_lat(0))
    halo_b = lax.ppermute(lat_b, "lat", pairs_of_lat(1))

    row_flops = 2 * 288 * 640 * CHAN
    scalars = (info, amps)
    filters = (own0_f, own1_f, own2_f, *shapes, own0_c)
    inner, part = call(inner_kernel, [shape((12 * PAD, 384)), shape((128, 384), F32)], [], 12 * row_flops, scalars, filters)
    half = shape((192, CHAN), F32)
    outer, mine, other = call(
        outer_kernel,
        [shape((4 * PAD, 384)), half, half],
        [pltpu.VMEM((384, CHAN), F32)],
        4 * row_flops,
        scalars,
        (*filters, halo_a, halo_b, part),
    )

    def add(*parts, after=()):
        return call(functools.partial(sum_kernel, len(parts)), [half, token], [], 0, (), (*parts, *after))

    def back(piece, before, *done):
        return call(
            functools.partial(back_kernel, piece),
            [shape((1, COLS, ROWS, CHAN), F32), token],
            [pltpu.VMEM((12 * 288, CHAN), F32)],
            2 * row_flops,
            scalars,
            (own0_c, own1_c, own2_c, *shapes, halo_a, halo_b, mix_weight, before, *done),
        )

    mine, before = add(mine, flip(other, "lat", 1))
    steps = [flip(mine, "dp", bit) for bit in (1, 2, 3)]
    grad, done = back(0, before)
    mine, before = add(mine, *steps, after=(done,))
    steps = [flip(mine, "lon", bit) for bit in (1, 2, 3)]
    grad, done = back(1, before, grad)
    mine, before = add(mine, *steps, after=(done,))
    step = flip(mine, "lat", 2)
    convolved, done = call(
        mix_kernel,
        [shape((1, COLS, ROWS, CHAN)), token],
        [],
        2 * ROWS * PAD * 384 * CHAN,
        (),
        (inner, outer, mix_weight.reshape(384, CHAN), before),
    )
    mine, _ = add(mine, step, after=(done,))
    mine, _ = add(mine, flip(mine, "lat", 4))
    mine, _ = add(mine, lax.ppermute(mine, LL, z_pairs()))
    other = flip(mine, "lat", 1)
    (whole,) = call(join_kernel, [shape((384, CHAN), F32)], [], 0, (info,), (mine, other))
    return convolved.transpose(0, 2, 1, 3), grad.transpose(0, 2, 1, 3), whole.reshape(3, 128, 128)


def solution(mesh):
    cells = P("dp", "lat", "lon", None)
    return jax.shard_map(
        body,
        mesh=mesh,
        in_specs=(cells, cells, P(), P(), P()),
        out_specs=(cells, cells, P()),
        check_vma=False,
    )
```

```python
import functools
import math

import jax
import jax.numpy as jnp
from jax import lax
from jax.experimental import pallas as pl
from jax.experimental.pallas import tpu as pltpu
from jax.sharding import PartitionSpec as P

ROWS = 16
COLS = 90
CHAN = 128
PAD = 96
F32 = jnp.float32
BF16 = jnp.bfloat16
LL = ("lat", "lon")
POLAR_FAR = 40
SECOND = 18
OTHERS = 9


def offsets_of(group):
    col = lax.broadcasted_iota(jnp.int32, (PAD, 128), 0)
    lane = lax.broadcasted_iota(jnp.int32, (PAD, 128), 1)
    none = jnp.full((PAD, 128), 1000000, jnp.int32)
    if group == 0:
        source = jnp.where(lane < PAD, lane, jnp.where(lane < PAD + 16, lane - 112, lane - 22))
        source = jnp.where((lane >= COLS) & (lane < PAD), none, source)
    elif group == 1:
        source = jnp.where(lane < 64, lane - 80, lane + 42)
    else:
        source = jnp.where(lane < 16, lane - 90, lane + 148)
        source = jnp.where((lane >= 10) & (lane < 22), none, source)
        source = jnp.where(lane >= 32, none, source)
    return (source - col).astype(F32)


def fill_shapes(table, offsets, spans, first, low, high):
    def fill(row, carry):
        span = spans[row_of(first, row)].astype(F32)
        divisor = jnp.full((1, 128), span + 1.0, F32)
        norm = lax.rsqrt(divisor)
        inside = jnp.abs(offsets) <= span
        scaled = jnp.where(inside, offsets * (1.0 / divisor), 0.0)
        square = scaled * scaled
        half = jnp.full(square.shape, 4.7108746e-07, F32)
        for term in (-2.5202042e-05, 9.1926025e-04, -2.0863481e-02, 2.5366950e-01, -1.2337005, 1.0):
            half = half * square + term
        cosine = 2.0 * half * half - 1.0
        shapes = (1.0 - jnp.abs(scaled), scaled, cosine)
        for k in range(3):
            at = pl.multiple_of(row * 288 + k * PAD, PAD)
            value = jnp.where(inside, shapes[k] * norm, 0.0)
            high = value.astype(BF16)
            table[pl.ds(at, PAD), :128] = high
            table[pl.ds(at, PAD), 128:] = (value - high.astype(F32)).astype(BF16)
        return carry

    def four(index, carry):
        for part in range(4):
            fill(low + index * 4 + part, carry)
        return carry

    lax.fori_loop(0, (high - low) // 4, four, 0)
    lax.fori_loop(low + (high - low) // 4 * 4, high, fill, 0)


def position():
    lat = lax.axis_index("lat")
    return lat, lat * ROWS


def row_of(first, ext):
    if isinstance(ext, int) and 2 <= ext < 18:
        return first + ext - 2
    return jnp.clip(first + ext - 2, 0, 127)


def factor_of(amps, first, ext, k, tap):
    return amps[tap, k, row_of(first, ext)]


def pack_kernel(field, cot, near_a, second_a, polar_a, second_b, polar_b, whole, sems):
    odd = lax.axis_index("lon") % 2 == 1

    def edges(is_odd):
        copies = []
        for which, source in enumerate((field, cot)):
            for out, width, right in ((near_a, OTHERS, is_odd), (second_a, SECOND, is_odd), (second_b, SECOND, not is_odd)):
                begin = COLS - width if right else 0
                copies.append((source.at[0, begin : begin + width], out.at[which]))
        copies = [pltpu.make_async_copy(a, b, sems.at[i]) for i, (a, b) in enumerate(copies)]
        for copy in copies:
            copy.start()

        @pl.when(lax.axis_index("lat") == 0)
        def _():
            loads = []
            for which, source in enumerate((field, cot)):
                for part in range(3):
                    at = pl.ds(part * 30, 30)
                    sem = sems.at[6 + which * 3 + part]
                    loads.append(pltpu.make_async_copy(source.at[0, at], whole.at[which, at], sem))
            for load in loads:
                load.start()
            for load in loads:
                load.wait()
            for which in range(2):
                low = jnp.concatenate([whole[which, :45, :8], whole[which, 45:, :8]], axis=1)
                left = jnp.concatenate([whole[which, :20, 8:], whole[which, 20:40, 8:]], axis=1)
                right = jnp.concatenate([whole[which, 50:70, 8:], whole[which, 70:, 8:]], axis=1)
                polar_a[which, :45] = low
                polar_b[which, :45] = low
                polar_a[which, 45:] = right if is_odd else left
                polar_b[which, 45:] = left if is_odd else right

        for copy in copies:
            copy.wait()

    pl.when(odd)(lambda: edges(True))
    pl.when(jnp.logical_not(odd))(lambda: edges(False))


def pre_kernel(spans, field, cot, own_f, own_c, shape0, shape1, shape2, whole, sems):
    lat, first = position()
    loads = []
    for which, source in enumerate((field, cot)):
        for part in range(3):
            at = pl.ds(part * 30, 30)
            loads.append(pltpu.make_async_copy(source.at[0, at], whole.at[which, at], sems.at[which * 3 + part]))
    for load in loads:
        load.start()
    fill_shapes(shape0, offsets_of(0), spans, first, 0, 20)

    @pl.when(lat < 2)
    def _():
        low = jnp.where(lat == 0, 2, 0)
        fill_shapes(shape1, offsets_of(1), spans, first, low, jnp.where(lat == 0, 18, 2))

    @pl.when(lat == 0)
    def _():
        fill_shapes(shape2, offsets_of(2), spans, first, 2, 5)

    for load in loads:
        load.wait()
    for which, own in enumerate((own_f, own_c)):
        own[:, COLS:, :] = jnp.zeros((ROWS, 128 - COLS, CHAN), BF16)
        own[:, :COLS, :] = jnp.swapaxes(whole[which], 0, 1)


def assemble_kernel(old_f, old_c, near_a, second_a, polar_a, second_b, polar_b, *outs):
    lat = lax.axis_index("lat")
    odd = lax.axis_index("lon") % 2 == 1
    groups = ((outs[0], outs[2], outs[4]), (outs[1], outs[3], outs[5]))
    lat_a, lat_b = outs[6], outs[7]

    def left_right(a_ref, b_ref, which, lo, hi):
        left = jnp.where(odd, b_ref[which, lo:hi], a_ref[which, lo:hi])
        right = jnp.where(odd, a_ref[which, lo:hi], b_ref[which, lo:hi])
        return jnp.swapaxes(left, 0, 1), jnp.swapaxes(right, 0, 1)

    for which in range(2):
        own0, own1, own2 = groups[which]
        own0[...] = (old_f, old_c)[which][...]

        @pl.when(lat >= 2)
        def _(which=which, own0=own0):
            a = near_a[which]
            left = jnp.where(odd, second_b[which, SECOND - OTHERS :], a)
            right = jnp.where(odd, a, second_b[which, :OTHERS])
            own0[:, 112 - OTHERS : 112, :] = jnp.swapaxes(left, 0, 1)
            own0[:, 112 : 112 + OTHERS, :] = jnp.swapaxes(right, 0, 1)

        @pl.when(lat == 1)
        def _(which=which, own0=own0, own1=own1):
            left, right = left_right(second_a, second_b, which, 0, SECOND)
            own0[:, 96:112, :] = left[:, 2:]
            own0[:, 112:128, :] = right[:, :16]
            own1[...] = jnp.zeros(own1.shape, BF16)
            own1[:, 62:64, :] = left[:, :2]
            own1[:, 64:66, :] = right[:, 16:]

        @pl.when(lat == 0)
        def _(which=which, own0=own0, own1=own1, own2=own2):
            a, b = polar_a[which], polar_b[which]
            left, right = jnp.where(odd, b, a), jnp.where(odd, a, b)

            def opened(lo, hi):
                return [jnp.swapaxes(jnp.concatenate([x[lo:hi, :8], x[lo:hi, 8:]], axis=0), 0, 1) for x in (left, right)]

            high_left, high_right = opened(45, 65)
            left, right = opened(0, 45)
            own0[:8, 96:112, :] = left[:, 74:90]
            own0[:8, 112:128, :] = right[:, 0:16]
            own1[:8, :64, :] = left[:, 10:74]
            own1[:8, 64:, :] = right[:, 16:80]
            own2[:, :16, :] = left[:5, 0:16]
            own2[:, 16:, :] = right[:5, 74:90]
            left, right = high_left, high_right
            own0[8:, 96:112, :] = left[:, 24:40]
            own0[8:, 112:128, :] = right[:, 0:16]
            own1[8:] = jnp.zeros((8, 128, CHAN), BF16)
            own1[8:, 40:64, :] = left[:, 0:24]
            own1[8:, 64:88, :] = right[:, 16:40]

        even = lat % 2 == 0
        for row in range(2):
            lat_a[which, row, :128, :] = jnp.where(even, own0[14 + row], own0[row])
            lat_a[which, row, 128:, :] = jnp.where(even, own1[14 + row, 48:80, :], own1[row, 48:80, :])
            lat_b[which, row, :128, :] = jnp.where(even, own0[row], own0[14 + row])


def tapped(amps, first, ext, rows):
    factors = [[factor_of(amps, first, ext, k, tap) for tap in range(5)] for k in range(3)]
    height = rows[0].shape[0]
    parts = [[] for _ in range(3)]
    for at in range(0, height, 32):
        wide = [row[at : at + 32].astype(F32) for row in rows]
        for k in range(3):
            total = wide[0] * factors[k][0]
            for tap in range(1, 5):
                total += wide[tap] * factors[k][tap]
            parts[k].append(total.astype(BF16))
    return [jnp.concatenate(part, axis=0) if len(part) > 1 else part[0] for part in parts]


def filtered(table, at, amps, first, ext, rows):
    out = []
    for k, taps in enumerate(tapped(amps, first, ext, rows)):
        shapes = rows_at(table, at + k * PAD, PAD)
        if taps.shape[0] < 128:
            shapes = jnp.concatenate([shapes[:, : taps.shape[0]], shapes[:, 128 : 128 + taps.shape[0]]], axis=1)
        out.append(jnp.dot(shapes, jnp.concatenate([taps, taps], axis=0), preferred_element_type=F32))
    return out


def plus(values, more):
    return [x + y for x, y in zip(values, more)]


def rows_at(ref, start, count=288):
    return ref[pl.ds(start if isinstance(start, int) else pl.multiple_of(start, 32), count), :]


def store_basis(basis, row, values):
    at = row * PAD if isinstance(row, int) else pl.multiple_of(row * PAD, PAD)
    for k in range(3):
        basis[pl.ds(at, PAD), k * 128 : (k + 1) * 128] = values[k].astype(BF16)


def times_cotangent(cot, basis):
    return lax.dot_general(cot, basis, (((0,), (0,)), ((), ())), preferred_element_type=F32)


def inner_kernel(amps, own0, own1, own2, shape0, shape1, shape2, cot, basis, part):
    lat, first = position()

    def one(row, wide, extra=None):
        at = (row + 2) * 288
        values = filtered(shape0, at, amps, first, row + 2, [own0[row - 2 + tap] for tap in range(5)])
        if wide:
            values = plus(values, filtered(shape1, at, amps, first, row + 2, [own1[row - 2 + tap] for tap in range(5)]))
        store_basis(basis, row - 2, values if extra is None else plus(values, extra))

    def loop(start, wide):
        for row in range(start, 14):
            one(row, wide)

    @pl.when(lat != 0)
    def _():
        loop(2, False)

    @pl.when(lat == 0)
    def _():
        far = filtered(shape2, 4 * 288, amps, first, 4, [own2[tap] for tap in range(5)])
        one(2, True, far)
        loop(3, True)

    part[...] = times_cotangent(cot[2:14, :PAD, :].reshape(12 * PAD, CHAN), basis[...])


def halo_row(halo_a, halo_b, which, row, even, top):
    a, b = halo_a[which, row, :128], halo_b[which, row, :128]
    return jnp.where(even, b, a) if top else jnp.where(even, a, b)


def far_halo_row(halo_a, which, row):
    zeros = jnp.zeros((48, CHAN), BF16)
    return jnp.concatenate([zeros, halo_a[which, row, 128:], zeros], axis=0)


def outer_kernel(amps, own0, own1, own2, shape0, shape1, shape2, cot, halo_a, halo_b, part, basis, mine, other, grad):
    lat, first = position()
    even = lat % 2 == 0

    def run(wide):
        for place, row in enumerate((0, 1, 14, 15)):
            near, far, last = [], [], []
            for at in range(row - 2, row + 3):
                inside = 0 <= at < ROWS
                if inside:
                    near.append(own0[at])
                else:
                    near.append(halo_row(halo_a, halo_b, 0, at + 2 if at < 0 else at - ROWS, even, at < 0))
                if wide:
                    zeros = jnp.zeros((128, CHAN), BF16)
                    far.append(own1[at] if inside else zeros if at < 0 else far_halo_row(halo_a, 0, at - ROWS))
                    last.append(own2[at] if 0 <= at < 5 else zeros[:32])
            at = (row + 2) * 288
            values = filtered(shape0, at, amps, first, row + 2, near)
            if wide:
                values = plus(values, filtered(shape1, at, amps, first, row + 2, far))
            if wide and row < 2:
                values = plus(values, filtered(shape2, at, amps, first, row + 2, last))
            store_basis(basis, place, values)

    pl.when(lat != 0)(lambda: run(False))
    pl.when(lat == 0)(lambda: run(True))
    ends = jnp.concatenate([cot[0:2, :PAD, :], cot[14:16, :PAD, :]], axis=0).reshape(4 * PAD, CHAN)
    product = part[...] + times_cotangent(ends, basis[...])
    for k in range(3):
        grad[k * 128 : (k + 1) * 128, :] = product[:, k * 128 : (k + 1) * 128].T
    core = lat % 2
    mine[...] = grad[pl.ds(pl.multiple_of(core * 192, 192), 192), :]
    other[...] = grad[pl.ds(pl.multiple_of((1 - core) * 192, 192), 192), :]


def mix_kernel(inner, outer, weight, before, out, token):
    w = weight[...]

    def mixed(basis, rows):
        return jnp.dot(basis, w, preferred_element_type=F32).astype(BF16).reshape(rows, PAD, CHAN)[:, :COLS]

    ends = mixed(outer[...], 4)
    whole = jnp.concatenate([ends[:2], mixed(inner[...], 12), ends[2:]], axis=0)
    out[0] = jnp.swapaxes(whole, 0, 1)
    token[...] = before[...]


def back_kernel(piece, amps, own0, own1, own2, shape0, shape1, shape2, halo_a, halo_b, weight, before, *refs):
    out, token, spread, joined = refs[-4:]
    lat, first = position()
    even = lat % 2 == 0
    begin = 8 * piece

    def put(index, value, fresh):
        at = index * 288 if isinstance(index, int) else pl.multiple_of(index * 288, 32)
        if fresh:
            spread[pl.ds(at, 288), :] = value
        else:
            spread[pl.ds(at, 288), :] += value

    def twice(shapes, rows):
        return jnp.dot(shapes, jnp.concatenate([rows, rows], axis=0), preferred_element_type=F32)

    def own_rows(low, high, wide):
        for ext in range(low, high):
            value = twice(rows_at(shape0, ext * 288), own0[ext - 2])
            if wide:
                value += twice(rows_at(shape1, ext * 288), own1[ext - 2])
            put(ext - begin, value, True)

    low, high = max(begin, 2), min(begin + 12, 18)
    pl.when(lat != 0)(lambda: own_rows(low, high, False))
    pl.when(lat == 0)(lambda: own_rows(low, high, True))
    for row in range(2):
        ext = row if piece == 0 else 18 + row
        gathered = halo_row(halo_a, halo_b, 1, row, even, piece == 0)
        put(ext - begin, twice(shape0[ext * 288 : (ext + 1) * 288, :], gathered), True)
    if piece == 0:

        @pl.when(lat == 1)
        def _():
            for row in range(2):
                far = far_halo_row(halo_a, 1, row)
                put(row, twice(shape1[row * 288 : (row + 1) * 288, :], far), False)

        @pl.when(lat == 0)
        def _():
            for ext in range(2, 5):
                at = slice(ext * 288, (ext + 1) * 288)
                shapes = jnp.concatenate([shape2[at, :32], shape2[at, 128:160]], axis=1)
                put(ext, twice(shapes, own2[ext - 2]), False)

    if piece:
        out[...] = refs[0][...]
    for row in range(8):
        for k in range(3):
            total = None
            for slot in range(5):
                factor = factor_of(amps, first, begin + row + slot, k, 4 - slot) * (-1.0 if k == 1 else 1.0)
                at = (row + slot) * 288 + k * PAD
                term = spread[at : at + PAD, :] * factor
                total = term if total is None else total + term
            joined[row * PAD : (row + 1) * PAD, k * 128 : (k + 1) * 128] = total.astype(BF16)
    weights = jnp.concatenate([weight[k] for k in range(3)], axis=1)
    mixed = lax.dot_general(joined[...], weights, (((1,), (1,)), ((), ())), preferred_element_type=F32)
    out[0, :, begin : begin + 8, :] = jnp.swapaxes(mixed.reshape(8, PAD, CHAN)[:, :COLS], 0, 1)
    token[...] = before[...]


def sum_kernel(count, *refs):
    parts = [ref[...] for ref in refs[:count]]
    while len(parts) > 1:
        parts = [parts[i] + parts[i + 1] for i in range(0, len(parts), 2)]
    out, *token = refs[-2:] if refs[-1].shape[0] == 8 else refs[-1:]
    out[...] = parts[0]
    if token:
        token[0][...] = jnp.zeros((8, 128), F32)


def pairs_of_lon(parity, lats):
    out = []
    for lat in lats:
        for lon in range(8):
            other = lon ^ 1 if parity == 0 else ((lon + 1) % 8 if lon % 2 else (lon - 1) % 8)
            out.append((lat * 8 + lon, lat * 8 + other))
    return out


def pairs_of_lat(parity):
    out = []
    for lat in range(8):
        other = lat ^ 1 if parity == 0 else (lat + 1 if lat % 2 else lat - 1)
        if 0 <= other < 8:
            out.append((lat, other))
    return out


def z_pairs():
    across = {0: 6, 6: 0, 1: 7, 7: 1, 2: 4, 4: 2, 3: 5, 5: 3}
    out = []
    for lat in range(8):
        for lon in range(8):
            other = across[(lon >> 2) * 4 + (lat >> 1)]
            out.append((lat * 8 + lon, ((other % 4) * 2 + lat % 2) * 8 + (other // 4) * 4 + lon % 4))
    return out


def flip(x, axis, bit):
    return lax.ppermute(x, axis, [(i, i ^ bit) for i in range(lax.axis_size(axis))])


VMEM = pl.BlockSpec(memory_space=pltpu.VMEM)
SMEM = pl.BlockSpec(memory_space=pltpu.SMEM)


def call(kernel, outs, scratch, flops, scalars, arrays, limit=12, space=pltpu.VMEM):
    moved = sum(math.prod(x.shape) * x.dtype.itemsize for x in (*arrays, *outs))
    return pl.pallas_call(
        kernel,
        out_shape=outs,
        in_specs=[SMEM] * len(scalars) + [pl.BlockSpec(memory_space=space)] * len(arrays),
        out_specs=[VMEM] * len(outs),
        scratch_shapes=scratch,
        compiler_params=pltpu.CompilerParams(vmem_limit_bytes=limit * 1024 * 1024),
        cost_estimate=pl.CostEstimate(flops=flops, bytes_accessed=moved, transcendentals=0),
    )(*scalars, *arrays)


def shape(dims, dtype=BF16):
    return jax.ShapeDtypeStruct(dims, dtype)


def body(features, cotangent, mix_weight, amplitude, row_spans):
    amps = amplitude.transpose(2, 0, 1)

    field, cot = features.transpose(0, 2, 1, 3), cotangent.transpose(0, 2, 1, 3)
    field, cot = (pltpu.with_memory_space_constraint(x, pltpu.HBM) for x in (field, cot))
    token = shape((8, 128), F32)
    near = shape((2, OTHERS, ROWS, CHAN))
    second = shape((2, SECOND, ROWS, CHAN))
    polar = shape((2, 65, ROWS, CHAN))
    scratch = [
        pltpu.VMEM((2, COLS, ROWS, CHAN), BF16),
        pltpu.SemaphoreType.DMA((12,)),
    ]
    messages = call(
        pack_kernel,
        [near, second, polar, second, polar],
        scratch,
        0,
        (),
        (field, cot),
        space=pltpu.HBM,
    )
    targets = ((1, range(2, 8)), (1, (1,)), (1, (0,)), (0, range(1, 8)), (0, (0,)))
    got = [None] * 5
    for index in (2, 1, 0, 4, 3):
        got[index] = lax.ppermute(messages[index], LL, pairs_of_lon(*targets[index]))

    gathered = shape((ROWS, 128, CHAN))
    tables = [shape((20 * 288, 256)), shape((20 * 288, 256)), shape((5 * 288, 256))]
    own_f, own_c, *shapes = call(
        pre_kernel,
        [gathered, gathered, *tables],
        [pltpu.VMEM((2, COLS, ROWS, CHAN), BF16), pltpu.SemaphoreType.DMA((6,))],
        2 * 10**8,
        (row_spans,),
        (field, cot),
        space=pltpu.HBM,
    )
    own2 = shape((5, 32, CHAN))
    own0_f, own0_c, own1_f, own1_c, own2_f, own2_c, lat_a, lat_b = call(
        assemble_kernel,
        [gathered] * 4 + [own2] * 2 + [shape((2, 2, 160, CHAN)), shape((2, 2, 176, CHAN))],
        [],
        0,
        (),
        (own_f, own_c, *got),
    )
    halo_a = lax.ppermute(lat_a, "lat", pairs_of_lat(0))
    halo_b = lax.ppermute(lat_b, "lat", pairs_of_lat(1))

    row_flops = 2 * 288 * 640 * CHAN
    scalars = (amps,)
    filters = (own0_f, own1_f, own2_f, *shapes, own0_c)
    inner, part = call(inner_kernel, [shape((12 * PAD, 384)), shape((128, 384), F32)], [], 12 * row_flops, scalars, filters)
    half = shape((192, CHAN), F32)
    outer, mine, other = call(
        outer_kernel,
        [shape((4 * PAD, 384)), half, half],
        [pltpu.VMEM((384, CHAN), F32)],
        4 * row_flops,
        scalars,
        (*filters, halo_a, halo_b, part),
    )

    def add(*parts, after=(), more=True):
        outs = [half, token] if more else [half]
        return call(functools.partial(sum_kernel, len(parts)), outs, [], 0, (), (*parts, *after))

    def back(piece, before, *done):
        return call(
            functools.partial(back_kernel, piece),
            [shape((1, COLS, ROWS, CHAN), F32), token],
            [pltpu.VMEM((12 * 288, CHAN), F32), pltpu.VMEM((8 * PAD, 384), BF16)],
            2 * row_flops,
            scalars,
            (own0_c, own1_c, own2_c, *shapes, halo_a, halo_b, mix_weight, before, *done),
        )

    mine, before = add(mine, flip(other, "lat", 1))
    steps = [flip(mine, "dp", bit) for bit in (1, 2, 3)]
    convolved, done = call(
        mix_kernel,
        [shape((1, COLS, ROWS, CHAN)), token],
        [],
        2 * ROWS * PAD * 384 * CHAN,
        (),
        (inner, outer, mix_weight.reshape(384, CHAN), before),
    )
    (mine,) = add(mine, *steps, after=(done,), more=False)
    steps = [flip(mine, "lon", bit) for bit in (1, 2, 3)]
    mine, before = add(mine, *steps)
    steps = [flip(mine, "lat", bit) for bit in (2, 4, 6)]
    grad, done = back(0, before)
    mine, before = add(mine, *steps, after=(done,))
    step = lax.ppermute(mine, LL, z_pairs())
    grad, done = back(1, before, grad)
    (mine,) = add(mine, step, after=(done,), more=False)
    other = flip(mine, "lat", 1)
    first_half = lax.axis_index("lat") % 2 == 0
    whole = jnp.concatenate([jnp.where(first_half, mine, other), jnp.where(first_half, other, mine)])
    whole = whole * (1.0 / math.sqrt(4 * 128 * 720))
    return convolved.transpose(0, 2, 1, 3), grad.transpose(0, 2, 1, 3), whole.reshape(3, 128, 128)


def solution(mesh):
    cells = P("dp", "lat", "lon", None)
    return jax.shard_map(
        body,
        mesh=mesh,
        in_specs=(cells, cells, P(), P(), P()),
        out_specs=(cells, cells, P()),
        check_vma=False,
    )
```

```python
import functools
import math

import jax
import jax.numpy as jnp
from jax import lax
from jax.experimental import pallas as pl
from jax.experimental.pallas import tpu as pltpu
from jax.sharding import PartitionSpec as P

ROWS = 16
COLS = 90
CHAN = 128
PAD = 96
F32 = jnp.float32
BF16 = jnp.bfloat16
LL = ("lat", "lon")
POLAR_FAR = 40
SECOND = 18
OTHERS = 9


def offsets_of(group):
    col = lax.broadcasted_iota(jnp.int32, (PAD, 128), 0)
    lane = lax.broadcasted_iota(jnp.int32, (PAD, 128), 1)
    none = jnp.full((PAD, 128), 1000000, jnp.int32)
    if group == 0:
        source = jnp.where(lane < PAD, lane, jnp.where(lane < PAD + 16, lane - 112, lane - 22))
        source = jnp.where((lane >= COLS) & (lane < PAD), none, source)
    elif group == 1:
        source = jnp.where(lane < 64, lane - 80, lane + 42)
    else:
        source = jnp.where(lane < 16, lane - 90, lane + 148)
        source = jnp.where((lane >= 10) & (lane < 22), none, source)
        source = jnp.where(lane >= 32, none, source)
    return (source - col).astype(F32)


def fill_shapes(table, offsets, spans, first, low, high):
    def fill(row, carry):
        span = spans[row_of(first, row)].astype(F32)
        divisor = jnp.full((1, 128), span + 1.0, F32)
        norm = lax.rsqrt(divisor)
        inside = jnp.abs(offsets) <= span
        scaled = jnp.where(inside, offsets * (1.0 / divisor), 0.0)
        square = scaled * scaled
        half = jnp.full(square.shape, 4.7108746e-07, F32)
        for term in (-2.5202042e-05, 9.1926025e-04, -2.0863481e-02, 2.5366950e-01, -1.2337005, 1.0):
            half = half * square + term
        cosine = 2.0 * half * half - 1.0
        shapes = (1.0 - jnp.abs(scaled), scaled, cosine)
        for k in range(3):
            at = pl.multiple_of(row * 288 + k * PAD, PAD)
            value = jnp.where(inside, shapes[k] * norm, 0.0)
            high = value.astype(BF16)
            table[pl.ds(at, PAD), :128] = high
            table[pl.ds(at, PAD), 128:] = (value - high.astype(F32)).astype(BF16)
        return carry

    def four(index, carry):
        for part in range(4):
            fill(low + index * 4 + part, carry)
        return carry

    lax.fori_loop(0, (high - low) // 4, four, 0)
    lax.fori_loop(low + (high - low) // 4 * 4, high, fill, 0)


def position():
    lat = lax.axis_index("lat")
    return lat, lat * ROWS


def row_of(first, ext):
    if isinstance(ext, int) and 2 <= ext < 18:
        return first + ext - 2
    return jnp.clip(first + ext - 2, 0, 127)


def factor_of(amps, first, ext, k, tap):
    return amps[tap, k, row_of(first, ext)]


def pack_kernel(field, cot, near_a, second_a, polar_a, near_b, polar_b, whole, sems):
    lat, odd = lax.axis_index("lat"), lax.axis_index("lon") % 2 == 1

    def edges(is_odd):
        def part(out, width, right, sem):
            source, target = pl.ds(COLS - width if right else 0, width), pl.ds(0, width)
            return [
                pltpu.make_async_copy(x.at[0, source], out.at[i, target], sems.at[sem + i]) for i, x in enumerate((field, cot))
            ]

        def run(copies):
            for copy in copies:
                copy.start()
            for copy in copies:
                copy.wait()

        pl.when(lat >= 2)(lambda: run(part(near_a, OTHERS + 1, is_odd, 0) + part(near_b, OTHERS, not is_odd, 2)))
        pl.when(lat == 1)(lambda: run(part(second_a, SECOND, is_odd, 0) + part(polar_b, SECOND, not is_odd, 2)))

        @pl.when(lat == 0)
        def _():
            loads = []
            for which, source in enumerate((field, cot)):
                for part in range(3):
                    at = pl.ds(part * 30, 30)
                    sem = sems.at[6 + which * 3 + part]
                    loads.append(pltpu.make_async_copy(source.at[0, at], whole.at[which, at], sem))
            for load in loads:
                load.start()
            for load in loads:
                load.wait()
            for which in range(2):
                low = jnp.concatenate([whole[which, :45, :8], whole[which, 45:, :8]], axis=1)
                left = jnp.concatenate([whole[which, :20, 8:], whole[which, 20:40, 8:]], axis=1)
                right = jnp.concatenate([whole[which, 50:70, 8:], whole[which, 70:, 8:]], axis=1)
                polar_a[which, :45] = low
                polar_b[which, :45] = low
                polar_a[which, 45:] = right if is_odd else left
                polar_b[which, 45:] = left if is_odd else right

    pl.when(odd)(lambda: edges(True))
    pl.when(jnp.logical_not(odd))(lambda: edges(False))


def pre_kernel(spans, field, cot, own_f, own_c, shape0, shape1, shape2, whole, sems):
    lat, first = position()
    loads = []
    for which, source in enumerate((field, cot)):
        for part in range(3):
            at = pl.ds(part * 30, 30)
            loads.append(pltpu.make_async_copy(source.at[0, at], whole.at[which, at], sems.at[which * 3 + part]))
    for load in loads:
        load.start()
    fill_shapes(shape0, offsets_of(0), spans, first, 0, 20)

    @pl.when(lat < 2)
    def _():
        low = jnp.where(lat == 0, 2, 0)
        fill_shapes(shape1, offsets_of(1), spans, first, low, jnp.where(lat == 0, 18, 2))

    @pl.when(lat == 0)
    def _():
        fill_shapes(shape2, offsets_of(2), spans, first, 2, 5)

    for load in loads:
        load.wait()
    for which, own in enumerate((own_f, own_c)):
        own[:, COLS:, :] = jnp.zeros((ROWS, 128 - COLS, CHAN), BF16)
        own[:, :COLS, :] = jnp.swapaxes(whole[which], 0, 1)


def assemble_kernel(old_f, old_c, near_a, second_a, polar_a, near_b, polar_b, tie, *outs):
    lat = lax.axis_index("lat")
    odd = lax.axis_index("lon") % 2 == 1
    groups = ((outs[0], outs[2], outs[4]), (outs[1], outs[3], outs[5]))
    lat_a, lat_b = outs[6], outs[7]

    def left_right(a_ref, b_ref, which, lo, hi):
        left = jnp.where(odd, b_ref[which, lo:hi], a_ref[which, lo:hi])
        right = jnp.where(odd, a_ref[which, lo:hi], b_ref[which, lo:hi])
        return jnp.swapaxes(left, 0, 1), jnp.swapaxes(right, 0, 1)

    for which in range(2):
        own0, own1, own2 = groups[which]
        own0[...] = (old_f, old_c)[which][...]

        @pl.when(lat >= 2)
        def _(which=which, own0=own0):
            left = jnp.where(odd, near_b[which], near_a[which, 1:])
            right = jnp.where(odd, near_a[which, :OTHERS], near_b[which])
            own0[:, 112 - OTHERS : 112, :] = jnp.swapaxes(left, 0, 1)
            own0[:, 112 : 112 + OTHERS, :] = jnp.swapaxes(right, 0, 1)

        @pl.when(lat == 1)
        def _(which=which, own0=own0, own1=own1):
            left, right = left_right(second_a, polar_b, which, 0, SECOND)
            own0[:, 96:112, :] = left[:, 2:]
            own0[:, 112:128, :] = right[:, :16]
            own1[...] = jnp.zeros(own1.shape, BF16)
            own1[:, 62:64, :] = left[:, :2]
            own1[:, 64:66, :] = right[:, 16:]

        @pl.when(lat == 0)
        def _(which=which, own0=own0, own1=own1, own2=own2):
            a, b = polar_a[which], polar_b[which]
            left, right = jnp.where(odd, b, a), jnp.where(odd, a, b)

            def opened(lo, hi):
                return [jnp.swapaxes(jnp.concatenate([x[lo:hi, :8], x[lo:hi, 8:]], axis=0), 0, 1) for x in (left, right)]

            high_left, high_right = opened(45, 65)
            left, right = opened(0, 45)
            own0[:8, 96:112, :] = left[:, 74:90]
            own0[:8, 112:128, :] = right[:, 0:16]
            own1[:8, :64, :] = left[:, 10:74]
            own1[:8, 64:, :] = right[:, 16:80]
            own2[:, :16, :] = left[:5, 0:16]
            own2[:, 16:, :] = right[:5, 74:90]
            left, right = high_left, high_right
            own0[8:, 96:112, :] = left[:, 24:40]
            own0[8:, 112:128, :] = right[:, 0:16]
            own1[8:] = jnp.zeros((8, 128, CHAN), BF16)
            own1[8:, 40:64, :] = left[:, 0:24]
            own1[8:, 64:88, :] = right[:, 16:40]

        even = lat % 2 == 0
        for row in range(2):
            lat_a[which, row, :128, :] = jnp.where(even, own0[14 + row], own0[row])
            lat_a[which, row, 128:, :] = jnp.where(even, own1[14 + row, 48:80, :], own1[row, 48:80, :])
            lat_b[which, row, :128, :] = jnp.where(even, own0[row], own0[14 + row])


def tapped(amps, first, ext, rows):
    factors = [[factor_of(amps, first, ext, k, tap) for tap in range(5)] for k in range(3)]
    height = rows[0].shape[0]
    parts = [[] for _ in range(3)]
    for at in range(0, height, 32):
        wide = [row[at : at + 32].astype(F32) for row in rows]
        for k in range(3):
            total = wide[0] * factors[k][0]
            for tap in range(1, 5):
                total += wide[tap] * factors[k][tap]
            parts[k].append(total.astype(BF16))
    return [jnp.concatenate(part, axis=0) if len(part) > 1 else part[0] for part in parts]


def filtered(table, at, amps, first, ext, rows, lane=0):
    out = []
    for k, taps in enumerate(tapped(amps, first, ext, rows)):
        shapes = rows_at(table, at + k * PAD, PAD)
        if taps.shape[0] < 128:
            end = lane + taps.shape[0]
            shapes = jnp.concatenate([shapes[:, lane:end], shapes[:, 128 + lane : 128 + end]], axis=1)
        out.append(jnp.dot(shapes, jnp.concatenate([taps, taps], axis=0), preferred_element_type=F32))
    return out


def plus(values, more):
    return [x + y for x, y in zip(values, more)]


def rows_at(ref, start, count=288):
    return ref[pl.ds(start if isinstance(start, int) else pl.multiple_of(start, 32), count), :]


def store_basis(basis, row, values):
    at = row * PAD if isinstance(row, int) else pl.multiple_of(row * PAD, PAD)
    for k in range(3):
        basis[pl.ds(at, PAD), k * 128 : (k + 1) * 128] = values[k].astype(BF16)


def times_cotangent(cot, basis):
    return lax.dot_general(cot, basis, (((0,), (0,)), ((), ())), preferred_element_type=F32)


def center_kernel(amps, own, shape0, center):
    _, first = position()
    for row in range(2, 14):
        values = filtered(shape0, (row + 2) * 288, amps, first, row + 2, [own[row - 2 + tap, :PAD] for tap in range(5)])
        for k in range(3):
            at = (row - 2) * 288 + k * PAD
            center[at : at + PAD, :] = values[k]


def inner_kernel(amps, center, own0, own1, own2, shape0, shape1, shape2, cot, basis, part):
    lat, first = position()

    def one(row, wide, extra=None):
        at = (row + 2) * 288
        values = filtered(shape0, at, amps, first, row + 2, [own0[row - 2 + tap, PAD:] for tap in range(5)], PAD)
        values = plus(values, [center[(row - 2) * 288 + k * PAD : (row - 2) * 288 + (k + 1) * PAD, :] for k in range(3)])
        if wide:
            values = plus(values, filtered(shape1, at, amps, first, row + 2, [own1[row - 2 + tap] for tap in range(5)]))
        store_basis(basis, row - 2, values if extra is None else plus(values, extra))

    def loop(start, wide):
        for row in range(start, 14):
            one(row, wide)

    @pl.when(lat != 0)
    def _():
        loop(2, False)

    @pl.when(lat == 0)
    def _():
        far = filtered(shape2, 4 * 288, amps, first, 4, [own2[tap] for tap in range(5)])
        one(2, True, far)
        loop(3, True)

    part[...] = times_cotangent(cot[2:14, :PAD, :].reshape(12 * PAD, CHAN), basis[...])


def halo_row(halo_a, halo_b, which, row, even, top):
    a, b = halo_a[which, row, :128], halo_b[which, row, :128]
    return jnp.where(even, b, a) if top else jnp.where(even, a, b)


def far_halo_row(halo_a, which, row):
    zeros = jnp.zeros((48, CHAN), BF16)
    return jnp.concatenate([zeros, halo_a[which, row, 128:], zeros], axis=0)


def outer_kernel(amps, own0, own1, own2, shape0, shape1, shape2, cot, halo_a, halo_b, part, basis, mine, other, grad):
    lat, first = position()
    even = lat % 2 == 0

    def run(wide):
        for place, row in enumerate((0, 1, 14, 15)):
            near, far, last = [], [], []
            for at in range(row - 2, row + 3):
                inside = 0 <= at < ROWS
                if inside:
                    near.append(own0[at])
                else:
                    near.append(halo_row(halo_a, halo_b, 0, at + 2 if at < 0 else at - ROWS, even, at < 0))
                if wide:
                    zeros = jnp.zeros((128, CHAN), BF16)
                    far.append(own1[at] if inside else zeros if at < 0 else far_halo_row(halo_a, 0, at - ROWS))
                    last.append(own2[at] if 0 <= at < 5 else zeros[:32])
            at = (row + 2) * 288
            values = filtered(shape0, at, amps, first, row + 2, near)
            if wide:
                values = plus(values, filtered(shape1, at, amps, first, row + 2, far))
            if wide and row < 2:
                values = plus(values, filtered(shape2, at, amps, first, row + 2, last))
            store_basis(basis, place, values)

    pl.when(lat != 0)(lambda: run(False))
    pl.when(lat == 0)(lambda: run(True))
    ends = jnp.concatenate([cot[0:2, :PAD, :], cot[14:16, :PAD, :]], axis=0).reshape(4 * PAD, CHAN)
    product = part[...] + times_cotangent(ends, basis[...])
    for k in range(3):
        grad[k * 128 : (k + 1) * 128, :] = product[:, k * 128 : (k + 1) * 128].T
    core = lat % 2
    mine[...] = grad[pl.ds(pl.multiple_of(core * 192, 192), 192), :]
    other[...] = grad[pl.ds(pl.multiple_of((1 - core) * 192, 192), 192), :]


def mix_kernel(inner, outer, weight, before, out, token):
    w = weight[...]

    def mixed(basis, rows):
        return jnp.dot(basis, w, preferred_element_type=F32).astype(BF16).reshape(rows, PAD, CHAN)[:, :COLS]

    ends = mixed(outer[...], 4)
    whole = jnp.concatenate([ends[:2], mixed(inner[...], 12), ends[2:]], axis=0)
    out[0] = jnp.swapaxes(whole, 0, 1)
    token[...] = before[...]


def back_kernel(piece, amps, own0, own1, own2, shape0, shape1, shape2, halo_a, halo_b, weight, before, *refs):
    out, token, spread, joined = refs[-4:]
    lat, first = position()
    even = lat % 2 == 0
    begin = 8 * piece

    def put(index, value, fresh):
        at = index * 288 if isinstance(index, int) else pl.multiple_of(index * 288, 32)
        if fresh:
            spread[pl.ds(at, 288), :] = value
        else:
            spread[pl.ds(at, 288), :] += value

    def twice(shapes, rows):
        return jnp.dot(shapes, jnp.concatenate([rows, rows], axis=0), preferred_element_type=F32)

    def own_rows(low, high, wide):
        for ext in range(low, high):
            value = twice(rows_at(shape0, ext * 288), own0[ext - 2])
            if wide:
                value += twice(rows_at(shape1, ext * 288), own1[ext - 2])
            put(ext - begin, value, True)

    low, high = max(begin, 2), min(begin + 12, 18)
    pl.when(lat != 0)(lambda: own_rows(low, high, False))
    pl.when(lat == 0)(lambda: own_rows(low, high, True))
    for row in range(2):
        ext = row if piece == 0 else 18 + row
        gathered = halo_row(halo_a, halo_b, 1, row, even, piece == 0)
        put(ext - begin, twice(shape0[ext * 288 : (ext + 1) * 288, :], gathered), True)
    if piece == 0:

        @pl.when(lat == 1)
        def _():
            for row in range(2):
                far = far_halo_row(halo_a, 1, row)
                put(row, twice(shape1[row * 288 : (row + 1) * 288, :], far), False)

        @pl.when(lat == 0)
        def _():
            for ext in range(2, 5):
                at = slice(ext * 288, (ext + 1) * 288)
                shapes = jnp.concatenate([shape2[at, :32], shape2[at, 128:160]], axis=1)
                put(ext, twice(shapes, own2[ext - 2]), False)

    if piece:
        out[...] = refs[0][...]
    for row in range(8):
        for k in range(3):
            total = None
            for slot in range(5):
                factor = factor_of(amps, first, begin + row + slot, k, 4 - slot) * (-1.0 if k == 1 else 1.0)
                at = (row + slot) * 288 + k * PAD
                term = spread[at : at + PAD, :] * factor
                total = term if total is None else total + term
            joined[row * PAD : (row + 1) * PAD, k * 128 : (k + 1) * 128] = total.astype(BF16)
    weights = jnp.concatenate([weight[k] for k in range(3)], axis=1)
    mixed = lax.dot_general(joined[...], weights, (((1,), (1,)), ((), ())), preferred_element_type=F32)
    out[0, :, begin : begin + 8, :] = jnp.swapaxes(mixed.reshape(8, PAD, CHAN)[:, :COLS], 0, 1)
    token[...] = before[...]


def sum_kernel(count, *refs):
    parts = [ref[...].astype(F32) for ref in refs[:count]]
    while len(parts) > 1:
        parts = [parts[i] + parts[i + 1] for i in range(0, len(parts), 2)]
    out, *token = refs[-2:] if refs[-1].shape[0] == 8 else refs[-1:]
    out[...] = parts[0].astype(out.dtype)
    if token:
        token[0][...] = jnp.zeros((8, 128), F32)


def pairs_of_lon(parity, lats):
    out = []
    for lat in lats:
        for lon in range(8):
            other = lon ^ 1 if parity == 0 else ((lon + 1) % 8 if lon % 2 else (lon - 1) % 8)
            out.append((lat * 8 + lon, lat * 8 + other))
    return out


def pairs_of_lat(parity):
    out = []
    for lat in range(8):
        other = lat ^ 1 if parity == 0 else (lat + 1 if lat % 2 else lat - 1)
        if 0 <= other < 8:
            out.append((lat, other))
    return out


def z_pairs():
    across = {0: 6, 6: 0, 1: 7, 7: 1, 2: 4, 4: 2, 3: 5, 5: 3}
    out = []
    for lat in range(8):
        for lon in range(8):
            other = across[(lon >> 2) * 4 + (lat >> 1)]
            out.append((lat * 8 + lon, ((other % 4) * 2 + lat % 2) * 8 + (other // 4) * 4 + lon % 4))
    return out


def flip(x, axis, bit):
    return lax.ppermute(x, axis, [(i, i ^ bit) for i in range(lax.axis_size(axis))])


VMEM = pl.BlockSpec(memory_space=pltpu.VMEM)
SMEM = pl.BlockSpec(memory_space=pltpu.SMEM)


def call(kernel, outs, scratch, flops, scalars, arrays, limit=12, space=pltpu.VMEM):
    moved = sum(math.prod(x.shape) * x.dtype.itemsize for x in (*arrays, *outs))
    return pl.pallas_call(
        kernel,
        out_shape=outs,
        in_specs=[SMEM] * len(scalars) + [pl.BlockSpec(memory_space=space)] * len(arrays),
        out_specs=[VMEM] * len(outs),
        scratch_shapes=scratch,
        compiler_params=pltpu.CompilerParams(vmem_limit_bytes=limit * 1024 * 1024),
        cost_estimate=pl.CostEstimate(flops=flops, bytes_accessed=moved, transcendentals=0),
    )(*scalars, *arrays)


def shape(dims, dtype=BF16):
    return jax.ShapeDtypeStruct(dims, dtype)


def body(features, cotangent, mix_weight, amplitude, row_spans):
    amps = amplitude.transpose(2, 0, 1)

    field, cot = features.transpose(0, 2, 1, 3), cotangent.transpose(0, 2, 1, 3)
    field, cot = (pltpu.with_memory_space_constraint(x, pltpu.HBM) for x in (field, cot))
    token = shape((8, 128), F32)
    near_a, near_b = shape((2, OTHERS + 1, ROWS, CHAN)), shape((2, OTHERS, ROWS, CHAN))
    second = shape((2, SECOND, ROWS, CHAN))
    polar = shape((2, 65, ROWS, CHAN))
    scratch = [
        pltpu.VMEM((2, COLS, ROWS, CHAN), BF16),
        pltpu.SemaphoreType.DMA((12,)),
    ]
    messages = call(
        pack_kernel,
        [near_a, second, polar, near_b, polar],
        scratch,
        0,
        (),
        (field, cot),
        space=pltpu.HBM,
    )
    targets = ((1, range(2, 8)), (1, (1,)), (1, (0,)), (0, range(2, 8)), (0, (0, 1)))
    got = [None] * 5
    for index in (2, 1, 0, 4, 3):
        got[index] = lax.ppermute(messages[index], LL, pairs_of_lon(*targets[index]))

    gathered = shape((ROWS, 128, CHAN))
    tables = [shape((20 * 288, 256)), shape((20 * 288, 256)), shape((5 * 288, 256))]
    own_f, own_c, *shapes = call(
        pre_kernel,
        [gathered, gathered, *tables],
        [pltpu.VMEM((2, COLS, ROWS, CHAN), BF16), pltpu.SemaphoreType.DMA((6,))],
        2 * 10**8,
        (row_spans,),
        (field, cot),
        space=pltpu.HBM,
    )
    row_flops = 2 * 288 * 640 * CHAN
    scalars = (amps,)
    (center,) = call(center_kernel, [shape((12 * 288, CHAN), F32)], [], 10**8, scalars, (own_f, shapes[0]))
    own2 = shape((5, 32, CHAN))
    own0_f, own0_c, own1_f, own1_c, own2_f, own2_c, lat_a, lat_b = call(
        assemble_kernel,
        [gathered] * 4 + [own2] * 2 + [shape((2, 2, 160, CHAN)), shape((2, 2, 176, CHAN))],
        [],
        0,
        (),
        (own_f, own_c, *got, center),
    )
    halo_a = lax.ppermute(lat_a, "lat", pairs_of_lat(0))
    halo_b = lax.ppermute(lat_b, "lat", pairs_of_lat(1))

    filters = (own0_f, own1_f, own2_f, *shapes, own0_c)
    outs = [shape((12 * PAD, 384)), shape((128, 384), F32)]
    inner, part = call(inner_kernel, outs, [], 12 * row_flops, scalars, (center, *filters))
    half = shape((192, CHAN), F32)
    outer, mine, other = call(
        outer_kernel,
        [shape((4 * PAD, 384)), half, half],
        [pltpu.VMEM((384, CHAN), F32)],
        4 * row_flops,
        scalars,
        (*filters, halo_a, halo_b, part),
    )

    def add(*parts, after=(), more=True, dtype=BF16):
        total = shape((192, CHAN), dtype)
        outs = [total, token] if more else [total]
        return call(functools.partial(sum_kernel, len(parts)), outs, [], 0, (), (*parts, *after))

    def back(piece, before, *done):
        return call(
            functools.partial(back_kernel, piece),
            [shape((1, COLS, ROWS, CHAN), F32), token],
            [pltpu.VMEM((12 * 288, CHAN), F32), pltpu.VMEM((8 * PAD, 384), BF16)],
            2 * row_flops,
            scalars,
            (own0_c, own1_c, own2_c, *shapes, halo_a, halo_b, mix_weight, before, *done),
        )

    mine, before = add(mine, flip(other, "lat", 1))
    steps = [flip(mine, "dp", bit) for bit in (1, 2, 3)]
    convolved, done = call(
        mix_kernel,
        [shape((1, COLS, ROWS, CHAN)), token],
        [],
        2 * ROWS * PAD * 384 * CHAN,
        (),
        (inner, outer, mix_weight.reshape(384, CHAN), before),
    )
    mine, before = add(mine, *steps, after=(done,))
    steps = [flip(mine, "lon", bit) for bit in (1, 2, 3)]
    grad, done = back(0, before)
    mine, before = add(mine, *steps, after=(done,))
    steps = [flip(mine, "lat", bit) for bit in (2, 4, 6)]
    grad, done = back(1, before, grad)
    (mine,) = add(mine, *steps, after=(done,), more=False)
    (mine,) = add(mine, lax.ppermute(mine, LL, z_pairs()), more=False, dtype=F32)
    other = flip(mine, "lat", 1)
    first_half = lax.axis_index("lat") % 2 == 0
    whole = jnp.concatenate([jnp.where(first_half, mine, other), jnp.where(first_half, other, mine)])
    whole = whole * (1.0 / math.sqrt(4 * 128 * 720))
    return convolved.transpose(0, 2, 1, 3), grad.transpose(0, 2, 1, 3), whole.reshape(3, 128, 128)


def solution(mesh):
    cells = P("dp", "lat", "lon", None)
    return jax.shard_map(
        body,
        mesh=mesh,
        in_specs=(cells, cells, P(), P(), P()),
        out_specs=(cells, cells, P()),
        check_vma=False,
    )
```

```python
import functools
import math

import jax
import jax.numpy as jnp
from jax import lax
from jax.experimental import pallas as pl
from jax.experimental.pallas import tpu as pltpu
from jax.sharding import PartitionSpec as P

ROWS = 16
COLS = 90
CHAN = 128
PAD = 96
F32 = jnp.float32
BF16 = jnp.bfloat16
LL = ("lat", "lon")
POLAR_FAR = 40
SECOND = 18
OTHERS = 9


def offsets_of(group):
    col = lax.broadcasted_iota(jnp.int32, (PAD, 128), 0)
    lane = lax.broadcasted_iota(jnp.int32, (PAD, 128), 1)
    none = jnp.full((PAD, 128), 1000000, jnp.int32)
    if group == 0:
        source = jnp.where(lane < PAD, lane, jnp.where(lane < PAD + 16, lane - 112, lane - 22))
        source = jnp.where((lane >= COLS) & (lane < PAD), none, source)
    elif group == 1:
        source = jnp.where(lane < 64, lane - 80, lane + 42)
    else:
        source = jnp.where(lane < 16, lane - 90, lane + 148)
        source = jnp.where((lane >= 10) & (lane < 22), none, source)
        source = jnp.where(lane >= 32, none, source)
    return (source - col).astype(F32)


def fill_shapes(table, offsets, spans, first, low, high):
    def fill(row, carry):
        span = spans[row_of(first, row)].astype(F32)
        divisor = jnp.full((1, 128), span + 1.0, F32)
        norm = lax.rsqrt(divisor)
        inside = jnp.abs(offsets) <= span
        scaled = jnp.where(inside, offsets * (1.0 / divisor), 0.0)
        square = scaled * scaled
        half = jnp.full(square.shape, 4.7108746e-07, F32)
        for term in (-2.5202042e-05, 9.1926025e-04, -2.0863481e-02, 2.5366950e-01, -1.2337005, 1.0):
            half = half * square + term
        cosine = 2.0 * half * half - 1.0
        shapes = (1.0 - jnp.abs(scaled), scaled, cosine)
        for k in range(3):
            at = pl.multiple_of(row * 288 + k * PAD, PAD)
            value = jnp.where(inside, shapes[k] * norm, 0.0)
            high = value.astype(BF16)
            table[pl.ds(at, PAD), :128] = high
            table[pl.ds(at, PAD), 128:] = (value - high.astype(F32)).astype(BF16)
        return carry

    def four(index, carry):
        for part in range(4):
            fill(low + index * 4 + part, carry)
        return carry

    lax.fori_loop(0, (high - low) // 4, four, 0)
    lax.fori_loop(low + (high - low) // 4 * 4, high, fill, 0)


def position():
    lat = lax.axis_index("lat")
    return lat, lat * ROWS


def row_of(first, ext):
    if isinstance(ext, int) and 2 <= ext < 18:
        return first + ext - 2
    return jnp.clip(first + ext - 2, 0, 127)


def factor_of(amps, first, ext, k, tap):
    return amps[tap, k, row_of(first, ext)]


def pack_kernel(field, cot, near_a, second_a, polar_a, near_b, polar_b, whole, sems):
    lat, odd = lax.axis_index("lat"), lax.axis_index("lon") % 2 == 1

    def edges(is_odd):
        def part(out, width, right, sem):
            source, target = pl.ds(COLS - width if right else 0, width), pl.ds(0, width)
            return [
                pltpu.make_async_copy(x.at[0, source], out.at[i, target], sems.at[sem + i]) for i, x in enumerate((field, cot))
            ]

        def run(copies):
            for copy in copies:
                copy.start()
            for copy in copies:
                copy.wait()

        pl.when(lat >= 2)(lambda: run(part(near_a, OTHERS, is_odd, 0) + part(near_b, OTHERS, not is_odd, 2)))
        pl.when(lat == 1)(lambda: run(part(second_a, SECOND, is_odd, 0) + part(polar_b, SECOND, not is_odd, 2)))

        @pl.when(lat == 0)
        def _():
            loads = []
            for which, source in enumerate((field, cot)):
                for part in range(3):
                    at = pl.ds(part * 30, 30)
                    sem = sems.at[6 + which * 3 + part]
                    loads.append(pltpu.make_async_copy(source.at[0, at], whole.at[which, at], sem))
            for load in loads:
                load.start()
            for load in loads:
                load.wait()
            for which in range(2):
                low = jnp.concatenate([whole[which, :45, :8], whole[which, 45:, :8]], axis=1)
                left = jnp.concatenate([whole[which, :20, 8:], whole[which, 20:40, 8:]], axis=1)
                right = jnp.concatenate([whole[which, 50:70, 8:], whole[which, 70:, 8:]], axis=1)
                polar_a[which, :45] = low
                polar_b[which, :45] = low
                polar_a[which, 45:] = right if is_odd else left
                polar_b[which, 45:] = left if is_odd else right

    pl.when(odd)(lambda: edges(True))
    pl.when(jnp.logical_not(odd))(lambda: edges(False))


def prepare_kernel(field, cot, spans, amps, *refs):
    own_f, own_c, shape0, shape1, shape2, center, amps_out, whole, spans_in, amps_in, sems = refs
    lat, first = position()
    fetch = pltpu.make_async_copy(spans, spans_in, sems.at[6])
    fetch_amps = pltpu.make_async_copy(amps, amps_in, sems.at[7])
    hand_on = pltpu.make_async_copy(amps, amps_out, sems.at[8])
    loads = []
    for which, source in enumerate((field, cot)):
        for part in range(3):
            at = pl.ds(part * 30, 30)
            loads.append(pltpu.make_async_copy(source.at[0, at], whole.at[which, at], sems.at[which * 3 + part]))
    for load in (fetch, fetch_amps, hand_on, *loads):
        load.start()
    fetch.wait()
    fill_shapes(shape0, offsets_of(0), spans_in, first, 0, 20)

    @pl.when(lat < 2)
    def _():
        low = jnp.where(lat == 0, 2, 0)
        fill_shapes(shape1, offsets_of(1), spans_in, first, low, jnp.where(lat == 0, 18, 2))

    @pl.when(lat == 0)
    def _():
        fill_shapes(shape2, offsets_of(2), spans_in, first, 2, 5)

    for load in (fetch_amps, hand_on, *loads):
        load.wait()
    for which, own in enumerate((own_f, own_c)):
        own[:, COLS:, :] = jnp.zeros((ROWS, 128 - COLS, CHAN), BF16)
        own[:, :COLS, :] = jnp.swapaxes(whole[which], 0, 1)
    for row in range(ROWS):
        rows = [own_f[row - 2 + tap, :PAD] if 0 <= row - 2 + tap < ROWS else None for tap in range(5)]
        values = filtered(shape0, (row + 2) * 288, amps_in, first, row + 2, rows)
        for k in range(3):
            at = row * 288 + k * PAD
            center[at : at + PAD, :] = values[k]


def assemble_kernel(old_f, old_c, near_a, second_a, polar_a, near_b, polar_b, tie, *outs):
    lat = lax.axis_index("lat")
    odd = lax.axis_index("lon") % 2 == 1
    groups = ((outs[0], outs[2], outs[4]), (outs[1], outs[3], outs[5]))
    lat_a, lat_b = outs[6], outs[7]

    def left_right(a_ref, b_ref, which, lo, hi):
        left = jnp.where(odd, b_ref[which, lo:hi], a_ref[which, lo:hi])
        right = jnp.where(odd, a_ref[which, lo:hi], b_ref[which, lo:hi])
        return jnp.swapaxes(left, 0, 1), jnp.swapaxes(right, 0, 1)

    for which in range(2):
        own0, own1, own2 = groups[which]
        own0[...] = (old_f, old_c)[which][...]

        @pl.when(lat >= 2)
        def _(which=which, own0=own0):
            left = jnp.where(odd, near_b[which], near_a[which])
            right = jnp.where(odd, near_a[which], near_b[which])
            own0[:, 112 - OTHERS : 112, :] = jnp.swapaxes(left, 0, 1)
            own0[:, 112 : 112 + OTHERS, :] = jnp.swapaxes(right, 0, 1)

        @pl.when(lat == 1)
        def _(which=which, own0=own0, own1=own1):
            left, right = left_right(second_a, polar_b, which, 0, SECOND)
            own0[:, 96:112, :] = left[:, 2:]
            own0[:, 112:128, :] = right[:, :16]
            own1[...] = jnp.zeros(own1.shape, BF16)
            own1[:, 62:64, :] = left[:, :2]
            own1[:, 64:66, :] = right[:, 16:]

        @pl.when(lat == 0)
        def _(which=which, own0=own0, own1=own1, own2=own2):
            a, b = polar_a[which], polar_b[which]
            left, right = jnp.where(odd, b, a), jnp.where(odd, a, b)

            def opened(lo, hi):
                return [jnp.swapaxes(jnp.concatenate([x[lo:hi, :8], x[lo:hi, 8:]], axis=0), 0, 1) for x in (left, right)]

            high_left, high_right = opened(45, 65)
            left, right = opened(0, 45)
            own0[:8, 96:112, :] = left[:, 74:90]
            own0[:8, 112:128, :] = right[:, 0:16]
            own1[:8, :64, :] = left[:, 10:74]
            own1[:8, 64:, :] = right[:, 16:80]
            own2[:, :16, :] = left[:5, 0:16]
            own2[:, 16:, :] = right[:5, 74:90]
            left, right = high_left, high_right
            own0[8:, 96:112, :] = left[:, 24:40]
            own0[8:, 112:128, :] = right[:, 0:16]
            own1[8:] = jnp.zeros((8, 128, CHAN), BF16)
            own1[8:, 40:64, :] = left[:, 0:24]
            own1[8:, 64:88, :] = right[:, 16:40]

        even = lat % 2 == 0
        for row in range(2):
            lat_a[which, row] = jnp.where(even, own0[14 + row], own0[row])
            lat_b[which, row, :128, :] = jnp.where(even, own0[row], own0[14 + row])

        @pl.when(lat < 2)
        def _(which=which, own1=own1):
            for row in range(2):
                lat_a[which, row, COLS : COLS + 4, :] = jnp.where(even, own1[14 + row, 62:66, :], own1[row, 62:66, :])


def tapped(amps, first, ext, rows):
    taps = [tap for tap in range(5) if rows[tap] is not None]
    factors = [{tap: factor_of(amps, first, ext, k, tap) for tap in taps} for k in range(3)]
    height = rows[taps[0]].shape[0]
    parts = [[] for _ in range(3)]
    for at in range(0, height, 32):
        wide = {tap: rows[tap][at : at + 32].astype(F32) for tap in taps}
        for k in range(3):
            total = wide[taps[0]] * factors[k][taps[0]]
            for tap in taps[1:]:
                total += wide[tap] * factors[k][tap]
            parts[k].append(total.astype(BF16))
    return [jnp.concatenate(part, axis=0) if len(part) > 1 else part[0] for part in parts]


def filtered(table, at, amps, first, ext, rows, lane=0):
    out = []
    for k, taps in enumerate(tapped(amps, first, ext, rows)):
        shapes = rows_at(table, at + k * PAD, PAD)
        if taps.shape[0] < 128:
            end = lane + taps.shape[0]
            shapes = jnp.concatenate([shapes[:, lane:end], shapes[:, 128 + lane : 128 + end]], axis=1)
        out.append(jnp.dot(shapes, jnp.concatenate([taps, taps], axis=0), preferred_element_type=F32))
    return out


def plus(values, more):
    return [x + y for x, y in zip(values, more)]


def rows_at(ref, start, count=288):
    return ref[pl.ds(start if isinstance(start, int) else pl.multiple_of(start, 32), count), :]


def store_basis(basis, row, values):
    at = row * PAD if isinstance(row, int) else pl.multiple_of(row * PAD, PAD)
    for k in range(3):
        basis[pl.ds(at, PAD), k * 128 : (k + 1) * 128] = values[k].astype(BF16)


def times_cotangent(cot, basis):
    return lax.dot_general(cot, basis, (((0,), (0,)), ((), ())), preferred_element_type=F32)


def inner_kernel(amps, center, own0, own1, own2, shape0, shape1, shape2, cot, basis, part, ends):
    lat, first = position()

    def one(row, wide):
        def own(ref, low, high):
            return [ref[row - 2 + tap, low:] if 0 <= row - 2 + tap < high else None for tap in range(5)]

        at = (row + 2) * 288
        values = filtered(shape0, at, amps, first, row + 2, own(own0, PAD, ROWS), PAD)
        values = plus(values, [center[row * 288 + k * PAD : row * 288 + (k + 1) * PAD, :] for k in range(3)])
        if wide:
            values = plus(values, filtered(shape1, at, amps, first, row + 2, own(own1, 0, ROWS)))
        if wide and row < 3:
            values = plus(values, filtered(shape2, at, amps, first, row + 2, own(own2, 0, 5)))
        if 2 <= row < 14:
            store_basis(basis, row - 2, values)
        else:
            place = row if row < 2 else row - 12
            for k in range(3):
                ends[place * 288 + k * PAD : place * 288 + (k + 1) * PAD, :] = values[k]

    def run(wide):
        for row in range(ROWS):
            one(row, wide)

    pl.when(lat != 0)(lambda: run(False))
    pl.when(lat == 0)(lambda: run(True))
    part[...] = times_cotangent(cot[2:14, :PAD, :].reshape(12 * PAD, CHAN), basis[...])


def halo_row(halo_a, halo_b, which, row, even, top):
    a, b = halo_a[which, row], halo_b[which, row, :128]
    return jnp.where(even, b, a) if top else jnp.where(even, a, b)


def far_halo_row(halo_a, which, row):
    zeros = jnp.zeros((62, CHAN), BF16)
    return jnp.concatenate([zeros, halo_a[which, row, COLS : COLS + 4], zeros], axis=0)


def outer_kernel(amps, ends, shape0, shape1, cot, halo_a, halo_b, part, basis, mine, other, grad):
    lat, first = position()
    even = lat % 2 == 0

    def run(wide):
        for place, row in enumerate((0, 1, 14, 15)):
            near, far = [], []
            for at in range(row - 2, row + 3):
                inside, index = 0 <= at < ROWS, at + 2 if at < 0 else at - ROWS
                near.append(None if inside else halo_row(halo_a, halo_b, 0, index, even, at < 0))
                far.append(None if inside or at < 0 else far_halo_row(halo_a, 0, index))
            at = (row + 2) * 288
            values = filtered(shape0, at, amps, first, row + 2, near)
            values = plus(values, [ends[place * 288 + k * PAD : place * 288 + (k + 1) * PAD, :] for k in range(3)])
            if wide and row > 2:
                values = plus(values, filtered(shape1, at, amps, first, row + 2, far))
            store_basis(basis, place, values)

    pl.when(lat != 0)(lambda: run(False))
    pl.when(lat == 0)(lambda: run(True))
    cells = jnp.concatenate([cot[0:2, :PAD, :], cot[14:16, :PAD, :]], axis=0).reshape(4 * PAD, CHAN)
    product = part[...] + times_cotangent(cells, basis[...])
    for k in range(3):
        grad[k * 128 : (k + 1) * 128, :] = product[:, k * 128 : (k + 1) * 128].T
    core = lat % 2
    mine[...] = grad[pl.ds(pl.multiple_of(core * 192, 192), 192), :]
    other[...] = grad[pl.ds(pl.multiple_of((1 - core) * 192, 192), 192), :]


def mix_kernel(inner, outer, weight, before, out, token):
    w = weight[...]

    def mixed(basis, rows):
        return jnp.dot(basis, w, preferred_element_type=F32).astype(BF16).reshape(rows, PAD, CHAN)[:, :COLS]

    ends = mixed(outer[...], 4)
    whole = jnp.concatenate([ends[:2], mixed(inner[...], 12), ends[2:]], axis=0)
    out[0] = jnp.swapaxes(whole, 0, 1)
    token[...] = before[...]


def back_kernel(piece, amps, own0, own1, own2, shape0, shape1, shape2, halo_a, halo_b, weight, before, *refs):
    out, token, spread, joined = refs[-4:]
    lat, first = position()
    even = lat % 2 == 0
    begin = 8 * piece

    def put(index, value, fresh):
        at = index * 288 if isinstance(index, int) else pl.multiple_of(index * 288, 32)
        if fresh:
            spread[pl.ds(at, 288), :] = value
        else:
            spread[pl.ds(at, 288), :] += value

    def twice(shapes, rows):
        return jnp.dot(shapes, jnp.concatenate([rows, rows], axis=0), preferred_element_type=F32)

    def own_rows(low, high, wide):
        for ext in range(low, high):
            value = twice(rows_at(shape0, ext * 288), own0[ext - 2])
            if wide:
                value += twice(rows_at(shape1, ext * 288), own1[ext - 2])
            put(ext - begin, value, True)

    low, high = max(begin, 2), min(begin + 12, 18)
    pl.when(lat != 0)(lambda: own_rows(low, high, False))
    pl.when(lat == 0)(lambda: own_rows(low, high, True))
    for row in range(2):
        ext = row if piece == 0 else 18 + row
        gathered = halo_row(halo_a, halo_b, 1, row, even, piece == 0)
        put(ext - begin, twice(shape0[ext * 288 : (ext + 1) * 288, :], gathered), True)
    if piece == 0:

        @pl.when(lat == 1)
        def _():
            for row in range(2):
                far = far_halo_row(halo_a, 1, row)
                put(row, twice(shape1[row * 288 : (row + 1) * 288, :], far), False)

        @pl.when(lat == 0)
        def _():
            for ext in range(2, 5):
                at = slice(ext * 288, (ext + 1) * 288)
                shapes = jnp.concatenate([shape2[at, :32], shape2[at, 128:160]], axis=1)
                put(ext, twice(shapes, own2[ext - 2]), False)

    if piece:
        out[...] = refs[0][...]
    for row in range(8):
        for k in range(3):
            total = None
            for slot in range(5):
                factor = factor_of(amps, first, begin + row + slot, k, 4 - slot) * (-1.0 if k == 1 else 1.0)
                at = (row + slot) * 288 + k * PAD
                term = spread[at : at + PAD, :] * factor
                total = term if total is None else total + term
            joined[row * PAD : (row + 1) * PAD, k * 128 : (k + 1) * 128] = total.astype(BF16)
    weights = jnp.concatenate([weight[k] for k in range(3)], axis=1)
    mixed = lax.dot_general(joined[...], weights, (((1,), (1,)), ((), ())), preferred_element_type=F32)
    out[0, :, begin : begin + 8, :] = jnp.swapaxes(mixed.reshape(8, PAD, CHAN)[:, :COLS], 0, 1)
    token[...] = before[...]


def sum_kernel(count, *refs):
    parts = [ref[...].astype(F32) for ref in refs[:count]]
    while len(parts) > 1:
        parts = [parts[i] + parts[i + 1] for i in range(0, len(parts), 2)]
    out, *token = refs[-2:] if refs[-1].shape[0] == 8 else refs[-1:]
    out[...] = parts[0].astype(out.dtype)
    if token:
        token[0][...] = jnp.zeros((8, 128), F32)


def pairs_of_lon(parity, lats):
    out = []
    for lat in lats:
        for lon in range(8):
            other = lon ^ 1 if parity == 0 else ((lon + 1) % 8 if lon % 2 else (lon - 1) % 8)
            out.append((lat * 8 + lon, lat * 8 + other))
    return out


def pairs_of_lat(parity):
    out = []
    for lat in range(8):
        other = lat ^ 1 if parity == 0 else (lat + 1 if lat % 2 else lat - 1)
        if 0 <= other < 8:
            out.append((lat, other))
    return out


def z_pairs():
    across = {0: 6, 6: 0, 1: 7, 7: 1, 2: 4, 4: 2, 3: 5, 5: 3}
    out = []
    for lat in range(8):
        for lon in range(8):
            other = across[(lon >> 2) * 4 + (lat >> 1)]
            out.append((lat * 8 + lon, ((other % 4) * 2 + lat % 2) * 8 + (other // 4) * 4 + lon % 4))
    return out


def flip(x, axis, bit):
    return lax.ppermute(x, axis, [(i, i ^ bit) for i in range(lax.axis_size(axis))])


VMEM = pl.BlockSpec(memory_space=pltpu.VMEM)
SMEM = pl.BlockSpec(memory_space=pltpu.SMEM)


def call(kernel, outs, scratch, flops, scalars, arrays, limit=12, space=pltpu.VMEM):
    moved = sum(math.prod(x.shape) * x.dtype.itemsize for x in (*arrays, *outs))
    return pl.pallas_call(
        kernel,
        out_shape=outs,
        in_specs=[SMEM] * len(scalars) + [pl.BlockSpec(memory_space=space)] * len(arrays),
        out_specs=[VMEM] * len(outs),
        scratch_shapes=scratch,
        compiler_params=pltpu.CompilerParams(vmem_limit_bytes=limit * 1024 * 1024),
        cost_estimate=pl.CostEstimate(flops=flops, bytes_accessed=moved, transcendentals=0),
    )(*scalars, *arrays)


def shape(dims, dtype=BF16):
    return jax.ShapeDtypeStruct(dims, dtype)


def body(features, cotangent, mix_weight, amplitude, row_spans):
    amps = amplitude.transpose(2, 0, 1)

    field, cot = features.transpose(0, 2, 1, 3), cotangent.transpose(0, 2, 1, 3)
    field, cot, spans, amps = (pltpu.with_memory_space_constraint(x, pltpu.HBM) for x in (field, cot, row_spans, amps))
    token = shape((8, 128), F32)
    near_a, near_b = shape((2, OTHERS, ROWS, CHAN)), shape((2, OTHERS, ROWS, CHAN))
    second = shape((2, SECOND, ROWS, CHAN))
    polar = shape((2, 65, ROWS, CHAN))
    scratch = [
        pltpu.VMEM((2, COLS, ROWS, CHAN), BF16),
        pltpu.SemaphoreType.DMA((12,)),
    ]
    messages = call(
        pack_kernel,
        [near_a, second, polar, near_b, polar],
        scratch,
        0,
        (),
        (field, cot),
        space=pltpu.HBM,
    )
    targets = ((1, range(2, 8)), (1, (1,)), (1, (0,)), (0, range(2, 8)), (0, (0, 1)))
    got = [None] * 5
    for index in (2, 1, 0, 4, 3):
        got[index] = lax.ppermute(messages[index], LL, pairs_of_lon(*targets[index]))

    gathered = shape((ROWS, 128, CHAN))
    tables = [shape((20 * 288, 256)), shape((20 * 288, 256)), shape((5 * 288, 256))]
    row_flops = 2 * 288 * 640 * CHAN
    scratch = [
        pltpu.VMEM((2, COLS, ROWS, CHAN), BF16),
        pltpu.SMEM((128,), jnp.int32),
        pltpu.SMEM((5, 3, 128), F32),
        pltpu.SemaphoreType.DMA((9,)),
    ]
    outs = [gathered, gathered, *tables, shape((ROWS * 288, CHAN), F32), shape((5, 3, 128), F32)]
    own_f, own_c, *shapes, center, amps = call(prepare_kernel, outs, scratch, 2 * 10**8, (), (field, cot, spans, amps), space=pltpu.HBM)
    scalars = (amps,)
    own2 = shape((5, 32, CHAN))
    own0_f, own0_c, own1_f, own1_c, own2_f, own2_c, lat_a, lat_b = call(
        assemble_kernel,
        [gathered] * 4 + [own2] * 2 + [shape((2, 2, 128, CHAN)), shape((2, 2, 144, CHAN))],
        [],
        0,
        (),
        (own_f, own_c, *got, center),
    )
    halo_a = lax.ppermute(lat_a, "lat", pairs_of_lat(0))
    halo_b = lax.ppermute(lat_b, "lat", pairs_of_lat(1))

    own = (own0_f, own1_f, own2_f, *shapes, own0_c)
    half, ends = shape((192, CHAN), F32), shape((4 * 288, CHAN), F32)
    outs = [shape((12 * PAD, 384)), shape((128, 384), F32), ends]
    inner, part, ends = call(inner_kernel, outs, [], 12 * row_flops, scalars, (center, *own))
    outer, mine, other = call(
        outer_kernel,
        [shape((4 * PAD, 384)), half, half],
        [pltpu.VMEM((384, CHAN), F32)],
        4 * row_flops,
        scalars,
        (ends, shapes[0], shapes[1], own0_c, halo_a, halo_b, part),
    )

    def add(*parts, after=(), more=True, dtype=BF16):
        total = shape((192, CHAN), dtype)
        outs = [total, token] if more else [total]
        return call(functools.partial(sum_kernel, len(parts)), outs, [], 0, (), (*parts, *after))

    def back(piece, before, *done):
        return call(
            functools.partial(back_kernel, piece),
            [shape((1, COLS, ROWS, CHAN), F32), token],
            [pltpu.VMEM((12 * 288, CHAN), F32), pltpu.VMEM((8 * PAD, 384), BF16)],
            2 * row_flops,
            scalars,
            (own0_c, own1_c, own2_c, *shapes, halo_a, halo_b, mix_weight, before, *done),
        )

    mine, before = add(mine, flip(other, "lat", 1))
    steps = [flip(mine, "dp", bit) for bit in (1, 2, 3)]
    convolved, done = call(
        mix_kernel,
        [shape((1, COLS, ROWS, CHAN)), token],
        [],
        2 * ROWS * PAD * 384 * CHAN,
        (),
        (inner, outer, mix_weight.reshape(384, CHAN), before),
    )
    (mine,) = add(mine, *steps, after=(done,), more=False)
    steps = [flip(mine, "lon", bit) for bit in (1, 2, 3)]
    mine, before = add(mine, *steps)
    steps = [flip(mine, "lat", bit) for bit in (2, 4, 6)]
    grad, done = back(0, before)
    mine, before = add(mine, *steps, after=(done,))
    step = lax.ppermute(mine, LL, z_pairs())
    grad, done = back(1, before, grad)
    (mine,) = add(mine, step, after=(done,), more=False, dtype=F32)
    other = flip(mine, "lat", 1)
    first_half = lax.axis_index("lat") % 2 == 0
    whole = jnp.concatenate([jnp.where(first_half, mine, other), jnp.where(first_half, other, mine)])
    whole = whole * (1.0 / math.sqrt(4 * 128 * 720))
    return convolved.transpose(0, 2, 1, 3), grad.transpose(0, 2, 1, 3), whole.reshape(3, 128, 128)


def solution(mesh):
    cells = P("dp", "lat", "lon", None)
    return jax.shard_map(
        body,
        mesh=mesh,
        in_specs=(cells, cells, P(), P(), P()),
        out_specs=(cells, cells, P()),
        check_vma=False,
    )
```

```python
import functools
import math

import jax
import jax.numpy as jnp
from jax import lax
from jax.experimental import pallas as pl
from jax.experimental.pallas import tpu as pltpu
from jax.sharding import PartitionSpec as P

ROWS = 16
COLS = 90
CHAN = 128
PAD = 96
F32 = jnp.float32
BF16 = jnp.bfloat16
LL = ("lat", "lon")
POLAR_FAR = 40
SECOND = 18
FEW = 5


def offsets_of(group):
    col = lax.broadcasted_iota(jnp.int32, (PAD, 128), 0)
    lane = lax.broadcasted_iota(jnp.int32, (PAD, 128), 1)
    none = jnp.full((PAD, 128), 1000000, jnp.int32)
    if group == 0:
        source = jnp.where(lane < PAD, lane, jnp.where(lane < PAD + 16, lane - 112, lane - 22))
        source = jnp.where((lane >= COLS) & (lane < PAD), none, source)
    elif group == 1:
        source = jnp.where(lane < 64, lane - 80, lane + 42)
    else:
        source = jnp.where(lane < 16, lane - 90, lane + 148)
        source = jnp.where((lane >= 10) & (lane < 22), none, source)
        source = jnp.where(lane >= 32, none, source)
    return (source - col).astype(F32)


def fill_shapes(table, offsets, spans, first, low, high):
    def fill(row, carry):
        span = spans[row_of(first, row)].astype(F32)
        divisor = jnp.full((1, 128), span + 1.0, F32)
        norm = lax.rsqrt(divisor)
        inside = jnp.abs(offsets) <= span
        scaled = jnp.where(inside, offsets * (1.0 / divisor), 0.0)
        square = scaled * scaled
        half = jnp.full(square.shape, 4.7108746e-07, F32)
        for term in (-2.5202042e-05, 9.1926025e-04, -2.0863481e-02, 2.5366950e-01, -1.2337005, 1.0):
            half = half * square + term
        cosine = 2.0 * half * half - 1.0
        shapes = (1.0 - jnp.abs(scaled), scaled, cosine)
        for k in range(3):
            at = pl.multiple_of(row * 288 + k * PAD, PAD)
            value = jnp.where(inside, shapes[k] * norm, 0.0)
            high = value.astype(BF16)
            table[pl.ds(at, PAD), :128] = high
            table[pl.ds(at, PAD), 128:] = (value - high.astype(F32)).astype(BF16)
        return carry

    def four(index, carry):
        for part in range(4):
            fill(low + index * 4 + part, carry)
        return carry

    lax.fori_loop(0, (high - low) // 4, four, 0)
    lax.fori_loop(low + (high - low) // 4 * 4, high, fill, 0)


def position():
    lat = lax.axis_index("lat")
    return lat, lat * ROWS


def row_of(first, ext):
    if isinstance(ext, int) and 2 <= ext < 18:
        return first + ext - 2
    return jnp.clip(first + ext - 2, 0, 127)


def factor_of(amps, first, ext, k, tap):
    return amps[tap, k, row_of(first, ext)]


def pack_kernel(field, cot, few_a, second_a, polar_a, few_b, polar_b, whole, sems):
    lat, odd = lax.axis_index("lat"), lax.axis_index("lon") % 2 == 1

    def edges(is_odd):
        def part(out, width, right, sem, skip=0):
            source, target = pl.ds(COLS - width - skip if right else skip, width), pl.ds(0, width)
            return [
                pltpu.make_async_copy(x.at[0, source], out.at[i, target], sems.at[sem + i]) for i, x in enumerate((field, cot))
            ]

        def run(copies):
            for copy in copies:
                copy.start()
            for copy in copies:
                copy.wait()

        pl.when(lat >= 4)(lambda: run(part(few_a, FEW, is_odd, 0) + part(few_b, FEW, not is_odd, 2)))
        pl.when(lat == 1)(lambda: run(part(second_a, SECOND, is_odd, 0) + part(polar_b, SECOND, not is_odd, 2)))

        @pl.when((lat == 2) | (lat == 3))
        def _():
            nearest = part(few_a, FEW, not is_odd, 2)
            run(part(second_a, SECOND, is_odd, 0) + nearest + part(few_b, FEW, not is_odd, 4, skip=FEW))


        @pl.when(lat == 0)
        def _():
            loads = []
            for which, source in enumerate((field, cot)):
                for part in range(3):
                    at = pl.ds(part * 30, 30)
                    sem = sems.at[6 + which * 3 + part]
                    loads.append(pltpu.make_async_copy(source.at[0, at], whole.at[which, at], sem))
            for load in loads:
                load.start()
            for load in loads:
                load.wait()
            for which in range(2):
                low = jnp.concatenate([whole[which, :45, :8], whole[which, 45:, :8]], axis=1)
                left = jnp.concatenate([whole[which, :20, 8:], whole[which, 20:40, 8:]], axis=1)
                right = jnp.concatenate([whole[which, 50:70, 8:], whole[which, 70:, 8:]], axis=1)
                polar_a[which, :45] = low
                polar_b[which, :45] = low
                polar_a[which, 45:] = right if is_odd else left
                polar_b[which, 45:] = left if is_odd else right

    pl.when(odd)(lambda: edges(True))
    pl.when(jnp.logical_not(odd))(lambda: edges(False))


def prepare_kernel(field, cot, spans, amps, *refs):
    own_f, own_c, shape0, shape1, shape2, center, amps_out, whole, spans_in, amps_in, sems = refs
    lat, first = position()
    fetch = pltpu.make_async_copy(spans, spans_in, sems.at[6])
    fetch_amps = pltpu.make_async_copy(amps, amps_in, sems.at[7])
    hand_on = pltpu.make_async_copy(amps, amps_out, sems.at[8])
    loads = []
    for which, source in enumerate((field, cot)):
        for part in range(3):
            at = pl.ds(part * 30, 30)
            loads.append(pltpu.make_async_copy(source.at[0, at], whole.at[which, at], sems.at[which * 3 + part]))
    for load in (fetch, fetch_amps, hand_on, *loads):
        load.start()
    fetch.wait()
    fill_shapes(shape0, offsets_of(0), spans_in, first, 0, 20)

    @pl.when(lat < 2)
    def _():
        low = jnp.where(lat == 0, 2, 0)
        fill_shapes(shape1, offsets_of(1), spans_in, first, low, jnp.where(lat == 0, 18, 2))

    @pl.when(lat == 0)
    def _():
        fill_shapes(shape2, offsets_of(2), spans_in, first, 2, 5)

    for load in (fetch_amps, hand_on, *loads):
        load.wait()
    for which, own in enumerate((own_f, own_c)):
        own[:, COLS:, :] = jnp.zeros((ROWS, 128 - COLS, CHAN), BF16)
        own[:, :COLS, :] = jnp.swapaxes(whole[which], 0, 1)
    for row in range(ROWS):
        rows = [own_f[row - 2 + tap, :PAD] if 0 <= row - 2 + tap < ROWS else None for tap in range(5)]
        values = filtered(shape0, (row + 2) * 288, amps_in, first, row + 2, rows)
        for k in range(3):
            at = row * 288 + k * PAD
            center[at : at + PAD, :] = values[k]


def assemble_kernel(old_f, old_c, few_a, second_a, polar_a, few_b, polar_b, tie, *outs):
    lat = lax.axis_index("lat")
    odd = lax.axis_index("lon") % 2 == 1
    groups = ((outs[0], outs[2], outs[4]), (outs[1], outs[3], outs[5]))
    lat_a, lat_b = outs[6], outs[7]

    def left_right(a_ref, b_ref, which, lo, hi):
        left = jnp.where(odd, b_ref[which, lo:hi], a_ref[which, lo:hi])
        right = jnp.where(odd, a_ref[which, lo:hi], b_ref[which, lo:hi])
        return jnp.swapaxes(left, 0, 1), jnp.swapaxes(right, 0, 1)

    for which in range(2):
        own0, own1, own2 = groups[which]
        own0[...] = (old_f, old_c)[which][...]

        def put_near(left, right, own0=own0):
            width = left.shape[0]
            own0[:, 112 - width : 112, :] = jnp.swapaxes(left, 0, 1)
            own0[:, 112 : 112 + width, :] = jnp.swapaxes(right, 0, 1)

        @pl.when(lat >= 4)
        def _(which=which, put_near=put_near):
            a, b = few_a[which], few_b[which]
            put_near(jnp.where(odd, b, a), jnp.where(odd, a, b))

        @pl.when((lat == 2) | (lat == 3))
        def _(which=which, put_near=put_near):
            near, next_ones = few_a[which], few_b[which]
            left = jnp.where(odd, jnp.concatenate([next_ones, near]), second_a[which, SECOND - 2 * FEW :])
            right = jnp.where(odd, second_a[which, : 2 * FEW], jnp.concatenate([near, next_ones]))
            put_near(left, right)

        @pl.when(lat == 1)
        def _(which=which, own0=own0, own1=own1):
            left, right = left_right(second_a, polar_b, which, 0, SECOND)
            own0[:, 96:112, :] = left[:, 2:]
            own0[:, 112:128, :] = right[:, :16]
            own1[...] = jnp.zeros(own1.shape, BF16)
            own1[:, 62:64, :] = left[:, :2]
            own1[:, 64:66, :] = right[:, 16:]

        @pl.when(lat == 0)
        def _(which=which, own0=own0, own1=own1, own2=own2):
            a, b = polar_a[which], polar_b[which]
            left, right = jnp.where(odd, b, a), jnp.where(odd, a, b)

            def opened(lo, hi):
                return [jnp.swapaxes(jnp.concatenate([x[lo:hi, :8], x[lo:hi, 8:]], axis=0), 0, 1) for x in (left, right)]

            high_left, high_right = opened(45, 65)
            left, right = opened(0, 45)
            own0[:8, 96:112, :] = left[:, 74:90]
            own0[:8, 112:128, :] = right[:, 0:16]
            own1[:8, :64, :] = left[:, 10:74]
            own1[:8, 64:, :] = right[:, 16:80]
            own2[:, :16, :] = left[:5, 0:16]
            own2[:, 16:, :] = right[:5, 74:90]
            left, right = high_left, high_right
            own0[8:, 96:112, :] = left[:, 24:40]
            own0[8:, 112:128, :] = right[:, 0:16]
            own1[8:] = jnp.zeros((8, 128, CHAN), BF16)
            own1[8:, 40:64, :] = left[:, 0:24]
            own1[8:, 64:88, :] = right[:, 16:40]

        even = lat % 2 == 0
        for row in range(2):
            lat_a[which, row] = jnp.where(even, own0[14 + row], own0[row])
            lat_b[which, row, :128, :] = jnp.where(even, own0[row], own0[14 + row])

        @pl.when(lat < 2)
        def _(which=which, own1=own1):
            for row in range(2):
                lat_a[which, row, COLS : COLS + 4, :] = jnp.where(even, own1[14 + row, 62:66, :], own1[row, 62:66, :])


def tapped(amps, first, ext, rows):
    taps = [tap for tap in range(5) if rows[tap] is not None]
    factors = [{tap: factor_of(amps, first, ext, k, tap) for tap in taps} for k in range(3)]
    height = rows[taps[0]].shape[0]
    parts = [[] for _ in range(3)]
    for at in range(0, height, 32):
        wide = {tap: rows[tap][at : at + 32].astype(F32) for tap in taps}
        for k in range(3):
            total = wide[taps[0]] * factors[k][taps[0]]
            for tap in taps[1:]:
                total += wide[tap] * factors[k][tap]
            parts[k].append(total.astype(BF16))
    return [jnp.concatenate(part, axis=0) if len(part) > 1 else part[0] for part in parts]


def filtered(table, at, amps, first, ext, rows, lane=0):
    out = []
    for k, taps in enumerate(tapped(amps, first, ext, rows)):
        shapes = rows_at(table, at + k * PAD, PAD)
        if taps.shape[0] < 128:
            end = lane + taps.shape[0]
            shapes = jnp.concatenate([shapes[:, lane:end], shapes[:, 128 + lane : 128 + end]], axis=1)
        out.append(jnp.dot(shapes, jnp.concatenate([taps, taps], axis=0), preferred_element_type=F32))
    return out


def plus(values, more):
    return [x + y for x, y in zip(values, more)]


def rows_at(ref, start, count=288):
    return ref[pl.ds(start if isinstance(start, int) else pl.multiple_of(start, 32), count), :]


def store_basis(basis, row, values):
    at = row * PAD if isinstance(row, int) else pl.multiple_of(row * PAD, PAD)
    for k in range(3):
        basis[pl.ds(at, PAD), k * 128 : (k + 1) * 128] = values[k].astype(BF16)


def times_cotangent(cot, basis):
    return lax.dot_general(cot, basis, (((0,), (0,)), ((), ())), preferred_element_type=F32)


def inner_kernel(amps, center, own0, own1, own2, shape0, shape1, shape2, cot, basis, part, ends):
    lat, first = position()

    def one(row, wide):
        def own(ref, low, high):
            return [ref[row - 2 + tap, low:] if 0 <= row - 2 + tap < high else None for tap in range(5)]

        at = (row + 2) * 288
        values = filtered(shape0, at, amps, first, row + 2, own(own0, PAD, ROWS), PAD)
        values = plus(values, [center[row * 288 + k * PAD : row * 288 + (k + 1) * PAD, :] for k in range(3)])
        if wide:
            values = plus(values, filtered(shape1, at, amps, first, row + 2, own(own1, 0, ROWS)))
        if wide and row < 3:
            values = plus(values, filtered(shape2, at, amps, first, row + 2, own(own2, 0, 5)))
        if 2 <= row < 14:
            store_basis(basis, row - 2, values)
        else:
            place = row if row < 2 else row - 12
            for k in range(3):
                ends[place * 288 + k * PAD : place * 288 + (k + 1) * PAD, :] = values[k]

    def run(wide):
        for row in range(ROWS):
            one(row, wide)

    pl.when(lat != 0)(lambda: run(False))
    pl.when(lat == 0)(lambda: run(True))
    part[...] = times_cotangent(cot[2:14, :PAD, :].reshape(12 * PAD, CHAN), basis[...])


def halo_row(halo_a, halo_b, which, row, even, top):
    a, b = halo_a[which, row], halo_b[which, row, :128]
    return jnp.where(even, b, a) if top else jnp.where(even, a, b)


def far_halo_row(halo_a, which, row):
    zeros = jnp.zeros((62, CHAN), BF16)
    return jnp.concatenate([zeros, halo_a[which, row, COLS : COLS + 4], zeros], axis=0)


def outer_kernel(amps, ends, shape0, shape1, cot, halo_a, halo_b, part, basis, mine, other, grad):
    lat, first = position()
    even = lat % 2 == 0

    def run(wide):
        for place, row in enumerate((0, 1, 14, 15)):
            near, far = [], []
            for at in range(row - 2, row + 3):
                inside, index = 0 <= at < ROWS, at + 2 if at < 0 else at - ROWS
                near.append(None if inside else halo_row(halo_a, halo_b, 0, index, even, at < 0))
                far.append(None if inside or at < 0 else far_halo_row(halo_a, 0, index))
            at = (row + 2) * 288
            values = filtered(shape0, at, amps, first, row + 2, near)
            values = plus(values, [ends[place * 288 + k * PAD : place * 288 + (k + 1) * PAD, :] for k in range(3)])
            if wide and row > 2:
                values = plus(values, filtered(shape1, at, amps, first, row + 2, far))
            store_basis(basis, place, values)

    pl.when(lat != 0)(lambda: run(False))
    pl.when(lat == 0)(lambda: run(True))
    cells = jnp.concatenate([cot[0:2, :PAD, :], cot[14:16, :PAD, :]], axis=0).reshape(4 * PAD, CHAN)
    product = part[...] + times_cotangent(cells, basis[...])
    for k in range(3):
        grad[k * 128 : (k + 1) * 128, :] = product[:, k * 128 : (k + 1) * 128].T
    core = lat % 2
    mine[...] = grad[pl.ds(pl.multiple_of(core * 192, 192), 192), :]
    other[...] = grad[pl.ds(pl.multiple_of((1 - core) * 192, 192), 192), :]


def mix_kernel(inner, outer, weight, before, out, token):
    w = weight[...]

    def mixed(basis, rows):
        return jnp.dot(basis, w, preferred_element_type=F32).astype(BF16).reshape(rows, PAD, CHAN)[:, :COLS]

    ends = mixed(outer[...], 4)
    whole = jnp.concatenate([ends[:2], mixed(inner[...], 12), ends[2:]], axis=0)
    out[0] = jnp.swapaxes(whole, 0, 1)
    token[...] = before[...]


def back_kernel(piece, amps, own0, own1, own2, shape0, shape1, shape2, halo_a, halo_b, weight, before, *refs):
    out, token, spread, joined = refs[-4:]
    lat, first = position()
    even = lat % 2 == 0
    begin = 8 * piece

    def put(index, value, fresh):
        at = index * 288 if isinstance(index, int) else pl.multiple_of(index * 288, 32)
        if fresh:
            spread[pl.ds(at, 288), :] = value
        else:
            spread[pl.ds(at, 288), :] += value

    def twice(shapes, rows):
        return jnp.dot(shapes, jnp.concatenate([rows, rows], axis=0), preferred_element_type=F32)

    def own_rows(low, high, wide):
        for ext in range(low, high):
            value = twice(rows_at(shape0, ext * 288), own0[ext - 2])
            if wide:
                value += twice(rows_at(shape1, ext * 288), own1[ext - 2])
            put(ext - begin, value, True)

    low, high = max(begin, 2), min(begin + 12, 18)
    pl.when(lat != 0)(lambda: own_rows(low, high, False))
    pl.when(lat == 0)(lambda: own_rows(low, high, True))
    for row in range(2):
        ext = row if piece == 0 else 18 + row
        gathered = halo_row(halo_a, halo_b, 1, row, even, piece == 0)
        put(ext - begin, twice(shape0[ext * 288 : (ext + 1) * 288, :], gathered), True)
    if piece == 0:

        @pl.when(lat == 1)
        def _():
            for row in range(2):
                far = far_halo_row(halo_a, 1, row)
                put(row, twice(shape1[row * 288 : (row + 1) * 288, :], far), False)

        @pl.when(lat == 0)
        def _():
            for ext in range(2, 5):
                at = slice(ext * 288, (ext + 1) * 288)
                shapes = jnp.concatenate([shape2[at, :32], shape2[at, 128:160]], axis=1)
                put(ext, twice(shapes, own2[ext - 2]), False)

    if piece:
        out[...] = refs[0][...]
    for row in range(8):
        for k in range(3):
            total = None
            for slot in range(5):
                factor = factor_of(amps, first, begin + row + slot, k, 4 - slot) * (-1.0 if k == 1 else 1.0)
                at = (row + slot) * 288 + k * PAD
                term = spread[at : at + PAD, :] * factor
                total = term if total is None else total + term
            joined[row * PAD : (row + 1) * PAD, k * 128 : (k + 1) * 128] = total.astype(BF16)
    weights = jnp.concatenate([weight[k] for k in range(3)], axis=1)
    mixed = lax.dot_general(joined[...], weights, (((1,), (1,)), ((), ())), preferred_element_type=F32)
    out[0, :, begin : begin + 8, :] = jnp.swapaxes(mixed.reshape(8, PAD, CHAN)[:, :COLS], 0, 1)
    token[...] = before[...]


def sum_kernel(count, *refs):
    parts = [ref[...].astype(F32) for ref in refs[:count]]
    while len(parts) > 1:
        parts = [parts[i] + parts[i + 1] for i in range(0, len(parts), 2)]
    out, *token = refs[-2:] if refs[-1].shape[0] == 8 else refs[-1:]
    out[...] = parts[0].astype(out.dtype)
    if token:
        token[0][...] = jnp.zeros((8, 128), F32)


def pairs_of_lon(parity, lats):
    out = []
    for lat in lats:
        for lon in range(8):
            other = lon ^ 1 if parity == 0 else ((lon + 1) % 8 if lon % 2 else (lon - 1) % 8)
            out.append((lat * 8 + lon, lat * 8 + other))
    return out


def pairs_of_lat(parity):
    out = []
    for lat in range(8):
        other = lat ^ 1 if parity == 0 else (lat + 1 if lat % 2 else lat - 1)
        if 0 <= other < 8:
            out.append((lat, other))
    return out


def z_pairs():
    across = {0: 6, 6: 0, 1: 7, 7: 1, 2: 4, 4: 2, 3: 5, 5: 3}
    out = []
    for lat in range(8):
        for lon in range(8):
            other = across[(lon >> 2) * 4 + (lat >> 1)]
            out.append((lat * 8 + lon, ((other % 4) * 2 + lat % 2) * 8 + (other // 4) * 4 + lon % 4))
    return out


def flip(x, axis, bit):
    return lax.ppermute(x, axis, [(i, i ^ bit) for i in range(lax.axis_size(axis))])


VMEM = pl.BlockSpec(memory_space=pltpu.VMEM)
SMEM = pl.BlockSpec(memory_space=pltpu.SMEM)


def call(kernel, outs, scratch, flops, scalars, arrays, limit=12, space=pltpu.VMEM):
    moved = sum(math.prod(x.shape) * x.dtype.itemsize for x in (*arrays, *outs))
    return pl.pallas_call(
        kernel,
        out_shape=outs,
        in_specs=[SMEM] * len(scalars) + [pl.BlockSpec(memory_space=space)] * len(arrays),
        out_specs=[VMEM] * len(outs),
        scratch_shapes=scratch,
        compiler_params=pltpu.CompilerParams(vmem_limit_bytes=limit * 1024 * 1024),
        cost_estimate=pl.CostEstimate(flops=flops, bytes_accessed=moved, transcendentals=0),
    )(*scalars, *arrays)


def shape(dims, dtype=BF16):
    return jax.ShapeDtypeStruct(dims, dtype)


def body(features, cotangent, mix_weight, amplitude, row_spans):
    amps = amplitude.transpose(2, 0, 1)

    field, cot = features.transpose(0, 2, 1, 3), cotangent.transpose(0, 2, 1, 3)
    field, cot, spans, amps = (pltpu.with_memory_space_constraint(x, pltpu.HBM) for x in (field, cot, row_spans, amps))
    token = shape((8, 128), F32)
    few = shape((2, FEW, ROWS, CHAN))
    second = shape((2, SECOND, ROWS, CHAN))
    polar = shape((2, 65, ROWS, CHAN))
    scratch = [
        pltpu.VMEM((2, COLS, ROWS, CHAN), BF16),
        pltpu.SemaphoreType.DMA((12,)),
    ]
    messages = call(
        pack_kernel,
        [few, second, polar, few, polar],
        scratch,
        0,
        (),
        (field, cot),
        space=pltpu.HBM,
    )
    a, b = 1, 0
    targets = (
        pairs_of_lon(a, range(4, 8)) + pairs_of_lon(b, (2, 3)),
        pairs_of_lon(a, (1, 2, 3)),
        pairs_of_lon(a, (0,)),
        pairs_of_lon(b, range(2, 8)),
        pairs_of_lon(b, (0, 1)),
    )
    got = [None] * 5
    for index in (2, 1, 0, 4, 3):
        got[index] = lax.ppermute(messages[index], LL, targets[index])

    gathered = shape((ROWS, 128, CHAN))
    tables = [shape((20 * 288, 256)), shape((20 * 288, 256)), shape((5 * 288, 256))]
    row_flops = 2 * 288 * 640 * CHAN
    scratch = [
        pltpu.VMEM((2, COLS, ROWS, CHAN), BF16),
        pltpu.SMEM((128,), jnp.int32),
        pltpu.SMEM((5, 3, 128), F32),
        pltpu.SemaphoreType.DMA((9,)),
    ]
    outs = [gathered, gathered, *tables, shape((ROWS * 288, CHAN), F32), shape((5, 3, 128), F32)]
    own_f, own_c, *shapes, center, amps = call(prepare_kernel, outs, scratch, 2 * 10**8, (), (field, cot, spans, amps), space=pltpu.HBM)
    scalars = (amps,)
    own2 = shape((5, 32, CHAN))
    own0_f, own0_c, own1_f, own1_c, own2_f, own2_c, lat_a, lat_b = call(
        assemble_kernel,
        [gathered] * 4 + [own2] * 2 + [shape((2, 2, 128, CHAN)), shape((2, 2, 144, CHAN))],
        [],
        0,
        (),
        (own_f, own_c, *got, center),
    )
    halo_a = lax.ppermute(lat_a, "lat", pairs_of_lat(0))
    halo_b = lax.ppermute(lat_b, "lat", pairs_of_lat(1))

    own = (own0_f, own1_f, own2_f, *shapes, own0_c)
    half, ends = shape((192, CHAN), F32), shape((4 * 288, CHAN), F32)
    outs = [shape((12 * PAD, 384)), shape((128, 384), F32), ends]
    inner, part, ends = call(inner_kernel, outs, [], 12 * row_flops, scalars, (center, *own))
    outer, mine, other = call(
        outer_kernel,
        [shape((4 * PAD, 384)), half, half],
        [pltpu.VMEM((384, CHAN), F32)],
        4 * row_flops,
        scalars,
        (ends, shapes[0], shapes[1], own0_c, halo_a, halo_b, part),
    )

    def add(*parts, after=(), more=True, dtype=BF16):
        total = shape((192, CHAN), dtype)
        outs = [total, token] if more else [total]
        return call(functools.partial(sum_kernel, len(parts)), outs, [], 0, (), (*parts, *after))

    def back(piece, before, *done):
        return call(
            functools.partial(back_kernel, piece),
            [shape((1, COLS, ROWS, CHAN), F32), token],
            [pltpu.VMEM((12 * 288, CHAN), F32), pltpu.VMEM((8 * PAD, 384), BF16)],
            2 * row_flops,
            scalars,
            (own0_c, own1_c, own2_c, *shapes, halo_a, halo_b, mix_weight, before, *done),
        )

    mine, before = add(mine, flip(other, "lat", 1))
    steps = [flip(mine, "dp", bit) for bit in (1, 2, 3)]
    convolved, done = call(
        mix_kernel,
        [shape((1, COLS, ROWS, CHAN)), token],
        [],
        2 * ROWS * PAD * 384 * CHAN,
        (),
        (inner, outer, mix_weight.reshape(384, CHAN), before),
    )
    (mine,) = add(mine, *steps, after=(done,), more=False)
    steps = [flip(mine, "lon", bit) for bit in (1, 2, 3)]
    mine, before = add(mine, *steps)
    steps = [flip(mine, "lat", bit) for bit in (2, 4, 6)]
    grad, done = back(0, before)
    mine, before = add(mine, *steps, after=(done,))
    step = lax.ppermute(mine, LL, z_pairs())
    grad, done = back(1, before, grad)
    (mine,) = add(mine, step, after=(done,), more=False, dtype=F32)
    other = flip(mine, "lat", 1)
    first_half = lax.axis_index("lat") % 2 == 0
    whole = jnp.concatenate([jnp.where(first_half, mine, other), jnp.where(first_half, other, mine)])
    whole = whole * (1.0 / math.sqrt(4 * 128 * 720))
    return convolved.transpose(0, 2, 1, 3), grad.transpose(0, 2, 1, 3), whole.reshape(3, 128, 128)


def solution(mesh):
    cells = P("dp", "lat", "lon", None)
    return jax.shard_map(
        body,
        mesh=mesh,
        in_specs=(cells, cells, P(), P(), P()),
        out_specs=(cells, cells, P()),
        check_vma=False,
    )
```

```python
import functools
import math

import jax
import jax.numpy as jnp
from jax import lax
from jax.experimental import pallas as pl
from jax.experimental.pallas import tpu as pltpu
from jax.sharding import PartitionSpec as P

ROWS = 16
COLS = 90
CHAN = 128
PAD = 96
F32 = jnp.float32
BF16 = jnp.bfloat16
LL = ("lat", "lon")
POLAR_FAR = 40
SECOND = 18
FEW = 5


def offsets_of(group):
    col = lax.broadcasted_iota(jnp.int32, (PAD, 128), 0)
    lane = lax.broadcasted_iota(jnp.int32, (PAD, 128), 1)
    none = jnp.full((PAD, 128), 1000000, jnp.int32)
    if group == 0:
        source = jnp.where(lane < PAD, lane, jnp.where(lane < PAD + 16, lane - 112, lane - 22))
        source = jnp.where((lane >= COLS) & (lane < PAD), none, source)
    elif group == 1:
        source = jnp.where(lane < 64, lane - 80, lane + 42)
    else:
        source = jnp.where(lane < 16, lane - 90, lane + 148)
        source = jnp.where((lane >= 10) & (lane < 22), none, source)
        source = jnp.where(lane >= 32, none, source)
    return (source - col).astype(F32)


def fill_shapes(table, offsets, spans, first, low, high):
    def fill(row, carry):
        span = spans[row_of(first, row)].astype(F32)
        divisor = jnp.full((1, 128), span + 1.0, F32)
        norm = lax.rsqrt(divisor)
        inside = jnp.abs(offsets) <= span
        scaled = jnp.where(inside, offsets * (1.0 / divisor), 0.0)
        square = scaled * scaled
        half = jnp.full(square.shape, 4.7108746e-07, F32)
        for term in (-2.5202042e-05, 9.1926025e-04, -2.0863481e-02, 2.5366950e-01, -1.2337005, 1.0):
            half = half * square + term
        cosine = 2.0 * half * half - 1.0
        shapes = (1.0 - jnp.abs(scaled), scaled, cosine)
        for k in range(3):
            at = pl.multiple_of(row * 288 + k * PAD, PAD)
            value = jnp.where(inside, shapes[k] * norm, 0.0)
            high = value.astype(BF16)
            table[pl.ds(at, PAD), :128] = high
            table[pl.ds(at, PAD), 128:] = (value - high.astype(F32)).astype(BF16)
        return carry

    def four(index, carry):
        for part in range(4):
            fill(low + index * 4 + part, carry)
        return carry

    lax.fori_loop(0, (high - low) // 4, four, 0)
    lax.fori_loop(low + (high - low) // 4 * 4, high, fill, 0)


def position():
    lat = lax.axis_index("lat")
    return lat, lat * ROWS


def row_of(first, ext):
    if isinstance(ext, int) and 2 <= ext < 18:
        return first + ext - 2
    return jnp.clip(first + ext - 2, 0, 127)


def factor_of(amps, first, ext, k, tap):
    return amps[tap, k, row_of(first, ext)]


def pack_polar(whole, out, right):
    def begin(width):
        return COLS - width if right else 0

    def two(which, at, width, rows):
        middle = at + width // 2
        return jnp.concatenate([whole[which, at:middle, rows], whole[which, middle : at + width, rows]], axis=1)

    low, high = slice(0, 8), slice(8, 16)
    out[0:45] = two(0, 0, COLS, low)
    out[45:65] = two(0, begin(40), 40, high)
    out[65:95] = two(1, begin(60), 60, low)
    far = 0 if right else COLS - 32
    out[95:103] = jnp.concatenate([whole[1, far + 8 * i : far + 8 * i + 8, 0:4] for i in range(4)], axis=1)
    out[103:119] = two(1, begin(32), 32, high)


def open_polar(message, which, is_left):
    def two(low, high):
        return jnp.concatenate([message[low:high, :8], message[low:high, 8:]], axis=0)

    if which == 0:
        low, high = two(0, 45), two(45, 65)
    else:
        far = jnp.concatenate([message[95:103, 4 * i : 4 * i + 4] for i in range(4)], axis=0)
        far = jnp.concatenate([far, jnp.zeros((32, 4, CHAN), BF16)], axis=1)
        near, nothing = two(65, 95), jnp.zeros((8, 8, CHAN), BF16)
        low = jnp.concatenate([far[:30], near] if is_left else [near, far[2:]], axis=0)
        high = jnp.concatenate([nothing, two(103, 119)] if is_left else [two(103, 119), nothing], axis=0)
    return jnp.swapaxes(low, 0, 1), jnp.swapaxes(high, 0, 1)


def pack_kernel(field, cot, few_a, second_a, polar_a, few_b, polar_b, whole, sems):
    lat, odd = lax.axis_index("lat"), lax.axis_index("lon") % 2 == 1

    def edges(is_odd):
        def part(out, width, right, sem, skip=0):
            source = pl.ds(COLS - width - skip if right else skip, width)
            targets = [out.at[pl.ds(i * width, width)] if out is polar_b else out.at[i] for i in range(2)]
            pairs = enumerate(zip((field, cot), targets))
            return [pltpu.make_async_copy(x.at[0, source], target, sems.at[sem + i]) for i, (x, target) in pairs]

        def run(copies):
            for copy in copies:
                copy.start()
            for copy in copies:
                copy.wait()

        pl.when(lat >= 4)(lambda: run(part(few_a, FEW, is_odd, 0) + part(few_b, FEW, not is_odd, 2)))
        pl.when(lat == 1)(lambda: run(part(second_a, SECOND, is_odd, 0) + part(polar_b, SECOND, not is_odd, 2)))

        @pl.when((lat == 2) | (lat == 3))
        def _():
            nearest = part(few_a, FEW, not is_odd, 2)
            run(part(second_a, SECOND, is_odd, 0) + nearest + part(few_b, FEW, not is_odd, 4, skip=FEW))

        @pl.when(lat == 0)
        def _():
            loads = []
            for which, source in enumerate((field, cot)):
                for part in range(3):
                    at = pl.ds(part * 30, 30)
                    sem = sems.at[6 + which * 3 + part]
                    loads.append(pltpu.make_async_copy(source.at[0, at], whole.at[which, at], sem))
            for load in loads:
                load.start()
            for load in loads:
                load.wait()
            pack_polar(whole, polar_a, is_odd)
            pack_polar(whole, polar_b, not is_odd)

    pl.when(odd)(lambda: edges(True))
    pl.when(jnp.logical_not(odd))(lambda: edges(False))


def prepare_kernel(field, cot, spans, amps, *refs):
    own_f, own_c, shape0, shape1, shape2, center, amps_out, whole, spans_in, amps_in, sems = refs
    lat, first = position()
    fetch = pltpu.make_async_copy(spans, spans_in, sems.at[6])
    fetch_amps = pltpu.make_async_copy(amps, amps_in, sems.at[7])
    hand_on = pltpu.make_async_copy(amps, amps_out, sems.at[8])
    loads = []
    for which, source in enumerate((field, cot)):
        for part in range(3):
            at = pl.ds(part * 30, 30)
            loads.append(pltpu.make_async_copy(source.at[0, at], whole.at[which, at], sems.at[which * 3 + part]))
    for load in (fetch, fetch_amps, hand_on, *loads):
        load.start()
    fetch.wait()
    fill_shapes(shape0, offsets_of(0), spans_in, first, 0, 20)

    @pl.when(lat < 2)
    def _():
        low = jnp.where(lat == 0, 2, 0)
        fill_shapes(shape1, offsets_of(1), spans_in, first, low, jnp.where(lat == 0, 18, 2))

    @pl.when(lat == 0)
    def _():
        fill_shapes(shape2, offsets_of(2), spans_in, first, 2, 5)

    for load in (fetch_amps, hand_on, *loads):
        load.wait()
    for which, own in enumerate((own_f, own_c)):
        own[:, COLS:, :] = jnp.zeros((ROWS, 128 - COLS, CHAN), BF16)
        own[:, :COLS, :] = jnp.swapaxes(whole[which], 0, 1)
    for row in range(ROWS):
        rows = [own_f[row - 2 + tap, :PAD] if 0 <= row - 2 + tap < ROWS else None for tap in range(5)]
        values = filtered(shape0, (row + 2) * 288, amps_in, first, row + 2, rows)
        for k in range(3):
            at = row * 288 + k * PAD
            center[at : at + PAD, :] = values[k]


def assemble_kernel(old_f, old_c, few_a, second_a, polar_a, few_b, polar_b, tie, *outs):
    lat = lax.axis_index("lat")
    odd = lax.axis_index("lon") % 2 == 1
    groups = ((outs[0], outs[2], outs[4]), (outs[1], outs[3], outs[5]))
    lat_a, lat_b = outs[6], outs[7]

    def left_right(a, b):
        return jnp.swapaxes(jnp.where(odd, b, a), 0, 1), jnp.swapaxes(jnp.where(odd, a, b), 0, 1)

    for which in range(2):
        own0, own1, own2 = groups[which]
        own0[...] = (old_f, old_c)[which][...]

        def put_near(left, right, own0=own0):
            width = left.shape[0]
            own0[:, 112 - width : 112, :] = jnp.swapaxes(left, 0, 1)
            own0[:, 112 : 112 + width, :] = jnp.swapaxes(right, 0, 1)

        @pl.when(lat >= 4)
        def _(which=which, put_near=put_near):
            a, b = few_a[which], few_b[which]
            put_near(jnp.where(odd, b, a), jnp.where(odd, a, b))

        @pl.when((lat == 2) | (lat == 3))
        def _(which=which, put_near=put_near):
            near, next_ones = few_a[which], few_b[which]
            left = jnp.where(odd, jnp.concatenate([next_ones, near]), second_a[which, SECOND - 2 * FEW :])
            right = jnp.where(odd, second_a[which, : 2 * FEW], jnp.concatenate([near, next_ones]))
            put_near(left, right)

        @pl.when(lat == 1)
        def _(which=which, own0=own0, own1=own1):
            left, right = left_right(second_a[which], polar_b[which * SECOND : (which + 1) * SECOND])
            own0[:, 96:112, :] = left[:, 2:]
            own0[:, 112:128, :] = right[:, :16]
            own1[...] = jnp.zeros(own1.shape, BF16)
            own1[:, 62:64, :] = left[:, :2]
            own1[:, 64:66, :] = right[:, 16:]

        @pl.when(lat == 0)
        def _(which=which, own0=own0, own1=own1, own2=own2):
            a, b = polar_a[...], polar_b[...]
            left, high_left = open_polar(jnp.where(odd, b, a), which, True)
            right, high_right = open_polar(jnp.where(odd, a, b), which, False)
            own0[:8, 96:112, :] = left[:, 74:90]
            own0[:8, 112:128, :] = right[:, 0:16]
            own1[:8, :64, :] = left[:, 10:74]
            own1[:8, 64:, :] = right[:, 16:80]
            own2[:, :16, :] = left[:5, 0:16]
            own2[:, 16:, :] = right[:5, 74:90]
            left, right = high_left, high_right
            own0[8:, 96:112, :] = left[:, 24:40]
            own0[8:, 112:128, :] = right[:, 0:16]
            own1[8:] = jnp.zeros((8, 128, CHAN), BF16)
            own1[8:, 40:64, :] = left[:, 0:24]
            own1[8:, 64:88, :] = right[:, 16:40]

    lat_messages(lat, outs[0], outs[2], lat_a, lat_b)


def lat_messages(lat, own0, own1, lat_a, lat_b):
    even = lat % 2 == 0
    for row in range(2):
        lat_a[row] = jnp.where(even, own0[14 + row], own0[row])
        lat_b[row, :128, :] = jnp.where(even, own0[row], own0[14 + row])

    @pl.when(lat < 2)
    def _():
        for row in range(2):
            lat_a[row, COLS : COLS + 4, :] = jnp.where(even, own1[14 + row, 62:66, :], own1[row, 62:66, :])


def tapped(amps, first, ext, rows):
    taps = [tap for tap in range(5) if rows[tap] is not None]
    factors = [{tap: factor_of(amps, first, ext, k, tap) for tap in taps} for k in range(3)]
    height = rows[taps[0]].shape[0]
    parts = [[] for _ in range(3)]
    for at in range(0, height, 32):
        wide = {tap: rows[tap][at : at + 32].astype(F32) for tap in taps}
        for k in range(3):
            total = wide[taps[0]] * factors[k][taps[0]]
            for tap in taps[1:]:
                total += wide[tap] * factors[k][tap]
            parts[k].append(total.astype(BF16))
    return [jnp.concatenate(part, axis=0) if len(part) > 1 else part[0] for part in parts]


def filtered(table, at, amps, first, ext, rows, lane=0):
    out = []
    for k, taps in enumerate(tapped(amps, first, ext, rows)):
        shapes = rows_at(table, at + k * PAD, PAD)
        if taps.shape[0] < 128:
            end = lane + taps.shape[0]
            shapes = jnp.concatenate([shapes[:, lane:end], shapes[:, 128 + lane : 128 + end]], axis=1)
        out.append(jnp.dot(shapes, jnp.concatenate([taps, taps], axis=0), preferred_element_type=F32))
    return out


def plus(values, more):
    return [x + y for x, y in zip(values, more)]


def rows_at(ref, start, count=288):
    return ref[pl.ds(start if isinstance(start, int) else pl.multiple_of(start, 32), count), :]


def store_basis(basis, row, values):
    at = row * PAD if isinstance(row, int) else pl.multiple_of(row * PAD, PAD)
    for k in range(3):
        basis[pl.ds(at, PAD), k * 128 : (k + 1) * 128] = values[k].astype(BF16)


def times_cotangent(cot, basis):
    return lax.dot_general(cot, basis, (((0,), (0,)), ((), ())), preferred_element_type=F32)


def inner_kernel(amps, center, own0, own1, own2, shape0, shape1, shape2, cot, cot1, basis, part, ends, lat_a, lat_b):
    lat, first = position()

    def one(row, wide):
        def own(ref, low, high, end=128):
            return [ref[row - 2 + tap, low:end] if 0 <= row - 2 + tap < high else None for tap in range(5)]

        at = (row + 2) * 288
        values = filtered(shape0, at, amps, first, row + 2, own(own0, PAD, ROWS), PAD)
        values = plus(values, [center[row * 288 + k * PAD : row * 288 + (k + 1) * PAD, :] for k in range(3)])
        if wide:
            low = 0 if row < 5 else 32 if row < 8 else 48
            values = plus(values, filtered(shape1, at, amps, first, row + 2, own(own1, low, ROWS, 128 - low), low))
        if wide and row < 3:
            values = plus(values, filtered(shape2, at, amps, first, row + 2, own(own2, 0, 5, 32)))
        if 2 <= row < 14:
            store_basis(basis, row - 2, values)
        else:
            place = row if row < 2 else row - 12
            for k in range(3):
                ends[place * 288 + k * PAD : place * 288 + (k + 1) * PAD, :] = values[k]

    def run(wide):
        for row in range(ROWS):
            one(row, wide)

    pl.when(lat != 0)(lambda: run(False))
    pl.when(lat == 0)(lambda: run(True))
    part[...] = times_cotangent(cot[2:14, :PAD, :].reshape(12 * PAD, CHAN), basis[...])
    lat_messages(lat, cot, cot1, lat_a, lat_b)


def halo_row(halo_a, halo_b, row, even, top):
    a, b = halo_a[row], halo_b[row, :128]
    return jnp.where(even, b, a) if top else jnp.where(even, a, b)


def far_halo_row(halo_a, row):
    zeros = jnp.zeros((62, CHAN), BF16)
    return jnp.concatenate([zeros, halo_a[row, COLS : COLS + 4], zeros], axis=0)


def outer_kernel(amps, ends, shape0, shape1, cot, halo_a, halo_b, part, basis, mine, other, grad):
    lat, first = position()
    even = lat % 2 == 0

    def run(wide):
        for place, row in enumerate((0, 1, 14, 15)):
            near, far = [], []
            for at in range(row - 2, row + 3):
                inside, index = 0 <= at < ROWS, at + 2 if at < 0 else at - ROWS
                near.append(None if inside else halo_row(halo_a, halo_b, index, even, at < 0))
                far.append(None if inside or at < 0 else far_halo_row(halo_a, index))
            at = (row + 2) * 288
            values = filtered(shape0, at, amps, first, row + 2, near)
            values = plus(values, [ends[place * 288 + k * PAD : place * 288 + (k + 1) * PAD, :] for k in range(3)])
            if wide and row > 2:
                values = plus(values, filtered(shape1, at, amps, first, row + 2, far))
            store_basis(basis, place, values)

    pl.when(lat != 0)(lambda: run(False))
    pl.when(lat == 0)(lambda: run(True))
    cells = jnp.concatenate([cot[0:2, :PAD, :], cot[14:16, :PAD, :]], axis=0).reshape(4 * PAD, CHAN)
    product = part[...] + times_cotangent(cells, basis[...])
    for k in range(3):
        grad[k * 128 : (k + 1) * 128, :] = product[:, k * 128 : (k + 1) * 128].T
    core = lat % 2
    mine[...] = grad[pl.ds(pl.multiple_of(core * 192, 192), 192), :]
    other[...] = grad[pl.ds(pl.multiple_of((1 - core) * 192, 192), 192), :]


def mix_kernel(inner, outer, weight, before, out, token):
    w = weight[...]

    def mixed(basis, rows):
        return jnp.dot(basis, w, preferred_element_type=F32).astype(BF16).reshape(rows, PAD, CHAN)[:, :COLS]

    ends = mixed(outer[...], 4)
    whole = jnp.concatenate([ends[:2], mixed(inner[...], 12), ends[2:]], axis=0)
    out[0] = jnp.swapaxes(whole, 0, 1)
    token[...] = before[...]


def back_kernel(piece, amps, own0, own1, own2, shape0, shape1, shape2, halo_a, halo_b, weight, before, *refs):
    out, token, spread, joined = refs[-4:]
    lat, first = position()
    even = lat % 2 == 0
    begin = 8 * piece

    def put(index, value, fresh):
        at = index * 288 if isinstance(index, int) else pl.multiple_of(index * 288, 32)
        if fresh:
            spread[pl.ds(at, 288), :] = value
        else:
            spread[pl.ds(at, 288), :] += value

    def twice(shapes, rows):
        return jnp.dot(shapes, jnp.concatenate([rows, rows], axis=0), preferred_element_type=F32)

    def own_rows(low, high, wide):
        for ext in range(low, high):
            value = twice(rows_at(shape0, ext * 288), own0[ext - 2])
            if wide:
                value += twice(rows_at(shape1, ext * 288), own1[ext - 2])
            put(ext - begin, value, True)

    low, high = max(begin, 2), min(begin + 12, 18)
    pl.when(lat != 0)(lambda: own_rows(low, high, False))
    pl.when(lat == 0)(lambda: own_rows(low, high, True))
    for row in range(2):
        ext = row if piece == 0 else 18 + row
        gathered = halo_row(halo_a, halo_b, row, even, piece == 0)
        put(ext - begin, twice(shape0[ext * 288 : (ext + 1) * 288, :], gathered), True)
    if piece == 0:

        @pl.when(lat == 1)
        def _():
            for row in range(2):
                far = far_halo_row(halo_a, row)
                put(row, twice(shape1[row * 288 : (row + 1) * 288, :], far), False)

        @pl.when(lat == 0)
        def _():
            for ext in range(2, 5):
                at = slice(ext * 288, (ext + 1) * 288)
                shapes = jnp.concatenate([shape2[at, :32], shape2[at, 128:160]], axis=1)
                put(ext, twice(shapes, own2[ext - 2]), False)

    if piece:
        out[...] = refs[0][...]
    for row in range(8):
        for k in range(3):
            total = None
            for slot in range(5):
                factor = factor_of(amps, first, begin + row + slot, k, 4 - slot) * (-1.0 if k == 1 else 1.0)
                at = (row + slot) * 288 + k * PAD
                term = spread[at : at + PAD, :] * factor
                total = term if total is None else total + term
            joined[row * PAD : (row + 1) * PAD, k * 128 : (k + 1) * 128] = total.astype(BF16)
    weights = jnp.concatenate([weight[k] for k in range(3)], axis=1)
    mixed = lax.dot_general(joined[...], weights, (((1,), (1,)), ((), ())), preferred_element_type=F32)
    out[0, :, begin : begin + 8, :] = jnp.swapaxes(mixed.reshape(8, PAD, CHAN)[:, :COLS], 0, 1)
    token[...] = before[...]


def sum_kernel(count, *refs):
    parts = [ref[...].astype(F32) for ref in refs[:count]]
    while len(parts) > 1:
        parts = [parts[i] + parts[i + 1] for i in range(0, len(parts), 2)]
    out, *token = refs[-2:] if refs[-1].shape[0] == 8 else refs[-1:]
    out[...] = parts[0].astype(out.dtype)
    if token:
        token[0][...] = jnp.zeros((8, 128), F32)


def pairs_of_lon(parity, lats):
    out = []
    for lat in lats:
        for lon in range(8):
            other = lon ^ 1 if parity == 0 else ((lon + 1) % 8 if lon % 2 else (lon - 1) % 8)
            out.append((lat * 8 + lon, lat * 8 + other))
    return out


def pairs_of_lat(parity):
    out = []
    for lat in range(8):
        other = lat ^ 1 if parity == 0 else (lat + 1 if lat % 2 else lat - 1)
        if 0 <= other < 8:
            out.append((lat, other))
    return out


def z_pairs():
    across = {0: 6, 6: 0, 1: 7, 7: 1, 2: 4, 4: 2, 3: 5, 5: 3}
    out = []
    for lat in range(8):
        for lon in range(8):
            other = across[(lon >> 2) * 4 + (lat >> 1)]
            out.append((lat * 8 + lon, ((other % 4) * 2 + lat % 2) * 8 + (other // 4) * 4 + lon % 4))
    return out


def flip(x, axis, bit):
    return lax.ppermute(x, axis, [(i, i ^ bit) for i in range(lax.axis_size(axis))])


VMEM = pl.BlockSpec(memory_space=pltpu.VMEM)
SMEM = pl.BlockSpec(memory_space=pltpu.SMEM)


def call(kernel, outs, scratch, flops, scalars, arrays, limit=12, space=pltpu.VMEM):
    moved = sum(math.prod(x.shape) * x.dtype.itemsize for x in (*arrays, *outs))
    return pl.pallas_call(
        kernel,
        out_shape=outs,
        in_specs=[SMEM] * len(scalars) + [pl.BlockSpec(memory_space=space)] * len(arrays),
        out_specs=[VMEM] * len(outs),
        scratch_shapes=scratch,
        compiler_params=pltpu.CompilerParams(vmem_limit_bytes=limit * 1024 * 1024),
        cost_estimate=pl.CostEstimate(flops=flops, bytes_accessed=moved, transcendentals=0),
    )(*scalars, *arrays)


def shape(dims, dtype=BF16):
    return jax.ShapeDtypeStruct(dims, dtype)


def body(features, cotangent, mix_weight, amplitude, row_spans):
    amps = amplitude.transpose(2, 0, 1)

    field, cot = features.transpose(0, 2, 1, 3), cotangent.transpose(0, 2, 1, 3)
    field, cot, spans, amps = (pltpu.with_memory_space_constraint(x, pltpu.HBM) for x in (field, cot, row_spans, amps))
    token = shape((8, 128), F32)
    few = shape((2, FEW, ROWS, CHAN))
    second = shape((2, SECOND, ROWS, CHAN))
    polar = shape((119, ROWS, CHAN))
    scratch = [
        pltpu.VMEM((2, COLS, ROWS, CHAN), BF16),
        pltpu.SemaphoreType.DMA((12,)),
    ]
    messages = call(
        pack_kernel,
        [few, second, polar, few, polar],
        scratch,
        0,
        (),
        (field, cot),
        space=pltpu.HBM,
    )
    a, b = 1, 0
    targets = (
        pairs_of_lon(a, range(4, 8)) + pairs_of_lon(b, (2, 3)),
        pairs_of_lon(a, (1, 2, 3)),
        pairs_of_lon(a, (0,)),
        pairs_of_lon(b, range(2, 8)),
        pairs_of_lon(b, (0, 1)),
    )
    got = [None] * 5
    for index in (2, 1, 0, 4, 3):
        got[index] = lax.ppermute(messages[index], LL, targets[index])

    gathered = shape((ROWS, 128, CHAN))
    tables = [shape((20 * 288, 256)), shape((20 * 288, 256)), shape((5 * 288, 256))]
    row_flops = 2 * 288 * 640 * CHAN
    scratch = [
        pltpu.VMEM((2, COLS, ROWS, CHAN), BF16),
        pltpu.SMEM((128,), jnp.int32),
        pltpu.SMEM((5, 3, 128), F32),
        pltpu.SemaphoreType.DMA((9,)),
    ]
    outs = [gathered, gathered, *tables, shape((ROWS * 288, CHAN), F32), shape((5, 3, 128), F32)]
    own_f, own_c, *shapes, center, amps = call(prepare_kernel, outs, scratch, 2 * 10**8, (), (field, cot, spans, amps), space=pltpu.HBM)
    scalars = (amps,)
    own2 = shape((5, 32, CHAN))
    lat_shapes = [shape((2, 128, CHAN)), shape((2, 144, CHAN))]
    own0_f, own0_c, own1_f, own1_c, own2_f, own2_c, lat_a, lat_b = call(
        assemble_kernel,
        [gathered] * 4 + [own2] * 2 + [*lat_shapes],
        [],
        0,
        (),
        (own_f, own_c, *got, center),
    )
    halo_a = lax.ppermute(lat_a, "lat", pairs_of_lat(0))
    halo_b = lax.ppermute(lat_b, "lat", pairs_of_lat(1))

    own = (own0_f, own1_f, own2_f, *shapes, own0_c)
    half, ends = shape((192, CHAN), F32), shape((4 * 288, CHAN), F32)
    outs = [shape((12 * PAD, 384)), shape((128, 384), F32), ends, *lat_shapes]
    inner, part, ends, lat_a, lat_b = call(inner_kernel, outs, [], 12 * row_flops, scalars, (center, *own, own1_c))
    cot_halo_a = lax.ppermute(lat_a, "lat", pairs_of_lat(0))
    cot_halo_b = lax.ppermute(lat_b, "lat", pairs_of_lat(1))
    outer, mine, other = call(
        outer_kernel,
        [shape((4 * PAD, 384)), half, half],
        [pltpu.VMEM((384, CHAN), F32)],
        4 * row_flops,
        scalars,
        (ends, shapes[0], shapes[1], own0_c, halo_a, halo_b, part),
    )

    def add(*parts, after=(), more=True, dtype=BF16):
        total = shape((192, CHAN), dtype)
        outs = [total, token] if more else [total]
        return call(functools.partial(sum_kernel, len(parts)), outs, [], 0, (), (*parts, *after))

    def back(piece, before, *done):
        return call(
            functools.partial(back_kernel, piece),
            [shape((1, COLS, ROWS, CHAN), F32), token],
            [pltpu.VMEM((12 * 288, CHAN), F32), pltpu.VMEM((8 * PAD, 384), BF16)],
            2 * row_flops,
            scalars,
            (own0_c, own1_c, own2_c, *shapes, cot_halo_a, cot_halo_b, mix_weight, before, *done),
        )

    mine, before = add(mine, flip(other, "lat", 1))
    steps = [flip(mine, "dp", bit) for bit in (1, 2, 3)]
    convolved, done = call(
        mix_kernel,
        [shape((1, COLS, ROWS, CHAN)), token],
        [],
        2 * ROWS * PAD * 384 * CHAN,
        (),
        (inner, outer, mix_weight.reshape(384, CHAN), before),
    )
    (mine,) = add(mine, *steps, after=(done,), more=False)
    steps = [flip(mine, "lon", bit) for bit in (1, 2, 3)]
    mine, before = add(mine, *steps)
    steps = [flip(mine, "lat", bit) for bit in (2, 4, 6)]
    grad, done = back(0, before)
    mine, before = add(mine, *steps, after=(done,))
    step = lax.ppermute(mine, LL, z_pairs())
    grad, done = back(1, before, grad)
    (mine,) = add(mine, step, after=(done,), more=False, dtype=F32)
    other = flip(mine, "lat", 1)
    first_half = lax.axis_index("lat") % 2 == 0
    whole = jnp.concatenate([jnp.where(first_half, mine, other), jnp.where(first_half, other, mine)])
    whole = whole * (1.0 / math.sqrt(4 * 128 * 720))
    return convolved.transpose(0, 2, 1, 3), grad.transpose(0, 2, 1, 3), whole.reshape(3, 128, 128)


def solution(mesh):
    cells = P("dp", "lat", "lon", None)
    return jax.shard_map(
        body,
        mesh=mesh,
        in_specs=(cells, cells, P(), P(), P()),
        out_specs=(cells, cells, P()),
        check_vma=False,
    )
```

```python
import functools
import math

import jax
import jax.numpy as jnp
from jax import lax
from jax.experimental import pallas as pl
from jax.experimental.pallas import tpu as pltpu
from jax.sharding import PartitionSpec as P

ROWS = 16
COLS = 90
CHAN = 128
PAD = 96
F32 = jnp.float32
BF16 = jnp.bfloat16
LL = ("lat", "lon")
POLAR_FAR = 40
SECOND = 18
FEW = 5


def offsets_of(group):
    col = lax.broadcasted_iota(jnp.int32, (PAD, 128), 0)
    lane = lax.broadcasted_iota(jnp.int32, (PAD, 128), 1)
    none = jnp.full((PAD, 128), 1000000, jnp.int32)
    if group == 0:
        source = jnp.where(lane < PAD, lane, jnp.where(lane < PAD + 16, lane - 112, lane - 22))
        source = jnp.where((lane >= COLS) & (lane < PAD), none, source)
    elif group == 1:
        source = jnp.where(lane < 64, lane - 80, lane + 42)
    else:
        source = jnp.where(lane < 16, lane - 90, lane + 148)
        source = jnp.where((lane >= 10) & (lane < 22), none, source)
        source = jnp.where(lane >= 32, none, source)
    return (source - col).astype(F32)


def fill_shapes(table, offsets, spans, first, low, high):
    def fill(row, carry):
        span = spans[row_of(first, row)].astype(F32)
        divisor = jnp.full((1, 128), span + 1.0, F32)
        norm = lax.rsqrt(divisor)
        inside = jnp.abs(offsets) <= span
        scaled = jnp.where(inside, offsets * (1.0 / divisor), 0.0)
        square = scaled * scaled
        half = jnp.full(square.shape, 4.7108746e-07, F32)
        for term in (-2.5202042e-05, 9.1926025e-04, -2.0863481e-02, 2.5366950e-01, -1.2337005, 1.0):
            half = half * square + term
        cosine = 2.0 * half * half - 1.0
        shapes = (1.0 - jnp.abs(scaled), scaled, cosine)
        for k in range(3):
            at = pl.multiple_of(row * 288 + k * PAD, PAD)
            value = jnp.where(inside, shapes[k] * norm, 0.0)
            high = value.astype(BF16)
            table[pl.ds(at, PAD), :128] = high
            table[pl.ds(at, PAD), 128:] = (value - high.astype(F32)).astype(BF16)
        return carry

    def four(index, carry):
        for part in range(4):
            fill(low + index * 4 + part, carry)
        return carry

    lax.fori_loop(0, (high - low) // 4, four, 0)
    lax.fori_loop(low + (high - low) // 4 * 4, high, fill, 0)


def position():
    lat = lax.axis_index("lat")
    return lat, lat * ROWS


def row_of(first, ext):
    if isinstance(ext, int) and 2 <= ext < 18:
        return first + ext - 2
    return jnp.clip(first + ext - 2, 0, 127)


def factor_of(amps, first, ext, k, tap):
    return amps[tap, k, row_of(first, ext)]


def pack_polar(whole, out, right):
    def begin(width):
        return COLS - width if right else 0

    def two(which, at, width, rows):
        middle = at + width // 2
        return jnp.concatenate([whole[which, at:middle, rows], whole[which, middle : at + width, rows]], axis=1)

    low, high = slice(0, 8), slice(8, 16)
    out[0:45] = two(0, 0, COLS, low)
    out[45:65] = two(0, begin(40), 40, high)
    out[65:95] = two(1, begin(60), 60, low)
    far = 0 if right else COLS - 32
    out[95:103] = jnp.concatenate([whole[1, far + 8 * i : far + 8 * i + 8, 0:4] for i in range(4)], axis=1)
    out[103:119] = two(1, begin(32), 32, high)


def open_polar(message, which, is_left):
    def two(low, high):
        return jnp.concatenate([message[low:high, :8], message[low:high, 8:]], axis=0)

    if which == 0:
        low, high = two(0, 45), two(45, 65)
    else:
        far = jnp.concatenate([message[95:103, 4 * i : 4 * i + 4] for i in range(4)], axis=0)
        far = jnp.concatenate([far, jnp.zeros((32, 4, CHAN), BF16)], axis=1)
        near, nothing = two(65, 95), jnp.zeros((8, 8, CHAN), BF16)
        low = jnp.concatenate([far[:30], near] if is_left else [near, far[2:]], axis=0)
        high = jnp.concatenate([nothing, two(103, 119)] if is_left else [two(103, 119), nothing], axis=0)
    return jnp.swapaxes(low, 0, 1), jnp.swapaxes(high, 0, 1)


def pack_kernel(field, cot, few_a, second_a, polar_a, few_b, polar_b, whole, sems):
    lat, odd = lax.axis_index("lat"), lax.axis_index("lon") % 2 == 1

    def edges(is_odd):
        def part(out, width, right, sem, skip=0):
            source = pl.ds(COLS - width - skip if right else skip, width)
            targets = [out.at[pl.ds(i * width, width)] if out is polar_b else out.at[i] for i in range(2)]
            pairs = enumerate(zip((field, cot), targets))
            return [pltpu.make_async_copy(x.at[0, source], target, sems.at[sem + i]) for i, (x, target) in pairs]

        def run(copies):
            for copy in copies:
                copy.start()
            for copy in copies:
                copy.wait()

        pl.when(lat >= 4)(lambda: run(part(few_a, FEW, is_odd, 0) + part(few_b, FEW, not is_odd, 2)))
        pl.when(lat == 1)(lambda: run(part(second_a, SECOND, is_odd, 0) + part(polar_b, SECOND, not is_odd, 2)))

        @pl.when((lat == 2) | (lat == 3))
        def _():
            nearest = part(few_a, FEW, not is_odd, 2)
            run(part(second_a, SECOND, is_odd, 0) + nearest + part(few_b, FEW, not is_odd, 4, skip=FEW))

        @pl.when(lat == 0)
        def _():
            loads = []
            for which, source in enumerate((field, cot)):
                for part in range(3):
                    at = pl.ds(part * 30, 30)
                    sem = sems.at[6 + which * 3 + part]
                    loads.append(pltpu.make_async_copy(source.at[0, at], whole.at[which, at], sem))
            for load in loads:
                load.start()
            for load in loads:
                load.wait()
            pack_polar(whole, polar_a, is_odd)
            pack_polar(whole, polar_b, not is_odd)

    pl.when(odd)(lambda: edges(True))
    pl.when(jnp.logical_not(odd))(lambda: edges(False))


def prepare_kernel(field, cot, spans, amps, *refs):
    own_f, own_c, shape0, shape1, shape2, center, amps_out, whole, spans_in, amps_in, sems = refs
    lat, first = position()
    fetch = pltpu.make_async_copy(spans, spans_in, sems.at[6])
    fetch_amps = pltpu.make_async_copy(amps, amps_in, sems.at[7])
    hand_on = pltpu.make_async_copy(amps, amps_out, sems.at[8])
    loads = []
    for which, source in enumerate((field, cot)):
        for part in range(3):
            at = pl.ds(part * 30, 30)
            loads.append(pltpu.make_async_copy(source.at[0, at], whole.at[which, at], sems.at[which * 3 + part]))
    for load in (fetch, fetch_amps, hand_on, *loads):
        load.start()
    fetch.wait()
    fill_shapes(shape0, offsets_of(0), spans_in, first, 0, 20)

    @pl.when(lat < 2)
    def _():
        low = jnp.where(lat == 0, 2, 0)
        fill_shapes(shape1, offsets_of(1), spans_in, first, low, jnp.where(lat == 0, 18, 2))

    @pl.when(lat == 0)
    def _():
        fill_shapes(shape2, offsets_of(2), spans_in, first, 2, 5)

    for load in (fetch_amps, hand_on, *loads):
        load.wait()
    for which, own in enumerate((own_f, own_c)):
        own[:, COLS:, :] = jnp.zeros((ROWS, 128 - COLS, CHAN), BF16)
        own[:, :COLS, :] = jnp.swapaxes(whole[which], 0, 1)
    for row in range(ROWS):
        rows = [own_f[row - 2 + tap, :PAD] if 0 <= row - 2 + tap < ROWS else None for tap in range(5)]
        values = filtered(shape0, (row + 2) * 288, amps_in, first, row + 2, rows)
        for k in range(3):
            at = row * 288 + k * PAD
            center[at : at + PAD, :] = values[k]


def assemble_kernel(old_f, old_c, few_a, second_a, polar_a, few_b, polar_b, tie, *outs):
    lat = lax.axis_index("lat")
    odd = lax.axis_index("lon") % 2 == 1
    groups = ((outs[0], outs[2], outs[4]), (outs[1], outs[3], outs[5]))
    lat_a, lat_b = outs[6], outs[7]

    def left_right(a, b):
        return jnp.swapaxes(jnp.where(odd, b, a), 0, 1), jnp.swapaxes(jnp.where(odd, a, b), 0, 1)

    for which in range(2):
        own0, own1, own2 = groups[which]
        own0[...] = (old_f, old_c)[which][...]

        def put_near(left, right, own0=own0):
            width = left.shape[0]
            own0[:, 112 - width : 112, :] = jnp.swapaxes(left, 0, 1)
            own0[:, 112 : 112 + width, :] = jnp.swapaxes(right, 0, 1)

        @pl.when(lat >= 4)
        def _(which=which, put_near=put_near):
            a, b = few_a[which], few_b[which]
            put_near(jnp.where(odd, b, a), jnp.where(odd, a, b))

        @pl.when((lat == 2) | (lat == 3))
        def _(which=which, put_near=put_near):
            near, next_ones = few_a[which], few_b[which]
            left = jnp.where(odd, jnp.concatenate([next_ones, near]), second_a[which, SECOND - 2 * FEW :])
            right = jnp.where(odd, second_a[which, : 2 * FEW], jnp.concatenate([near, next_ones]))
            put_near(left, right)

        @pl.when(lat == 1)
        def _(which=which, own0=own0, own1=own1):
            left, right = left_right(second_a[which], polar_b[which * SECOND : (which + 1) * SECOND])
            own0[:, 96:112, :] = left[:, 2:]
            own0[:, 112:128, :] = right[:, :16]
            own1[...] = jnp.zeros(own1.shape, BF16)
            own1[:, 62:64, :] = left[:, :2]
            own1[:, 64:66, :] = right[:, 16:]

        @pl.when(lat == 0)
        def _(which=which, own0=own0, own1=own1, own2=own2):
            a, b = polar_a[...], polar_b[...]
            left, high_left = open_polar(jnp.where(odd, b, a), which, True)
            right, high_right = open_polar(jnp.where(odd, a, b), which, False)
            own0[:8, 96:112, :] = left[:, 74:90]
            own0[:8, 112:128, :] = right[:, 0:16]
            own1[:8, :64, :] = left[:, 10:74]
            own1[:8, 64:, :] = right[:, 16:80]
            own2[:, :16, :] = left[:5, 0:16]
            own2[:, 16:, :] = right[:5, 74:90]
            left, right = high_left, high_right
            own0[8:, 96:112, :] = left[:, 24:40]
            own0[8:, 112:128, :] = right[:, 0:16]
            own1[8:] = jnp.zeros((8, 128, CHAN), BF16)
            own1[8:, 40:64, :] = left[:, 0:24]
            own1[8:, 64:88, :] = right[:, 16:40]

    lat_messages(lat, outs[0], outs[2], lat_a, lat_b)


def lat_messages(lat, own0, own1, lat_a, lat_b):
    even = lat % 2 == 0
    for row in range(2):
        lat_a[row] = jnp.where(even, own0[14 + row], own0[row])
        lat_b[row, :128, :] = jnp.where(even, own0[row], own0[14 + row])

    @pl.when(lat < 2)
    def _():
        for row in range(2):
            lat_a[row, COLS : COLS + 4, :] = jnp.where(even, own1[14 + row, 62:66, :], own1[row, 62:66, :])


def tapped(amps, first, ext, rows):
    taps = [tap for tap in range(5) if rows[tap] is not None]
    factors = [{tap: factor_of(amps, first, ext, k, tap) for tap in taps} for k in range(3)]
    height = rows[taps[0]].shape[0]
    parts = [[] for _ in range(3)]
    for at in range(0, height, 32):
        wide = {tap: rows[tap][at : at + 32].astype(F32) for tap in taps}
        for k in range(3):
            total = wide[taps[0]] * factors[k][taps[0]]
            for tap in taps[1:]:
                total += wide[tap] * factors[k][tap]
            parts[k].append(total.astype(BF16))
    return [jnp.concatenate(part, axis=0) if len(part) > 1 else part[0] for part in parts]


def filtered(table, at, amps, first, ext, rows, lane=0):
    out = []
    for k, taps in enumerate(tapped(amps, first, ext, rows)):
        shapes = rows_at(table, at + k * PAD, PAD)
        if taps.shape[0] < 128:
            end = lane + taps.shape[0]
            shapes = jnp.concatenate([shapes[:, lane:end], shapes[:, 128 + lane : 128 + end]], axis=1)
        out.append(jnp.dot(shapes, jnp.concatenate([taps, taps], axis=0), preferred_element_type=F32))
    return out


def plus(values, more):
    return [x + y for x, y in zip(values, more)]


def rows_at(ref, start, count=288):
    return ref[pl.ds(start if isinstance(start, int) else pl.multiple_of(start, 32), count), :]


def store_basis(basis, row, values):
    at = row * PAD if isinstance(row, int) else pl.multiple_of(row * PAD, PAD)
    for k in range(3):
        basis[pl.ds(at, PAD), k * 128 : (k + 1) * 128] = values[k].astype(BF16)


def times_cotangent(left, right):
    return lax.dot_general(left, right, (((0,), (0,)), ((), ())), preferred_element_type=F32)


def inner_kernel(amps, center, own0, own1, own2, shape0, shape1, shape2, cot, cot1, basis, part, ends, lat_a, lat_b):
    lat, first = position()

    def one(row, wide):
        def own(ref, low, high, end=128):
            return [ref[row - 2 + tap, low:end] if 0 <= row - 2 + tap < high else None for tap in range(5)]

        at = (row + 2) * 288
        values = filtered(shape0, at, amps, first, row + 2, own(own0, PAD, ROWS), PAD)
        values = plus(values, [center[row * 288 + k * PAD : row * 288 + (k + 1) * PAD, :] for k in range(3)])
        if wide:
            low = 0 if row < 5 else 32 if row < 8 else 48
            values = plus(values, filtered(shape1, at, amps, first, row + 2, own(own1, low, ROWS, 128 - low), low))
        if wide and row < 3:
            values = plus(values, filtered(shape2, at, amps, first, row + 2, own(own2, 0, 5, 32)))
        if 2 <= row < 14:
            store_basis(basis, row - 2, values)
        else:
            place = row if row < 2 else row - 12
            for k in range(3):
                ends[place * 288 + k * PAD : place * 288 + (k + 1) * PAD, :] = values[k]

    def run(wide):
        for row in range(ROWS):
            one(row, wide)

    pl.when(lat != 0)(lambda: run(False))
    pl.when(lat == 0)(lambda: run(True))
    product = times_cotangent(cot[2:14, :PAD, :].reshape(12 * PAD, CHAN), basis[...])
    for k in range(3):
        part[k * 128 : (k + 1) * 128, :] = product[:, k * 128 : (k + 1) * 128].T
    lat_messages(lat, cot, cot1, lat_a, lat_b)


def halo_row(halo_a, halo_b, row, even, top):
    a, b = halo_a[row], halo_b[row, :128]
    return jnp.where(even, b, a) if top else jnp.where(even, a, b)


def far_halo_row(halo_a, row):
    zeros = jnp.zeros((62, CHAN), BF16)
    return jnp.concatenate([zeros, halo_a[row, COLS : COLS + 4], zeros], axis=0)


def outer_kernel(amps, ends, shape0, shape1, cot, halo_a, halo_b, part, basis, mine, other):
    lat, first = position()
    even = lat % 2 == 0

    def run(wide):
        for place, row in enumerate((0, 1, 14, 15)):
            near, far = [], []
            for at in range(row - 2, row + 3):
                inside, index = 0 <= at < ROWS, at + 2 if at < 0 else at - ROWS
                near.append(None if inside else halo_row(halo_a, halo_b, index, even, at < 0))
                far.append(None if inside or at < 0 else far_halo_row(halo_a, index))
            at = (row + 2) * 288
            values = filtered(shape0, at, amps, first, row + 2, near)
            values = plus(values, [ends[place * 288 + k * PAD : place * 288 + (k + 1) * PAD, :] for k in range(3)])
            if wide and row > 2:
                values = plus(values, filtered(shape1, at, amps, first, row + 2, far))
            store_basis(basis, place, values)

    pl.when(lat != 0)(lambda: run(False))
    pl.when(lat == 0)(lambda: run(True))
    cells = jnp.concatenate([cot[0:2, :PAD, :], cot[14:16, :PAD, :]], axis=0).reshape(4 * PAD, CHAN)
    sums = [part[k * 128 : (k + 1) * 128, :] + times_cotangent(basis[:, k * 128 : (k + 1) * 128], cells) for k in range(3)]

    def halves(low, high):
        low[:128, :] = sums[0]
        low[128:, :] = sums[1][:64]
        high[:64, :] = sums[1][64:]
        high[64:, :] = sums[2]

    pl.when(even)(lambda: halves(mine, other))
    pl.when(jnp.logical_not(even))(lambda: halves(other, mine))


def mix_kernel(inner, outer, weight, before, out, token):
    w = weight[...]

    def mixed(basis, rows):
        return jnp.dot(basis, w, preferred_element_type=F32).astype(BF16).reshape(rows, PAD, CHAN)[:, :COLS]

    ends = mixed(outer[...], 4)
    whole = jnp.concatenate([ends[:2], mixed(inner[...], 12), ends[2:]], axis=0)
    out[0] = jnp.swapaxes(whole, 0, 1)
    token[...] = before[...]


def back_kernel(piece, amps, own0, own1, own2, shape0, shape1, shape2, halo_a, halo_b, weight, before, *refs):
    out, token, spread, joined = refs[-4:]
    lat, first = position()
    even = lat % 2 == 0
    begin = 8 * piece

    def put(index, value, fresh):
        at = index * 288 if isinstance(index, int) else pl.multiple_of(index * 288, 32)
        if fresh:
            spread[pl.ds(at, 288), :] = value
        else:
            spread[pl.ds(at, 288), :] += value

    def twice(shapes, rows):
        return jnp.dot(shapes, jnp.concatenate([rows, rows], axis=0), preferred_element_type=F32)

    def own_rows(low, high, wide):
        for ext in range(low, high):
            value = twice(rows_at(shape0, ext * 288), own0[ext - 2])
            if wide:
                value += twice(rows_at(shape1, ext * 288), own1[ext - 2])
            put(ext - begin, value, True)

    low, high = max(begin, 2), min(begin + 12, 18)
    pl.when(lat != 0)(lambda: own_rows(low, high, False))
    pl.when(lat == 0)(lambda: own_rows(low, high, True))
    for row in range(2):
        ext = row if piece == 0 else 18 + row
        gathered = halo_row(halo_a, halo_b, row, even, piece == 0)
        put(ext - begin, twice(shape0[ext * 288 : (ext + 1) * 288, :], gathered), True)
    if piece == 0:

        @pl.when(lat == 1)
        def _():
            for row in range(2):
                far = far_halo_row(halo_a, row)
                put(row, twice(shape1[row * 288 : (row + 1) * 288, :], far), False)

        @pl.when(lat == 0)
        def _():
            for ext in range(2, 5):
                at = slice(ext * 288, (ext + 1) * 288)
                shapes = jnp.concatenate([shape2[at, :32], shape2[at, 128:160]], axis=1)
                put(ext, twice(shapes, own2[ext - 2]), False)

    if piece:
        out[...] = refs[0][...]
    for row in range(8):
        for k in range(3):
            total = None
            for slot in range(5):
                factor = factor_of(amps, first, begin + row + slot, k, 4 - slot) * (-1.0 if k == 1 else 1.0)
                at = (row + slot) * 288 + k * PAD
                term = spread[at : at + PAD, :] * factor
                total = term if total is None else total + term
            joined[row * PAD : (row + 1) * PAD, k * 128 : (k + 1) * 128] = total.astype(BF16)
    weights = jnp.concatenate([weight[k] for k in range(3)], axis=1)
    mixed = lax.dot_general(joined[...], weights, (((1,), (1,)), ((), ())), preferred_element_type=F32)
    out[0, :, begin : begin + 8, :] = jnp.swapaxes(mixed.reshape(8, PAD, CHAN)[:, :COLS], 0, 1)
    token[...] = before[...]


def sum_kernel(count, *refs):
    parts = [ref[...].astype(F32) for ref in refs[:count]]
    while len(parts) > 1:
        parts = [parts[i] + parts[i + 1] for i in range(0, len(parts), 2)]
    out, *token = refs[-2:] if refs[-1].shape[0] == 8 else refs[-1:]
    out[...] = parts[0].astype(out.dtype)
    if token:
        token[0][...] = jnp.zeros((8, 128), F32)


def pairs_of_lon(parity, lats):
    out = []
    for lat in lats:
        for lon in range(8):
            other = lon ^ 1 if parity == 0 else ((lon + 1) % 8 if lon % 2 else (lon - 1) % 8)
            out.append((lat * 8 + lon, lat * 8 + other))
    return out


def pairs_of_lat(parity):
    out = []
    for lat in range(8):
        other = lat ^ 1 if parity == 0 else (lat + 1 if lat % 2 else lat - 1)
        if 0 <= other < 8:
            out.append((lat, other))
    return out


def z_pairs():
    across = {0: 6, 6: 0, 1: 7, 7: 1, 2: 4, 4: 2, 3: 5, 5: 3}
    out = []
    for lat in range(8):
        for lon in range(8):
            other = across[(lon >> 2) * 4 + (lat >> 1)]
            out.append((lat * 8 + lon, ((other % 4) * 2 + lat % 2) * 8 + (other // 4) * 4 + lon % 4))
    return out


def flip(x, axis, bit):
    return lax.ppermute(x, axis, [(i, i ^ bit) for i in range(lax.axis_size(axis))])


VMEM = pl.BlockSpec(memory_space=pltpu.VMEM)
SMEM = pl.BlockSpec(memory_space=pltpu.SMEM)


def call(kernel, outs, scratch, flops, scalars, arrays, limit=12, space=pltpu.VMEM):
    moved = sum(math.prod(x.shape) * x.dtype.itemsize for x in (*arrays, *outs))
    return pl.pallas_call(
        kernel,
        out_shape=outs,
        in_specs=[SMEM] * len(scalars) + [pl.BlockSpec(memory_space=space)] * len(arrays),
        out_specs=[VMEM] * len(outs),
        scratch_shapes=scratch,
        compiler_params=pltpu.CompilerParams(vmem_limit_bytes=limit * 1024 * 1024),
        cost_estimate=pl.CostEstimate(flops=flops, bytes_accessed=moved, transcendentals=0),
    )(*scalars, *arrays)


def shape(dims, dtype=BF16):
    return jax.ShapeDtypeStruct(dims, dtype)


def body(features, cotangent, mix_weight, amplitude, row_spans):
    amps = amplitude.transpose(2, 0, 1)

    field, cot = features.transpose(0, 2, 1, 3), cotangent.transpose(0, 2, 1, 3)
    field, cot, spans, amps = (pltpu.with_memory_space_constraint(x, pltpu.HBM) for x in (field, cot, row_spans, amps))
    token = shape((8, 128), F32)
    few = shape((2, FEW, ROWS, CHAN))
    second = shape((2, SECOND, ROWS, CHAN))
    polar = shape((119, ROWS, CHAN))
    scratch = [
        pltpu.VMEM((2, COLS, ROWS, CHAN), BF16),
        pltpu.SemaphoreType.DMA((12,)),
    ]
    messages = call(
        pack_kernel,
        [few, second, polar, few, polar],
        scratch,
        0,
        (),
        (field, cot),
        space=pltpu.HBM,
    )
    a, b = 1, 0
    targets = (
        pairs_of_lon(a, range(4, 8)) + pairs_of_lon(b, (2, 3)),
        pairs_of_lon(a, (1, 2, 3)),
        pairs_of_lon(a, (0,)),
        pairs_of_lon(b, range(2, 8)),
        pairs_of_lon(b, (0, 1)),
    )
    got = [None] * 5
    for index in (2, 1, 0, 4, 3):
        got[index] = lax.ppermute(messages[index], LL, targets[index])

    gathered = shape((ROWS, 128, CHAN))
    tables = [shape((20 * 288, 256)), shape((20 * 288, 256)), shape((5 * 288, 256))]
    row_flops = 2 * 288 * 640 * CHAN
    scratch = [
        pltpu.VMEM((2, COLS, ROWS, CHAN), BF16),
        pltpu.SMEM((128,), jnp.int32),
        pltpu.SMEM((5, 3, 128), F32),
        pltpu.SemaphoreType.DMA((9,)),
    ]
    outs = [gathered, gathered, *tables, shape((ROWS * 288, CHAN), F32), shape((5, 3, 128), F32)]
    own_f, own_c, *shapes, center, amps = call(prepare_kernel, outs, scratch, 2 * 10**8, (), (field, cot, spans, amps), space=pltpu.HBM)
    scalars = (amps,)
    own2 = shape((5, 32, CHAN))
    lat_shapes = [shape((2, 128, CHAN)), shape((2, 144, CHAN))]
    own0_f, own0_c, own1_f, own1_c, own2_f, own2_c, lat_a, lat_b = call(
        assemble_kernel,
        [gathered] * 4 + [own2] * 2 + [*lat_shapes],
        [],
        0,
        (),
        (own_f, own_c, *got, center),
    )
    halo_a = lax.ppermute(lat_a, "lat", pairs_of_lat(0))
    halo_b = lax.ppermute(lat_b, "lat", pairs_of_lat(1))

    own = (own0_f, own1_f, own2_f, *shapes, own0_c)
    half, ends = shape((192, CHAN), F32), shape((4 * 288, CHAN), F32)
    outs = [shape((12 * PAD, 384)), shape((384, CHAN), F32), ends, *lat_shapes]
    inner, part, ends, lat_a, lat_b = call(inner_kernel, outs, [], 12 * row_flops, scalars, (center, *own, own1_c))
    cot_halo_a = lax.ppermute(lat_a, "lat", pairs_of_lat(0))
    cot_halo_b = lax.ppermute(lat_b, "lat", pairs_of_lat(1))
    outer, mine, other = call(
        outer_kernel,
        [shape((4 * PAD, 384)), half, half],
        [],
        4 * row_flops,
        scalars,
        (ends, shapes[0], shapes[1], own0_c, halo_a, halo_b, part),
    )

    def add(*parts, after=(), more=True, dtype=BF16):
        total = shape((192, CHAN), dtype)
        outs = [total, token] if more else [total]
        return call(functools.partial(sum_kernel, len(parts)), outs, [], 0, (), (*parts, *after))

    def back(piece, before, *done):
        return call(
            functools.partial(back_kernel, piece),
            [shape((1, COLS, ROWS, CHAN), F32), token],
            [pltpu.VMEM((12 * 288, CHAN), F32), pltpu.VMEM((8 * PAD, 384), BF16)],
            2 * row_flops,
            scalars,
            (own0_c, own1_c, own2_c, *shapes, cot_halo_a, cot_halo_b, mix_weight, before, *done),
        )

    mine, before = add(mine, flip(other, "lat", 1))
    steps = [flip(mine, "dp", bit) for bit in (1, 2, 3)]
    convolved, done = call(
        mix_kernel,
        [shape((1, COLS, ROWS, CHAN)), token],
        [],
        2 * ROWS * PAD * 384 * CHAN,
        (),
        (inner, outer, mix_weight.reshape(384, CHAN), before),
    )
    (mine,) = add(mine, *steps, after=(done,), more=False)
    steps = [flip(mine, "lon", bit) for bit in (1, 2, 3)]
    mine, before = add(mine, *steps)
    steps = [flip(mine, "lat", bit) for bit in (2, 4, 6)]
    grad, done = back(0, before)
    mine, before = add(mine, *steps, after=(done,))
    step = lax.ppermute(mine, LL, z_pairs())
    grad, done = back(1, before, grad)
    (mine,) = add(mine, step, after=(done,), more=False, dtype=F32)
    other = flip(mine, "lat", 1)
    first_half = lax.axis_index("lat") % 2 == 0
    whole = jnp.concatenate([jnp.where(first_half, mine, other), jnp.where(first_half, other, mine)])
    whole = whole * (1.0 / math.sqrt(4 * 128 * 720))
    return convolved.transpose(0, 2, 1, 3), grad.transpose(0, 2, 1, 3), whole.reshape(3, 128, 128)


def solution(mesh):
    cells = P("dp", "lat", "lon", None)
    return jax.shard_map(
        body,
        mesh=mesh,
        in_specs=(cells, cells, P(), P(), P()),
        out_specs=(cells, cells, P()),
        check_vma=False,
    )
```

```python
import functools
import math

import jax
import jax.numpy as jnp
from jax import lax
from jax.experimental import pallas as pl
from jax.experimental.pallas import tpu as pltpu
from jax.sharding import PartitionSpec as P

ROWS = 16
COLS = 90
CHAN = 128
PAD = 96
F32 = jnp.float32
BF16 = jnp.bfloat16
LL = ("lat", "lon")
POLAR_FAR = 40
SECOND = 18
FEW = 5


def offsets_of(group):
    col = lax.broadcasted_iota(jnp.int32, (PAD, 128), 0)
    lane = lax.broadcasted_iota(jnp.int32, (PAD, 128), 1)
    none = jnp.full((PAD, 128), 1000000, jnp.int32)
    if group == 0:
        source = jnp.where(lane < PAD, lane, jnp.where(lane < PAD + 16, lane - 112, lane - 22))
        source = jnp.where((lane >= COLS) & (lane < PAD), none, source)
    elif group == 1:
        source = jnp.where(lane < 64, lane - 80, lane + 42)
    else:
        source = jnp.where(lane < 16, lane - 90, lane + 148)
        source = jnp.where((lane >= 10) & (lane < 22), none, source)
        source = jnp.where(lane >= 32, none, source)
    return (source - col).astype(F32)


def fill_shapes(table, offsets, spans, first, low, high):
    def fill(row, carry):
        span = spans[row_of(first, row)].astype(F32)
        divisor = jnp.full((1, 128), span + 1.0, F32)
        norm = lax.rsqrt(divisor)
        inside = jnp.abs(offsets) <= span
        scaled = jnp.where(inside, offsets * (1.0 / divisor), 0.0)
        square = scaled * scaled
        half = jnp.full(square.shape, 4.7108746e-07, F32)
        for term in (-2.5202042e-05, 9.1926025e-04, -2.0863481e-02, 2.5366950e-01, -1.2337005, 1.0):
            half = half * square + term
        cosine = 2.0 * half * half - 1.0
        shapes = (1.0 - jnp.abs(scaled), scaled, cosine)
        for k in range(3):
            at = pl.multiple_of(row * 288 + k * PAD, PAD)
            value = jnp.where(inside, shapes[k] * norm, 0.0)
            high = value.astype(BF16)
            table[pl.ds(at, PAD), :128] = high
            table[pl.ds(at, PAD), 128:] = (value - high.astype(F32)).astype(BF16)
        return carry

    def four(index, carry):
        for part in range(4):
            fill(low + index * 4 + part, carry)
        return carry

    lax.fori_loop(0, (high - low) // 4, four, 0)
    lax.fori_loop(low + (high - low) // 4 * 4, high, fill, 0)


def position():
    lat = lax.axis_index("lat")
    return lat, lat * ROWS


def row_of(first, ext):
    if isinstance(ext, int) and 2 <= ext < 18:
        return first + ext - 2
    return jnp.clip(first + ext - 2, 0, 127)


def factor_of(amps, first, ext, k, tap):
    return amps[tap, k, row_of(first, ext)]


def pack_polar(whole, out, right):
    def begin(width):
        return COLS - width if right else 0

    def two(which, at, width, rows):
        middle = at + width // 2
        return jnp.concatenate([whole[which, at:middle, rows], whole[which, middle : at + width, rows]], axis=1)

    low, high = slice(0, 8), slice(8, 16)
    out[0:45] = two(0, 0, COLS, low)
    out[45:65] = two(0, begin(40), 40, high)
    out[65:95] = two(1, begin(60), 60, low)
    far = 0 if right else COLS - 32
    out[95:103] = jnp.concatenate([whole[1, far + 8 * i : far + 8 * i + 8, 0:4] for i in range(4)], axis=1)
    out[103:119] = two(1, begin(32), 32, high)


def open_polar(message, which, is_left):
    def two(low, high):
        return jnp.concatenate([message[low:high, :8], message[low:high, 8:]], axis=0)

    if which == 0:
        low, high = two(0, 45), two(45, 65)
    else:
        far = jnp.concatenate([message[95:103, 4 * i : 4 * i + 4] for i in range(4)], axis=0)
        far = jnp.concatenate([far, jnp.zeros((32, 4, CHAN), BF16)], axis=1)
        near, nothing = two(65, 95), jnp.zeros((8, 8, CHAN), BF16)
        low = jnp.concatenate([far[:30], near] if is_left else [near, far[2:]], axis=0)
        high = jnp.concatenate([nothing, two(103, 119)] if is_left else [two(103, 119), nothing], axis=0)
    return jnp.swapaxes(low, 0, 1), jnp.swapaxes(high, 0, 1)


def pack_kernel(field, cot, few_a, second_a, polar_a, few_b, polar_b, whole, sems):
    lat, odd = lax.axis_index("lat"), lax.axis_index("lon") % 2 == 1

    def edges(is_odd):
        def part(out, width, right, sem, skip=0):
            source = pl.ds(COLS - width - skip if right else skip, width)
            targets = [out.at[pl.ds(i * width, width)] if out is polar_b else out.at[i] for i in range(2)]
            pairs = enumerate(zip((field, cot), targets))
            return [pltpu.make_async_copy(x.at[0, source], target, sems.at[sem + i]) for i, (x, target) in pairs]

        def run(copies):
            for copy in copies:
                copy.start()
            for copy in copies:
                copy.wait()

        pl.when(lat >= 4)(lambda: run(part(few_a, FEW, is_odd, 0) + part(few_b, FEW, not is_odd, 2)))
        pl.when(lat == 1)(lambda: run(part(second_a, SECOND, is_odd, 0) + part(polar_b, SECOND, not is_odd, 2)))

        @pl.when((lat == 2) | (lat == 3))
        def _():
            nearest = part(few_a, FEW, not is_odd, 2)
            run(part(second_a, SECOND, is_odd, 0) + nearest + part(few_b, FEW, not is_odd, 4, skip=FEW))

        @pl.when(lat == 0)
        def _():
            loads = []
            for which, source in enumerate((field, cot)):
                for part in range(5):
                    at = pl.ds(part * 18, 18)
                    sem = sems.at[6 + which * 5 + part]
                    loads.append(pltpu.make_async_copy(source.at[0, at], whole.at[which, at], sem))
            for load in loads:
                load.start()
            for load in loads:
                load.wait()
            pack_polar(whole, polar_a, is_odd)
            pack_polar(whole, polar_b, not is_odd)

    pl.when(odd)(lambda: edges(True))
    pl.when(jnp.logical_not(odd))(lambda: edges(False))


def prepare_kernel(field, cot, spans, amps, *refs):
    own_f, own_c, shape0, shape1, shape2, center, amps_out, whole, spans_in, amps_in, sems = refs
    lat, first = position()
    fetch = pltpu.make_async_copy(spans, spans_in, sems.at[6])
    fetch_amps = pltpu.make_async_copy(amps, amps_in, sems.at[7])
    hand_on = pltpu.make_async_copy(amps, amps_out, sems.at[8])
    loads = []
    for which, source in enumerate((field, cot)):
        for part in range(3):
            at = pl.ds(part * 30, 30)
            loads.append(pltpu.make_async_copy(source.at[0, at], whole.at[which, at], sems.at[which * 3 + part]))
    for load in (fetch, fetch_amps, hand_on, *loads):
        load.start()
    fetch.wait()
    fill_shapes(shape0, offsets_of(0), spans_in, first, 0, 20)

    @pl.when(lat < 2)
    def _():
        low = jnp.where(lat == 0, 2, 0)
        fill_shapes(shape1, offsets_of(1), spans_in, first, low, jnp.where(lat == 0, 18, 2))

    @pl.when(lat == 0)
    def _():
        fill_shapes(shape2, offsets_of(2), spans_in, first, 2, 5)

    for load in (fetch_amps, hand_on, *loads):
        load.wait()
    for which, own in enumerate((own_f, own_c)):
        own[:, COLS:, :] = jnp.zeros((ROWS, 128 - COLS, CHAN), BF16)
        own[:, :COLS, :] = jnp.swapaxes(whole[which], 0, 1)
    for row in range(ROWS):
        rows = [own_f[row - 2 + tap, :PAD] if 0 <= row - 2 + tap < ROWS else None for tap in range(5)]
        values = filtered(shape0, (row + 2) * 288, amps_in, first, row + 2, rows)
        for k in range(3):
            at = row * 288 + k * PAD
            center[at : at + PAD, :] = values[k]


def assemble_kernel(old_f, old_c, few_a, second_a, polar_a, few_b, polar_b, tie, *outs):
    lat = lax.axis_index("lat")
    odd = lax.axis_index("lon") % 2 == 1
    groups = ((outs[0], outs[2], outs[4]), (outs[1], outs[3], outs[5]))
    lat_a, lat_b = outs[6], outs[7]

    def left_right(a, b):
        return jnp.swapaxes(jnp.where(odd, b, a), 0, 1), jnp.swapaxes(jnp.where(odd, a, b), 0, 1)

    for which in range(2):
        own0, own1, own2 = groups[which]
        own0[...] = (old_f, old_c)[which][...]

        def put_near(left, right, own0=own0):
            width = left.shape[0]
            own0[:, 112 - width : 112, :] = jnp.swapaxes(left, 0, 1)
            own0[:, 112 : 112 + width, :] = jnp.swapaxes(right, 0, 1)

        @pl.when(lat >= 4)
        def _(which=which, put_near=put_near):
            a, b = few_a[which], few_b[which]
            put_near(jnp.where(odd, b, a), jnp.where(odd, a, b))

        @pl.when((lat == 2) | (lat == 3))
        def _(which=which, put_near=put_near):
            near, next_ones = few_a[which], few_b[which]
            left = jnp.where(odd, jnp.concatenate([next_ones, near]), second_a[which, SECOND - 2 * FEW :])
            right = jnp.where(odd, second_a[which, : 2 * FEW], jnp.concatenate([near, next_ones]))
            put_near(left, right)

        @pl.when(lat == 1)
        def _(which=which, own0=own0, own1=own1):
            left, right = left_right(second_a[which], polar_b[which * SECOND : (which + 1) * SECOND])
            own0[:, 96:112, :] = left[:, 2:]
            own0[:, 112:128, :] = right[:, :16]
            own1[...] = jnp.zeros(own1.shape, BF16)
            own1[:, 62:64, :] = left[:, :2]
            own1[:, 64:66, :] = right[:, 16:]

        @pl.when(lat == 0)
        def _(which=which, own0=own0, own1=own1, own2=own2):
            a, b = polar_a[...], polar_b[...]
            left, high_left = open_polar(jnp.where(odd, b, a), which, True)
            right, high_right = open_polar(jnp.where(odd, a, b), which, False)
            own0[:8, 96:112, :] = left[:, 74:90]
            own0[:8, 112:128, :] = right[:, 0:16]
            own1[:8, :64, :] = left[:, 10:74]
            own1[:8, 64:, :] = right[:, 16:80]
            own2[:, :16, :] = left[:5, 0:16]
            own2[:, 16:, :] = right[:5, 74:90]
            left, right = high_left, high_right
            own0[8:, 96:112, :] = left[:, 24:40]
            own0[8:, 112:128, :] = right[:, 0:16]
            own1[8:] = jnp.zeros((8, 128, CHAN), BF16)
            own1[8:, 40:64, :] = left[:, 0:24]
            own1[8:, 64:88, :] = right[:, 16:40]

    lat_messages(lat, outs[0], outs[2], lat_a, lat_b)


def lat_messages(lat, own0, own1, lat_a, lat_b):
    even = lat % 2 == 0
    for row in range(2):
        lat_a[row] = jnp.where(even, own0[14 + row], own0[row])
        lat_b[row, :128, :] = jnp.where(even, own0[row], own0[14 + row])

    @pl.when(lat < 2)
    def _():
        for row in range(2):
            lat_a[row, COLS : COLS + 4, :] = jnp.where(even, own1[14 + row, 62:66, :], own1[row, 62:66, :])


def tapped(amps, first, ext, rows):
    taps = [tap for tap in range(5) if rows[tap] is not None]
    factors = [{tap: factor_of(amps, first, ext, k, tap) for tap in taps} for k in range(3)]
    height = rows[taps[0]].shape[0]
    parts = [[] for _ in range(3)]
    for at in range(0, height, 32):
        wide = {tap: rows[tap][at : at + 32].astype(F32) for tap in taps}
        for k in range(3):
            total = wide[taps[0]] * factors[k][taps[0]]
            for tap in taps[1:]:
                total += wide[tap] * factors[k][tap]
            parts[k].append(total.astype(BF16))
    return [jnp.concatenate(part, axis=0) if len(part) > 1 else part[0] for part in parts]


def filtered(table, at, amps, first, ext, rows, lane=0):
    out = []
    for k, taps in enumerate(tapped(amps, first, ext, rows)):
        shapes = rows_at(table, at + k * PAD, PAD)
        if taps.shape[0] < 128:
            end = lane + taps.shape[0]
            shapes = jnp.concatenate([shapes[:, lane:end], shapes[:, 128 + lane : 128 + end]], axis=1)
        out.append(jnp.dot(shapes, jnp.concatenate([taps, taps], axis=0), preferred_element_type=F32))
    return out


def plus(values, more):
    return [x + y for x, y in zip(values, more)]


def rows_at(ref, start, count=288):
    return ref[pl.ds(start if isinstance(start, int) else pl.multiple_of(start, 32), count), :]


def store_basis(basis, row, values):
    at = row * PAD if isinstance(row, int) else pl.multiple_of(row * PAD, PAD)
    for k in range(3):
        basis[pl.ds(at, PAD), k * 128 : (k + 1) * 128] = values[k].astype(BF16)


def times_cotangent(left, right):
    return lax.dot_general(left, right, (((0,), (0,)), ((), ())), preferred_element_type=F32)


def inner_kernel(amps, center, own0, own1, own2, shape0, shape1, shape2, cot, cot1, basis, part, ends, lat_a, lat_b):
    lat, first = position()

    def one(row, wide):
        def own(ref, low, high, end=128):
            return [ref[row - 2 + tap, low:end] if 0 <= row - 2 + tap < high else None for tap in range(5)]

        at = (row + 2) * 288
        values = filtered(shape0, at, amps, first, row + 2, own(own0, PAD, ROWS), PAD)
        values = plus(values, [center[row * 288 + k * PAD : row * 288 + (k + 1) * PAD, :] for k in range(3)])
        if wide:
            low = 0 if row < 5 else 32 if row < 8 else 48
            values = plus(values, filtered(shape1, at, amps, first, row + 2, own(own1, low, ROWS, 128 - low), low))
        if wide and row < 3:
            values = plus(values, filtered(shape2, at, amps, first, row + 2, own(own2, 0, 5, 32)))
        if 2 <= row < 14:
            store_basis(basis, row - 2, values)
        else:
            place = row if row < 2 else row - 12
            for k in range(3):
                ends[place * 288 + k * PAD : place * 288 + (k + 1) * PAD, :] = values[k]

    def run(wide):
        for row in range(ROWS):
            one(row, wide)

    pl.when(lat != 0)(lambda: run(False))
    pl.when(lat == 0)(lambda: run(True))
    product = times_cotangent(cot[2:14, :PAD, :].reshape(12 * PAD, CHAN), basis[...])
    for k in range(3):
        part[k * 128 : (k + 1) * 128, :] = product[:, k * 128 : (k + 1) * 128].T
    lat_messages(lat, cot, cot1, lat_a, lat_b)


def halo_row(halo_a, halo_b, row, even, top):
    a, b = halo_a[row], halo_b[row, :128]
    return jnp.where(even, b, a) if top else jnp.where(even, a, b)


def far_halo_row(halo_a, row):
    zeros = jnp.zeros((62, CHAN), BF16)
    return jnp.concatenate([zeros, halo_a[row, COLS : COLS + 4], zeros], axis=0)


def outer_kernel(amps, ends, shape0, shape1, cot, halo_a, halo_b, part, basis, mine, other):
    lat, first = position()
    even = lat % 2 == 0

    def run(wide):
        for place, row in enumerate((0, 1, 14, 15)):
            near, far = [], []
            for at in range(row - 2, row + 3):
                inside, index = 0 <= at < ROWS, at + 2 if at < 0 else at - ROWS
                near.append(None if inside else halo_row(halo_a, halo_b, index, even, at < 0))
                far.append(None if inside or at < 0 else far_halo_row(halo_a, index))
            at = (row + 2) * 288
            values = filtered(shape0, at, amps, first, row + 2, near)
            values = plus(values, [ends[place * 288 + k * PAD : place * 288 + (k + 1) * PAD, :] for k in range(3)])
            if wide and row > 2:
                values = plus(values, filtered(shape1, at, amps, first, row + 2, far))
            store_basis(basis, place, values)

    pl.when(lat != 0)(lambda: run(False))
    pl.when(lat == 0)(lambda: run(True))
    cells = jnp.concatenate([cot[0:2, :PAD, :], cot[14:16, :PAD, :]], axis=0).reshape(4 * PAD, CHAN)
    sums = [part[k * 128 : (k + 1) * 128, :] + times_cotangent(basis[:, k * 128 : (k + 1) * 128], cells) for k in range(3)]

    def halves(low, high):
        low[:128, :] = sums[0]
        low[128:, :] = sums[1][:64]
        high[:64, :] = sums[1][64:]
        high[64:, :] = sums[2]

    pl.when(even)(lambda: halves(mine, other))
    pl.when(jnp.logical_not(even))(lambda: halves(other, mine))


def mix_kernel(inner, outer, weight, before, out, token):
    w = weight[...]

    def mixed(basis, rows):
        return jnp.dot(basis, w, preferred_element_type=F32).astype(BF16).reshape(rows, PAD, CHAN)[:, :COLS]

    ends = mixed(outer[...], 4)
    whole = jnp.concatenate([ends[:2], mixed(inner[...], 12), ends[2:]], axis=0)
    out[0] = jnp.swapaxes(whole, 0, 1)
    token[...] = before[...]


def back_kernel(piece, amps, own0, own1, own2, shape0, shape1, shape2, halo_a, halo_b, weight, before, *refs):
    out, token, spread, joined = refs[-4:]
    lat, first = position()
    even = lat % 2 == 0
    begin = 8 * piece

    def put(index, value, fresh):
        at = index * 288 if isinstance(index, int) else pl.multiple_of(index * 288, 32)
        if fresh:
            spread[pl.ds(at, 288), :] = value
        else:
            spread[pl.ds(at, 288), :] += value

    def twice(shapes, rows):
        return jnp.dot(shapes, jnp.concatenate([rows, rows], axis=0), preferred_element_type=F32)

    def own_rows(low, high, wide):
        for ext in range(low, high):
            value = twice(rows_at(shape0, ext * 288), own0[ext - 2])
            if wide:
                value += twice(rows_at(shape1, ext * 288), own1[ext - 2])
            put(ext - begin, value, True)

    low, high = max(begin, 2), min(begin + 12, 18)
    pl.when(lat != 0)(lambda: own_rows(low, high, False))
    pl.when(lat == 0)(lambda: own_rows(low, high, True))
    for row in range(2):
        ext = row if piece == 0 else 18 + row
        gathered = halo_row(halo_a, halo_b, row, even, piece == 0)
        put(ext - begin, twice(shape0[ext * 288 : (ext + 1) * 288, :], gathered), True)
    if piece == 0:

        @pl.when(lat == 1)
        def _():
            for row in range(2):
                far = far_halo_row(halo_a, row)
                put(row, twice(shape1[row * 288 : (row + 1) * 288, :], far), False)

        @pl.when(lat == 0)
        def _():
            for ext in range(2, 5):
                at = slice(ext * 288, (ext + 1) * 288)
                shapes = jnp.concatenate([shape2[at, :32], shape2[at, 128:160]], axis=1)
                put(ext, twice(shapes, own2[ext - 2]), False)

    if piece:
        out[...] = refs[0][...]
    for row in range(8):
        for k in range(3):
            total = None
            for slot in range(5):
                factor = factor_of(amps, first, begin + row + slot, k, 4 - slot) * (-1.0 if k == 1 else 1.0)
                at = (row + slot) * 288 + k * PAD
                term = spread[at : at + PAD, :] * factor
                total = term if total is None else total + term
            joined[row * PAD : (row + 1) * PAD, k * 128 : (k + 1) * 128] = total.astype(BF16)
    weights = jnp.concatenate([weight[k] for k in range(3)], axis=1)
    mixed = lax.dot_general(joined[...], weights, (((1,), (1,)), ((), ())), preferred_element_type=F32)
    out[0, :, begin : begin + 8, :] = jnp.swapaxes(mixed.reshape(8, PAD, CHAN)[:, :COLS], 0, 1)
    token[...] = before[...]


def sum_kernel(count, *refs):
    parts = [ref[...].astype(F32) for ref in refs[:count]]
    while len(parts) > 1:
        parts = [parts[i] + parts[i + 1] for i in range(0, len(parts), 2)]
    out, *token = refs[-2:] if refs[-1].shape[0] == 8 else refs[-1:]
    out[...] = parts[0].astype(out.dtype)
    if token:
        token[0][...] = jnp.zeros((8, 128), F32)


def pairs_of_lon(parity, lats):
    out = []
    for lat in lats:
        for lon in range(8):
            other = lon ^ 1 if parity == 0 else ((lon + 1) % 8 if lon % 2 else (lon - 1) % 8)
            out.append((lat * 8 + lon, lat * 8 + other))
    return out


def pairs_of_lat(parity):
    out = []
    for lat in range(8):
        other = lat ^ 1 if parity == 0 else (lat + 1 if lat % 2 else lat - 1)
        if 0 <= other < 8:
            out.append((lat, other))
    return out


def z_pairs():
    across = {0: 6, 6: 0, 1: 7, 7: 1, 2: 4, 4: 2, 3: 5, 5: 3}
    out = []
    for lat in range(8):
        for lon in range(8):
            other = across[(lon >> 2) * 4 + (lat >> 1)]
            out.append((lat * 8 + lon, ((other % 4) * 2 + lat % 2) * 8 + (other // 4) * 4 + lon % 4))
    return out


def flip(x, axis, bit):
    return lax.ppermute(x, axis, [(i, i ^ bit) for i in range(lax.axis_size(axis))])


VMEM = pl.BlockSpec(memory_space=pltpu.VMEM)
SMEM = pl.BlockSpec(memory_space=pltpu.SMEM)


def call(kernel, outs, scratch, flops, scalars, arrays, limit=12, space=pltpu.VMEM):
    moved = sum(math.prod(x.shape) * x.dtype.itemsize for x in (*arrays, *outs))
    return pl.pallas_call(
        kernel,
        out_shape=outs,
        in_specs=[SMEM] * len(scalars) + [pl.BlockSpec(memory_space=space)] * len(arrays),
        out_specs=[VMEM] * len(outs),
        scratch_shapes=scratch,
        compiler_params=pltpu.CompilerParams(vmem_limit_bytes=limit * 1024 * 1024),
        cost_estimate=pl.CostEstimate(flops=flops, bytes_accessed=moved, transcendentals=0),
    )(*scalars, *arrays)


def shape(dims, dtype=BF16):
    return jax.ShapeDtypeStruct(dims, dtype)


def body(features, cotangent, mix_weight, amplitude, row_spans):
    amps = amplitude.transpose(2, 0, 1)

    field, cot = features.transpose(0, 2, 1, 3), cotangent.transpose(0, 2, 1, 3)
    field, cot, spans, amps = (pltpu.with_memory_space_constraint(x, pltpu.HBM) for x in (field, cot, row_spans, amps))
    token = shape((8, 128), F32)
    few = shape((2, FEW, ROWS, CHAN))
    second = shape((2, SECOND, ROWS, CHAN))
    polar = shape((119, ROWS, CHAN))
    scratch = [
        pltpu.VMEM((2, COLS, ROWS, CHAN), BF16),
        pltpu.SemaphoreType.DMA((16,)),
    ]
    messages = call(
        pack_kernel,
        [few, second, polar, few, polar],
        scratch,
        0,
        (),
        (field, cot),
        space=pltpu.HBM,
    )
    a, b = 1, 0
    targets = (
        pairs_of_lon(a, range(4, 8)) + pairs_of_lon(b, (2, 3)),
        pairs_of_lon(a, (1, 2, 3)),
        pairs_of_lon(a, (0,)),
        pairs_of_lon(b, range(2, 8)),
        pairs_of_lon(b, (0, 1)),
    )
    got = [None] * 5
    for index in (2, 1, 0, 4, 3):
        got[index] = lax.ppermute(messages[index], LL, targets[index])

    gathered = shape((ROWS, 128, CHAN))
    tables = [shape((20 * 288, 256)), shape((20 * 288, 256)), shape((5 * 288, 256))]
    row_flops = 2 * 288 * 640 * CHAN
    scratch = [
        pltpu.VMEM((2, COLS, ROWS, CHAN), BF16),
        pltpu.SMEM((128,), jnp.int32),
        pltpu.SMEM((5, 3, 128), F32),
        pltpu.SemaphoreType.DMA((9,)),
    ]
    outs = [gathered, gathered, *tables, shape((ROWS * 288, CHAN), F32), shape((5, 3, 128), F32)]
    own_f, own_c, *shapes, center, amps = call(prepare_kernel, outs, scratch, 2 * 10**8, (), (field, cot, spans, amps), space=pltpu.HBM)
    scalars = (amps,)
    own2 = shape((5, 32, CHAN))
    lat_shapes = [shape((2, 128, CHAN)), shape((2, 144, CHAN))]
    own0_f, own0_c, own1_f, own1_c, own2_f, own2_c, lat_a, lat_b = call(
        assemble_kernel,
        [gathered] * 4 + [own2] * 2 + [*lat_shapes],
        [],
        0,
        (),
        (own_f, own_c, *got, center),
    )
    halo_a = lax.ppermute(lat_a, "lat", pairs_of_lat(0))
    halo_b = lax.ppermute(lat_b, "lat", pairs_of_lat(1))

    own = (own0_f, own1_f, own2_f, *shapes, own0_c)
    half, ends = shape((192, CHAN), F32), shape((4 * 288, CHAN), F32)
    outs = [shape((12 * PAD, 384)), shape((384, CHAN), F32), ends, *lat_shapes]
    inner, part, ends, lat_a, lat_b = call(inner_kernel, outs, [], 12 * row_flops, scalars, (center, *own, own1_c))
    cot_halo_a = lax.ppermute(lat_a, "lat", pairs_of_lat(0))
    cot_halo_b = lax.ppermute(lat_b, "lat", pairs_of_lat(1))
    outer, mine, other = call(
        outer_kernel,
        [shape((4 * PAD, 384)), half, half],
        [],
        4 * row_flops,
        scalars,
        (ends, shapes[0], shapes[1], own0_c, halo_a, halo_b, part),
    )

    def add(*parts, after=(), more=True, dtype=BF16):
        total = shape((192, CHAN), dtype)
        outs = [total, token] if more else [total]
        return call(functools.partial(sum_kernel, len(parts)), outs, [], 0, (), (*parts, *after))

    def back(piece, before, *done):
        return call(
            functools.partial(back_kernel, piece),
            [shape((1, COLS, ROWS, CHAN), F32), token],
            [pltpu.VMEM((12 * 288, CHAN), F32), pltpu.VMEM((8 * PAD, 384), BF16)],
            2 * row_flops,
            scalars,
            (own0_c, own1_c, own2_c, *shapes, cot_halo_a, cot_halo_b, mix_weight, before, *done),
        )

    mine, before = add(mine, flip(other, "lat", 1))
    steps = [flip(mine, "dp", bit) for bit in (1, 2, 3)]
    convolved, done = call(
        mix_kernel,
        [shape((1, COLS, ROWS, CHAN)), token],
        [],
        2 * ROWS * PAD * 384 * CHAN,
        (),
        (inner, outer, mix_weight.reshape(384, CHAN), before),
    )
    (mine,) = add(mine, *steps, after=(done,), more=False)
    steps = [flip(mine, "lon", bit) for bit in (1, 2, 3)]
    mine, before = add(mine, *steps)
    steps = [flip(mine, "lat", bit) for bit in (2, 4, 6)]
    grad, done = back(0, before)
    mine, before = add(mine, *steps, after=(done,))
    step = lax.ppermute(mine, LL, z_pairs())
    grad, done = back(1, before, grad)
    (mine,) = add(mine, step, after=(done,), more=False, dtype=F32)
    other = flip(mine, "lat", 1)
    first_half = lax.axis_index("lat") % 2 == 0
    whole = jnp.concatenate([jnp.where(first_half, mine, other), jnp.where(first_half, other, mine)])
    whole = whole * (1.0 / math.sqrt(4 * 128 * 720))
    return convolved.transpose(0, 2, 1, 3), grad.transpose(0, 2, 1, 3), whole.reshape(3, 128, 128)


def solution(mesh):
    cells = P("dp", "lat", "lon", None)
    return jax.shard_map(
        body,
        mesh=mesh,
        in_specs=(cells, cells, P(), P(), P()),
        out_specs=(cells, cells, P()),
        check_vma=False,
    )
```
